32 devices in a mesh: dp: 8 (over z, x), heads: 4 (over y, core).
Axes of the slice: x: 2, y: 2, z: 4, core: 2. Of those that a mesh axis runs over, the one named last changes fastest.
Arguments:
- tokens: bfloat16 [2, 8, 1024, 1024], P(None, 'dp', 'heads'), may hold values from -6 to 6
- counts: int32 [2, 8], P(None, 'dp'), may hold values from 64 to 512, as said below
- token_weights: bfloat16 [1024, 3, 1024], P('dp', None, 'heads'), may hold values from -0.1875 to 0.1875
- token_output: bfloat16 [1024, 1024], P('dp', 'heads'), may hold values from -3 to 3
- state_weights: bfloat16 [1024, 3, 1024], P('dp', None, 'heads'), may hold values from -0.1875 to 0.1875
- state_output: bfloat16 [1024, 1024], P('dp', 'heads'), may hold values from -3 to 3
- hidden_up: bfloat16 [1024, 4096], P('dp', 'heads'), may hold values from -0.1875 to 0.1875
- hidden_down: bfloat16 [1024, 4096], P('dp', 'heads'), may hold values from -0.09375 to 0.09375
- norm_gains: bfloat16 [3, 1024], P(None, 'dp'), may hold values from 0.5 to 1.5
- gate_bias: bfloat16 [1024], P('dp'), may hold values from -2 to 2
- init_state: bfloat16 [512, 1024], P(None, 'dp'), may hold values from -6 to 6
- cotangent: bfloat16 [2, 8, 1024, 1024], P(None, 'dp', 'heads'), may hold values from -6 to 6
- state_cotangent: bfloat16 [2, 8, 512, 1024], P(None, 'dp'), may hold values from -6 to 6
Outputs:
- output: bfloat16 [2, 8, 1024, 1024], P(None, 'dp', 'heads')
- final_state: bfloat16 [2, 8, 512, 1024], P(None, 'dp')
- input_grad: float32 [2, 8, 1024, 1024], P(None, 'dp', 'heads')
- grad_token_weights: float32 [1024, 3, 1024], P('dp', None, 'heads')
- grad_token_output: float32 [1024, 1024], P('dp', 'heads')
- grad_state_weights: float32 [1024, 3, 1024], P('dp', None, 'heads')
- grad_state_output: float32 [1024, 1024], P('dp', 'heads')
- grad_hidden_up: float32 [1024, 4096], P('dp', 'heads')
- grad_hidden_down: float32 [1024, 4096], P('dp', 'heads')
- grad_norm_gains: float32 [3, 1024], P(None, 'dp')
- grad_gate_bias: float32 [1024], P('dp')
- grad_init_state: float32 [512, 1024], P(None, 'dp')
The draws below stay inside these ranges and needn't reach their ends.
Inputs may be any that keep to these rules, and one draw needn't show every extreme that they name: `counts`: for every sequence index of a micro-batch, one of its 2 micro-batches has all 512 tokens of the final block valid.
All inputs are finite; a program needn't handle non-finite values.
Results may differ from the reference program's by a relative error of at most 0.019.
Values may be sent and summed in bfloat16 or wider, within the bound.
No kernel may reach another device: no remote copies, remote signals or barrier semaphores. Data moves between devices by JAX's collectives and lax.ppermute only.
A program may use at most 320 MiB of HBM per device.

```python
import jax
import jax.numpy as jnp
from jax import lax

D = 1024
HEAD_COUNT = 8
HEAD_DIM = 128
FF = 4096
BLOCK = 512
STATE = 512
SEQ_LEN = 1024
MICRO = 2
BLOCKS = 2
BATCH = 8


def draw_counts(key, part):
    key = jax.random.fold_in(key, 11)
    first_key, second_key, third_key = jax.random.split(key, 3)
    drawn = jax.random.randint(first_key, (MICRO, BATCH), BLOCK // 8, BLOCK + 1)
    full_micro = jax.random.randint(second_key, (BATCH,), 0, MICRO)
    micro_rows = jnp.arange(MICRO)[:, None]
    seq_columns = jnp.arange(BATCH)[None, :]
    drawn = jnp.where(micro_rows == full_micro[None, :], BLOCK, drawn)
    short_seq = jax.random.randint(third_key, (), 0, BATCH)
    other_micro = (full_micro[short_seq] + 1) % MICRO
    drawn = jnp.where((micro_rows == other_micro) & (seq_columns == short_seq), BLOCK // 8, drawn)
    return drawn.astype(jnp.int32)


def shard_levels(own_key, shape, pieces, smallest, largest):
    level = 1.0
    for dim, parts in pieces:
        draws = jax.random.uniform(jax.random.fold_in(jax.random.fold_in(own_key, 6), dim), (parts,), jnp.float32, smallest / len(pieces), largest / len(pieces))
        level = level * jnp.repeat(jnp.exp(draws), shape[dim] // parts).reshape((-1,) + (1,) * (len(shape) - 1 - dim))
    return level


def scatter_about(rng, dims, deviation, bound, pieces=(), dtype=jnp.bfloat16):
    level = shard_levels(rng, dims, pieces, -0.22, 0.18) if pieces else 1.0
    entries = jax.random.normal(rng, dims, jnp.float32) * deviation * level
    return jnp.minimum(jnp.maximum(entries, -bound), bound).astype(dtype)


def setup_inputs(seed: int = 0) -> dict:
    seeds = jax.random.split(jax.random.key(seed), 14)
    return {
        "tokens": scatter_about(seeds[0], (MICRO, BATCH, SEQ_LEN, D), 1.0, 6.0, ((1, 8), (2, 4))),
        "counts": draw_counts(jax.random.fold_in(seeds[13], 71), 0),
        "token_weights": scatter_about(seeds[2], (D, 3, D), D ** -0.5, 0.1875, ((0, 8), (2, 4))),
        "token_output": scatter_about(seeds[3], (D, D), (max(1, D // 256)) ** -0.5, 3.0, ((0, 8), (1, 4))),
        "state_weights": scatter_about(seeds[4], (D, 3, D), D ** -0.5, 0.1875, ((0, 8), (2, 4))),
        "state_output": scatter_about(seeds[5], (D, D), (max(1, D // 256)) ** -0.5, 3.0, ((0, 8), (1, 4))),
        "hidden_up": scatter_about(seeds[6], (D, FF), D ** -0.5, 0.1875, ((0, 8), (1, 4))),
        "hidden_down": scatter_about(seeds[7], (D, FF), FF ** -0.5, 0.09375, ((0, 8), (1, 4))),
        "norm_gains": jnp.clip(1.0 + 0.1 * jax.random.normal(seeds[8], (3, D), jnp.float32), 0.5, 1.5).astype(jnp.bfloat16),
        "gate_bias": jnp.clip(jax.random.uniform(seeds[9], (D,), jnp.float32, -2.0, 2.0) * shard_levels(seeds[9], (D,), ((0, 8),), -0.4, 0.0), -2.0, 2.0).astype(jnp.bfloat16),
        "init_state": scatter_about(seeds[10], (STATE, D), 1.0, 6.0, ((1, 8),)),
        "cotangent": scatter_about(seeds[11], (MICRO, BATCH, SEQ_LEN, D), 1.0, 6.0, ((1, 8), (2, 4))),
        "state_cotangent": scatter_about(seeds[12], (MICRO, BATCH, STATE, D), 1.0, 6.0, ((1, 8),)),
    }


@jax.custom_vjp
def low(v):
    return lax.optimization_barrier(v.astype(jnp.bfloat16)).astype(jnp.float32)

@jax.custom_vjp
def low_back(v):
    return v

def low_keep(v):
    return (low(v), None)

def low_pass(kept, grad):
    return (grad,)

def back_keep(v):
    return (v, None)

def back_low(kept, grad):
    return (low(grad),)
low.defvjp(low_keep, low_pass)
low_back.defvjp(back_keep, back_low)
EPSILON = 1e-06
HIGHEST = lax.Precision.HIGHEST
MASKED = -1e+30

def rms_scale(values, gain):
    return values * lax.rsqrt(lax.optimization_barrier(jnp.mean(values * values, axis=-1, keepdims=True)) + EPSILON) * gain

def matmul(left, right):
    return jnp.dot(left, right, precision=HIGHEST)

def to_heads(flat):
    return flat.reshape(flat.shape[0], HEAD_COUNT, HEAD_DIM).transpose(1, 0, 2)

def from_heads(split):
    return split.transpose(1, 0, 2).reshape(split.shape[1], D)

def attend(queries, key_rows, value_rows, allowed):
    scores = jnp.einsum('hqe,hke->hqk', queries, key_rows, precision=HIGHEST) * HEAD_DIM ** (-0.5)
    scores = low_back(scores)
    scores = jnp.where(allowed[None], scores, MASKED)
    weights = low(jax.nn.softmax(scores, axis=-1))
    return jnp.einsum('hqk,hke->hqe', weights, value_rows, precision=HIGHEST)

def sequence(params, token_rows, valid_count):
    token_weights, token_output, state_weights, state_output, hidden_up, hidden_down, norm_gains, gate_bias, init_state = params
    normed = low(rms_scale(token_rows, norm_gains[0]))
    projected = low_back(low(jnp.einsum('nd,dcf->cnf', normed, token_weights, precision=HIGHEST)))
    queries = to_heads(projected[0])
    key_rows = to_heads(projected[1])
    value_rows = to_heads(projected[2])
    position = jnp.arange(SEQ_LEN)
    valid_mask = position < (BLOCKS - 1) * BLOCK + valid_count
    gate_open = jax.nn.sigmoid(gate_bias)
    state_now = init_state
    mixed_parts = []
    for block_index in range(BLOCKS):
        state_norm = low(rms_scale(state_now, norm_gains[1]))
        state_proj = low_back(low(jnp.einsum('nd,dcf->cnf', state_norm, state_weights, precision=HIGHEST)))
        state_queries = to_heads(state_proj[0])
        state_keys = to_heads(state_proj[1])
        state_values = to_heads(state_proj[2])
        begin_row = block_index * BLOCK
        first_key = max(block_index - 1, 0) * BLOCK
        final_row = begin_row + BLOCK
        query_pos = position[begin_row:final_row]
        key_pos = position[first_key:final_row]
        nearby = (key_pos[None, :] <= query_pos[:, None]) & (key_pos[None, :] > query_pos[:, None] - BLOCK) & valid_mask[None, first_key:final_row]
        allowed = jnp.concatenate([nearby, jnp.ones((BLOCK, STATE), jnp.bool_)], axis=1)
        mixed_parts.append(attend(queries[:, begin_row:final_row], jnp.concatenate([key_rows[:, first_key:final_row], state_keys], axis=1), jnp.concatenate([value_rows[:, first_key:final_row], state_values], axis=1), allowed))
        state_allowed = jnp.concatenate([jnp.ones((STATE, STATE), jnp.bool_), jnp.broadcast_to(valid_mask[None, begin_row:final_row], (STATE, BLOCK))], axis=1)
        state_mixed = attend(state_queries, jnp.concatenate([state_keys, key_rows[:, begin_row:final_row]], axis=1), jnp.concatenate([state_values, value_rows[:, begin_row:final_row]], axis=1), state_allowed)
        state_mixed = low_back(low(from_heads(state_mixed)))
        update = low_back(matmul(state_mixed, state_output.T))
        state_now = gate_open * state_now + (1.0 - gate_open) * update
    mixed = low_back(low(from_heads(jnp.concatenate(mixed_parts, axis=1))))
    hidden = token_rows + low_back(matmul(mixed, token_output.T))
    hidden_norm = low(rms_scale(hidden, norm_gains[2]))
    up_value = low_back(matmul(hidden_norm, hidden_up))
    activated = low_back(low(jax.nn.gelu(up_value, approximate=True)))
    return (hidden + low_back(matmul(activated, hidden_down.T)), state_now)

def reference(tokens, counts, token_weights, token_output, state_weights, state_output, hidden_up, hidden_down, norm_gains, gate_bias, init_state, cotangent, state_cotangent):
    params = tuple((item.astype(jnp.float32) for item in (token_weights, token_output, state_weights, state_output, hidden_up, hidden_down, norm_gains, gate_bias, init_state)))
    total_seqs = MICRO * BATCH
    flat_tokens = tokens.reshape(total_seqs, SEQ_LEN, D)
    flat_counts = counts.reshape(total_seqs)
    flat_cotangent = cotangent.reshape(total_seqs, SEQ_LEN, D)
    flat_state_cot = state_cotangent.reshape(total_seqs, STATE, D)

    def per_sequence(running, item):
        seq_tokens, seq_count, seq_cotangent, seq_state_cot = item

        def forward(param_list, token_values):
            return sequence(param_list, token_values, seq_count)
        (result_rows, final_rows), pullback = jax.vjp(forward, params, seq_tokens.astype(jnp.float32))
        grad_params, grad_tokens = pullback((seq_cotangent.astype(jnp.float32), seq_state_cot.astype(jnp.float32)))
        running = jax.tree.map(jnp.add, running, grad_params)
        return (running, (result_rows.astype(jnp.bfloat16), final_rows.astype(jnp.bfloat16), grad_tokens.astype(jnp.float32)))
    zeros_start = jax.tree.map(jnp.zeros_like, params)
    totals, (results, finals, grads) = lax.scan(per_sequence, zeros_start, (flat_tokens, flat_counts, flat_cotangent, flat_state_cot))
    output = results.reshape(MICRO, BATCH, SEQ_LEN, D)
    final_state = finals.reshape(MICRO, BATCH, STATE, D)
    input_grad = grads.reshape(MICRO, BATCH, SEQ_LEN, D)
    return (output, final_state, input_grad, totals[0].astype(jnp.float32), totals[1].astype(jnp.float32), totals[2].astype(jnp.float32), totals[3].astype(jnp.float32), totals[4].astype(jnp.float32), totals[5].astype(jnp.float32), totals[6].astype(jnp.float32), totals[7].astype(jnp.float32), totals[8].astype(jnp.float32))
```

```python
import functools

import jax
import jax.numpy as jnp
from jax import lax
from jax.sharding import Mesh
from jax.sharding import PartitionSpec as P

HEAD_DIM = 128
BLOCK = 512
EPSILON = 1e-06
MASKED = -1e30
RING = 4
BF = jnp.bfloat16
F32 = jnp.float32


def swap(array, axis):
    return lax.ppermute(array, axis, [(0, 1), (1, 0)])


def turn(array, steps):
    return lax.ppermute(array, "z", [(i, (i + steps) % RING) for i in range(RING)])


def matmul(left, right, contract):
    return lax.dot_general(
        left, right, (contract, ((), ())), preferred_element_type=jnp.float32
    )


def mm(left, right):
    return matmul(left, right, ((1,), (0,)))


def mm_nt(left, right):
    return matmul(left, right, ((1,), (1,)))


def mm_tn(left, right):
    return matmul(left, right, ((0,), (0,)))


def width_places():
    z, x = lax.axis_index("z"), lax.axis_index("x")
    return [lax.rem(z - k + RING, RING) * 2 + jnp.bitwise_xor(x, dx) for dx in range(2) for k in range(RING)]


def take_pieces(array, places):
    groups = lax.axis_size("r")
    lead, width = array.shape[:-1], array.shape[-1]
    split = array.reshape(lead + (groups, len(places), width // (groups * len(places))))
    axis = len(lead) + 1
    return [lax.dynamic_index_in_dim(split, place, axis, keepdims=False) for place in places]


def to_local(array):
    pieces = take_pieces(array, width_places())
    lead = array.shape[:-1]
    return jnp.concatenate([p.reshape(lead + (-1,)) for p in pieces], axis=-1)


def from_local(array):
    z, x = lax.axis_index("z"), lax.axis_index("x")
    groups = lax.axis_size("r")
    lead, width = array.shape[:-1], array.shape[-1]
    split = array.reshape(lead + (2 * RING, groups, width // (groups * 2 * RING)))
    axis = len(lead)
    pieces = []
    for z_to in range(RING):
        for x_to in range(2):
            place = jnp.bitwise_xor(x, x_to) * RING + lax.rem(z - z_to + RING, RING)
            pieces.append(lax.dynamic_index_in_dim(split, place, axis, keepdims=False))
    return jnp.stack(pieces, axis=axis + 1).reshape(array.shape)


def gather_groups(array, axis):
    if lax.axis_size("r") == 1:
        return array
    return lax.all_gather(array, "r", axis=axis, tiled=True)


def gather_weight(shard):
    shard = gather_groups(shard, 1)
    half = shard.shape[2] // 2
    ring = [shard] + [turn(shard, k) for k in range(1, RING)]
    near_a = jnp.concatenate([piece[..., :half] for piece in ring], axis=1)
    near_b = jnp.concatenate([piece[..., half:] for piece in ring], axis=1)
    a_x, a_y = swap(near_a, "x"), swap(near_a, "y")
    b_y, b_x = swap(near_b, "y"), swap(near_b, "x")
    a_xy, b_xy = swap(a_x, "y"), swap(b_y, "x")
    top = jnp.concatenate([near_a, a_y, near_b, b_y], axis=2)
    bottom = jnp.concatenate([a_x, a_xy, b_x, b_xy], axis=2)
    return jnp.concatenate([top, bottom], axis=1)


def gather_rows(shard):
    if lax.axis_size("r") > 1:
        shard = lax.all_gather(shard, "r", axis=1, tiled=True)
    near = jnp.concatenate([shard] + [turn(shard, k) for k in range(1, RING)], axis=1)
    return jnp.concatenate([near, swap(near, "x")], axis=1)


def add_low(left, right):
    return (left.astype(F32) + right.astype(F32)).astype(BF)


def scatter_groups(array, axis):
    if lax.axis_size("r") == 1:
        return array
    return lax.psum_scatter(array, "r", scatter_dimension=axis, tiled=True)


def scatter_ring(near):
    groups, rows, width = near.shape
    split = near.reshape(groups, RING, rows // RING, width)
    total = split[:, 0].astype(F32)
    for k in range(1, RING):
        total = total + turn(split[:, k], RING - k).astype(F32)
    return total


def weight_grad(left, rights):
    width = left.shape[1]
    quarter = rights[0].shape[1] // 4
    half_rows = width // 2

    def part(rows, columns):
        return jnp.stack([mm_tn(left[:, rows], right[:, columns]).astype(BF) for right in rights])

    everything = slice(0, width)
    near, far = slice(0, half_rows), slice(half_rows, width)
    a_send = part(everything, slice(quarter, 2 * quarter))
    b_send = part(far, slice(2 * quarter, 4 * quarter))
    a_got, b_got = swap(a_send, "y"), swap(b_send, "x")
    a_sum = add_low(part(everything, slice(0, quarter)), a_got)
    b_sum = add_low(part(near, slice(2 * quarter, 4 * quarter)), b_got)
    a_got2 = swap(a_sum[:, half_rows:], "x")
    b_got2 = swap(b_sum[:, :, quarter:], "y")
    a_near = add_low(a_sum[:, :half_rows], a_got2)
    b_near = add_low(b_sum[:, :, :quarter], b_got2)
    total = scatter_ring(jnp.concatenate([a_near, b_near], axis=2))
    return scatter_groups(total, 1)


def rms_inverse(values):
    return lax.rsqrt(jnp.mean(values * values, axis=-1, keepdims=True) + EPSILON)


def rms_forward(values, gain):
    return (values * rms_inverse(values) * gain).astype(BF)


def rms_backward(values, gain, grad):
    inverse = rms_inverse(values)
    scaled = values * inverse
    weighted = grad * gain
    grad_values = inverse * (weighted - scaled * jnp.mean(scaled * weighted, axis=-1, keepdims=True))
    return grad_values, jnp.sum(grad * scaled, axis=0)


def gelu_tanh(values):
    return jax.nn.gelu(values, approximate=True)


def join(own):
    return jnp.concatenate([own, swap(own, "c")], axis=0)


def fold(partial):
    rows = partial.shape[0] // 2
    return partial[:rows].astype(F32) + swap(partial[rows:].astype(BF), "c").astype(F32)


def split_heads(flat):
    return flat.reshape(flat.shape[0], flat.shape[1] // HEAD_DIM, HEAD_DIM).transpose(1, 0, 2)


def merge_heads(split):
    return split.transpose(1, 0, 2).reshape(split.shape[1], split.shape[0] * HEAD_DIM)


def attend_forward(queries, key_rows, value_rows, allowed):
    scale = HEAD_DIM ** (-0.5)
    scores = jnp.einsum("hqe,hke->hqk", queries, key_rows, preferred_element_type=F32) * scale
    scores = jnp.where(allowed[None], scores, MASKED)
    row_top = jnp.max(scores, axis=-1, keepdims=True)
    weights = jnp.exp(scores - row_top)
    row_total = jnp.sum(weights, axis=-1, keepdims=True)
    probs = (weights / row_total).astype(BF)
    mixed = jnp.einsum("hqk,hke->hqe", probs, value_rows, preferred_element_type=F32)
    return (mixed, row_top + jnp.log(row_total))


def attend_backward(queries, key_rows, value_rows, allowed, log_total, grad_mixed):
    scale = HEAD_DIM ** (-0.5)
    scores = jnp.einsum("hqe,hke->hqk", queries, key_rows, preferred_element_type=F32) * scale
    scores = jnp.where(allowed[None], scores, MASKED)
    probs = jnp.exp(scores - log_total)
    grad_probs = jnp.einsum("hqe,hke->hqk", grad_mixed, value_rows, preferred_element_type=F32)
    grad_scores = probs * (grad_probs - jnp.sum(grad_probs * probs, axis=-1, keepdims=True))
    low_scores = grad_scores.astype(BF)
    grad_queries = jnp.einsum("hqk,hke->hqe", low_scores, key_rows, preferred_element_type=F32) * scale
    grad_keys = jnp.einsum("hqk,hqe->hke", low_scores, queries, preferred_element_type=F32) * scale
    grad_values = jnp.einsum("hqk,hqe->hke", probs.astype(BF), grad_mixed, preferred_element_type=F32)
    return (grad_queries, grad_keys, grad_values)


def rows_of_block(array, block_index, blocks):
    lead = array.shape[:-2]
    rows, width = array.shape[-2:]
    per = rows // (2 * blocks)
    split = array.reshape(lead + (2, blocks, per, width))
    return split[..., block_index, :, :].reshape(lead + (2 * per, width))


def rows_from_blocks(parts):
    blocks = len(parts)
    lead = parts[0].shape[:-2]
    rows, width = parts[0].shape[-2:]
    split = [part.reshape(lead + (2, 1, rows // 2, width)) for part in parts]
    joined = jnp.concatenate(split, axis=-3)
    return joined.reshape(lead + (blocks * rows, width))


def body(
    tokens,
    counts,
    token_weights,
    token_output,
    state_weights,
    state_output,
    hidden_up,
    hidden_down,
    norm_gains,
    gate_bias,
    init_state,
    cotangent,
    state_cotangent,
):
    y, c = lax.axis_index("y"), lax.axis_index("c")
    micro, rows_local, width = tokens.shape[0], tokens.shape[2], tokens.shape[3]
    state_rows = init_state.shape[0]
    state_half = state_rows // 2

    def own_rows(array):
        keep = lax.dynamic_index_in_dim(array[:, 0], y, 0, keepdims=False)
        send = lax.dynamic_index_in_dim(array[:, 0], 1 - y, 0, keepdims=False)
        got = swap(send, "y")
        return jnp.where(y == 0, jnp.concatenate([keep, got]), jnp.concatenate([got, keep]))

    def to_owner(rows, wide):
        split = rows.reshape(2, rows_local, width)
        keep = lax.dynamic_index_in_dim(split, y, 0, keepdims=False)
        send = lax.dynamic_index_in_dim(split, 1 - y, 0, keepdims=False)
        got = swap(send.astype(BF), "y").astype(wide)
        keep = keep.astype(wide)
        return jnp.where(y == 0, jnp.stack([keep, got]), jnp.stack([got, keep]))[:, None]

    x_rows = to_local(own_rows(tokens))
    valid_count = lax.dynamic_index_in_dim(counts[:, 0], y, 0, keepdims=False)

    small = jnp.concatenate(
        [
            lax.dynamic_slice_in_dim(init_state, c * state_half, state_half, 0),
            norm_gains,
            gate_bias[None],
            jnp.zeros((12, init_state.shape[1]), BF),
        ],
        axis=0,
    )
    w_token = gather_weight(token_weights.transpose(1, 0, 2))
    small = gather_rows(small)
    w_state = gather_weight(state_weights.transpose(1, 0, 2))
    w_state_out = gather_weight(state_output[None])[0]
    w_token_out = gather_weight(token_output[None])[0]
    w_up = gather_weight(hidden_up[None])[0]
    w_down = gather_weight(hidden_down[None])[0]
    gains = small[state_half : state_half + 3].astype(F32)
    gate_open = jax.nn.sigmoid(small[state_half + 3].astype(F32))
    state_now = small[:state_half].astype(F32)

    dy_rows = to_local(own_rows(cotangent))
    dy_all = join(dy_rows)
    grad_final = lax.dynamic_slice(
        state_cotangent, (y, 0, c * state_half, 0), (1, 1, state_half, width)
    )[0, 0]
    grad_final = to_local(grad_final)

    seq_length = 4 * rows_local
    blocks = seq_length // BLOCK
    x_values = x_rows.astype(F32)
    normed_all = join(rms_forward(x_values, gains[0]))
    queries, key_rows, value_rows = [
        split_heads(mm(normed_all, w_token[part]).astype(BF)) for part in range(3)
    ]
    core_of = jnp.bitwise_xor(jnp.arange(2), c)
    block_pos = (core_of[:, None] * rows_local + jnp.arange(rows_local)[None]).reshape(-1)

    def masks(block_index):
        query_pos = block_index * BLOCK + block_pos
        key_blocks = range(max(block_index - 1, 0), block_index + 1)
        key_pos = jnp.concatenate([k * BLOCK + block_pos for k in key_blocks])
        nearby = (
            (key_pos[None, :] <= query_pos[:, None])
            & (key_pos[None, :] > query_pos[:, None] - BLOCK)
            & (key_pos < (blocks - 1) * BLOCK + valid_count)[None]
        )
        own_valid = query_pos < (blocks - 1) * BLOCK + valid_count
        allowed = jnp.concatenate([nearby, jnp.ones((BLOCK, state_rows), jnp.bool_)], axis=1)
        state_allowed = jnp.concatenate(
            [
                jnp.ones((state_rows, state_rows), jnp.bool_),
                jnp.broadcast_to(own_valid[None], (state_rows, BLOCK)),
            ],
            axis=1,
        )
        return allowed, state_allowed

    def block_keys(array, block_index):
        first = max(block_index - 1, 0)
        return jnp.concatenate(
            [rows_of_block(array, k, blocks) for k in range(first, block_index + 1)], axis=1
        )

    kept = []
    mixed_parts = []
    for b in range(blocks):
        state_norm = join(rms_forward(state_now, gains[1]))
        s_query, s_key, s_value = [
            split_heads(mm(state_norm, w_state[part]).astype(BF)) for part in range(3)
        ]
        allowed, state_allowed = masks(b)
        token_in = (
            rows_of_block(queries, b, blocks),
            jnp.concatenate([block_keys(key_rows, b), s_key], axis=1),
            jnp.concatenate([block_keys(value_rows, b), s_value], axis=1),
            allowed,
        )
        state_in = (
            s_query,
            jnp.concatenate([s_key, rows_of_block(key_rows, b, blocks)], axis=1),
            jnp.concatenate([s_value, rows_of_block(value_rows, b, blocks)], axis=1),
            state_allowed,
        )
        mixed, log_total = attend_forward(*token_in)
        mixed_parts.append(mixed)
        state_mixed, state_log = attend_forward(*state_in)
        state_flat = merge_heads(state_mixed).astype(BF)
        update = fold(mm_nt(state_flat, w_state_out))
        kept.append((state_now, state_norm, token_in, state_in, log_total, state_log, state_flat, update))
        state_now = gate_open * state_now + (1.0 - gate_open) * update
    mixed_all = merge_heads(rows_from_blocks(mixed_parts)).astype(BF)
    hidden = x_values + fold(mm_nt(mixed_all, w_token_out))
    hidden_all = join(rms_forward(hidden, gains[2]))
    up_value = mm(hidden_all, w_up)
    activated = gelu_tanh(up_value).astype(BF)
    result = (hidden + fold(mm_nt(activated, w_down))).astype(BF)
    output = to_owner(from_local(result), BF)

    final_half = from_local(state_now.astype(BF))
    final_pair = jnp.stack([final_half, swap(final_half, "y")])
    final_pair = jnp.where(y == 0, final_pair, final_pair[::-1])
    final_other = swap(final_pair, "c")
    final_state = jnp.where(
        c == 0,
        jnp.concatenate([final_pair, final_other], axis=1),
        jnp.concatenate([final_other, final_pair], axis=1),
    )[:, None]

    grad_activated = mm(dy_all, w_down).astype(BF)
    unused, gelu_pull = jax.vjp(gelu_tanh, up_value)
    grad_up = gelu_pull(grad_activated.astype(F32))[0].astype(BF)
    grad_hidden_norm = fold(mm_nt(grad_up, w_up))
    grad_hidden_down = weight_grad(dy_all, [activated])[0]
    grad_hidden_up = weight_grad(hidden_all, [grad_up])[0]
    through, gain_hidden = rms_backward(hidden, gains[2], grad_hidden_norm)
    grad_hidden = dy_rows.astype(F32) + through
    branch_all = join(grad_hidden.astype(BF))
    grad_mixed = split_heads(mm(branch_all, w_token_out).astype(BF))
    grad_token_output = weight_grad(branch_all, [mixed_all])[0]

    grad_state = grad_final.astype(F32)
    grad_gate = jnp.zeros((width,), F32)
    gain_state = jnp.zeros((width,), F32)
    query_parts = [None] * blocks
    key_parts = [0.0] * blocks
    value_parts = [0.0] * blocks
    update_all, flat_all, norm_all, proj_all = [], [], [], []
    for b in reversed(range(blocks)):
        state_before, state_norm, token_in, state_in, log_total, state_log, state_flat, update = kept[b]
        grad_update = join(((1.0 - gate_open) * grad_state).astype(BF))
        grad_gate = grad_gate + jnp.sum(grad_state * (state_before - update), axis=0)
        grad_state_mixed = split_heads(mm(grad_update, w_state_out).astype(BF))
        update_all.append(grad_update)
        flat_all.append(state_flat)
        s_dq, s_dk, s_dv = attend_backward(*state_in, state_log, grad_state_mixed)
        t_dq, t_dk, t_dv = attend_backward(*token_in, log_total, rows_of_block(grad_mixed, b, blocks))
        query_parts[b] = t_dq
        first = max(b - 1, 0)
        for k in range(first, b + 1):
            rows = slice((k - first) * BLOCK, (k - first + 1) * BLOCK)
            key_parts[k] = key_parts[k] + t_dk[:, rows]
            value_parts[k] = value_parts[k] + t_dv[:, rows]
        near = (b + 1 - first) * BLOCK
        key_parts[b] = key_parts[b] + s_dk[:, state_rows:]
        value_parts[b] = value_parts[b] + s_dv[:, state_rows:]
        grad_proj = [
            merge_heads(s_dq).astype(BF),
            merge_heads(s_dk[:, :state_rows] + t_dk[:, near:]).astype(BF),
            merge_heads(s_dv[:, :state_rows] + t_dv[:, near:]).astype(BF),
        ]
        norm_all.append(state_norm)
        proj_all.append(grad_proj)
        partial = sum(mm_nt(grad_proj[part], w_state[part]) for part in range(3))
        previous, gain_piece = rms_backward(state_before, gains[1], fold(partial))
        gain_state = gain_state + gain_piece
        grad_state = gate_open * grad_state + previous
    grad_gate = grad_gate * gate_open * (1.0 - gate_open)
    grad_state_output = weight_grad(jnp.concatenate(update_all), [jnp.concatenate(flat_all)])[0]
    grad_state_weights = weight_grad(
        jnp.concatenate(norm_all),
        [jnp.concatenate([proj[part] for proj in proj_all]) for part in range(3)],
    ).transpose(1, 0, 2)
    grad_projected = [
        merge_heads(rows_from_blocks(parts)).astype(BF)
        for parts in (query_parts, key_parts, value_parts)
    ]
    grad_normed = fold(sum(mm_nt(grad_projected[part], w_token[part]) for part in range(3)))
    grad_token_weights = weight_grad(normed_all, grad_projected).transpose(1, 0, 2)
    through, gain_token = rms_backward(x_values, gains[0], grad_normed)
    input_grad = to_owner(from_local(grad_hidden + through), F32)

    vectors = from_local(jnp.stack([gain_token, gain_state, gain_hidden, grad_gate]))
    vectors = lax.psum_scatter(vectors, ("r", "z", "x"), scatter_dimension=1, tiled=True)
    vectors = lax.psum(vectors, ("y", "c"))
    init_grad = from_local(grad_state)
    init_grad = lax.psum_scatter(init_grad, ("r", "z", "x"), scatter_dimension=1, tiled=True)
    init_grad = lax.psum(init_grad, "y")
    init_grad = lax.all_gather(init_grad, "c", axis=0, tiled=True)
    return (
        output,
        final_state,
        input_grad,
        grad_token_weights,
        grad_token_output,
        grad_state_weights,
        grad_state_output,
        grad_hidden_up,
        grad_hidden_down,
        vectors[:3],
        vectors[3],
        init_grad,
    )


def solution(mesh):
    dp, heads = mesh.devices.shape
    fine = Mesh(mesh.devices.reshape(dp // (2 * RING), RING, 2, heads // 2, 2), ("r", "z", "x", "y", "c"))
    d, h = ("r", "z", "x"), ("y", "c")
    return jax.shard_map(
        body,
        mesh=fine,
        in_specs=(
            P(None, d, h, None),
            P(None, d),
            P(d, None, h),
            P(d, h),
            P(d, None, h),
            P(d, h),
            P(d, h),
            P(d, h),
            P(None, d),
            P(d),
            P(None, d),
            P(None, d, h, None),
            P(None, d, None, None),
        ),
        out_specs=(
            P(None, d, h, None),
            P(None, d, None, None),
            P(None, d, h, None),
            P(d, None, h),
            P(d, h),
            P(d, None, h),
            P(d, h),
            P(d, h),
            P(d, h),
            P(None, d),
            P(d),
            P(None, d),
        ),
        check_vma=False,
    )
```

```python
import functools

import jax
import jax.numpy as jnp
from jax import lax
from jax.experimental import pallas as pl
from jax.experimental.pallas import tpu as pltpu
from jax.sharding import Mesh
from jax.sharding import PartitionSpec as P

HEAD_DIM = 128
BLOCK = 512
EPSILON = 1e-06
MASKED = -1e30
GELU = 0.7978845608028654
RING = 4
BF = jnp.bfloat16
F32 = jnp.float32


def swap(array, axis):
    return lax.ppermute(array, axis, [(0, 1), (1, 0)])


def turn(array, steps):
    return lax.ppermute(array, "z", [(i, (i + steps) % RING) for i in range(RING)])


def matmul(left, right, contract):
    return lax.dot_general(
        left, right, (contract, ((), ())), preferred_element_type=jnp.float32
    )


def mm(left, right):
    return matmul(left, right, ((1,), (0,)))


def mm_nt(left, right):
    return matmul(left, right, ((1,), (1,)))


def mm_tn(left, right):
    return matmul(left, right, ((0,), (0,)))


def width_places():
    z, x = lax.axis_index("z"), lax.axis_index("x")
    return [lax.rem(z - k + RING, RING) * 2 + jnp.bitwise_xor(x, dx) for dx in range(2) for k in range(RING)]


def take_pieces(array, places):
    groups = lax.axis_size("r")
    lead, width = array.shape[:-1], array.shape[-1]
    split = array.reshape(lead + (groups, len(places), width // (groups * len(places))))
    axis = len(lead) + 1
    return [lax.dynamic_index_in_dim(split, place, axis, keepdims=False) for place in places]


def to_local(array):
    pieces = take_pieces(array, width_places())
    lead = array.shape[:-1]
    return jnp.concatenate([p.reshape(lead + (-1,)) for p in pieces], axis=-1)


def from_local(array):
    z, x = lax.axis_index("z"), lax.axis_index("x")
    groups = lax.axis_size("r")
    lead, width = array.shape[:-1], array.shape[-1]
    split = array.reshape(lead + (2 * RING, groups, width // (groups * 2 * RING)))
    axis = len(lead)
    pieces = []
    for z_to in range(RING):
        for x_to in range(2):
            place = jnp.bitwise_xor(x, x_to) * RING + lax.rem(z - z_to + RING, RING)
            pieces.append(lax.dynamic_index_in_dim(split, place, axis, keepdims=False))
    return jnp.stack(pieces, axis=axis + 1).reshape(array.shape)


def gather_groups(array, axis):
    if lax.axis_size("r") == 1:
        return array
    return lax.all_gather(array, "r", axis=axis, tiled=True)


def scatter_groups(array, axis):
    if lax.axis_size("r") == 1:
        return array
    return lax.psum_scatter(array, "r", scatter_dimension=axis, tiled=True)


def call(kernel, grid, inputs, in_specs, outputs, out_specs, flops=0, exps=0, **more):
    block_bytes = sum(a.size * a.dtype.itemsize for a in inputs)
    shapes = [jax.ShapeDtypeStruct(shape, dtype) for shape, dtype in outputs]
    out_bytes = sum(s.size * s.dtype.itemsize for s in shapes)
    return pl.pallas_call(
        kernel,
        grid=grid,
        in_specs=in_specs,
        out_specs=out_specs,
        out_shape=shapes,
        compiler_params=pltpu.CompilerParams(vmem_limit_bytes=48 * 2**20),
        cost_estimate=pl.CostEstimate(
            flops=flops, bytes_accessed=block_bytes + out_bytes, transcendentals=exps
        ),
        **more,
    )(*inputs)


def whole(array):
    return pl.BlockSpec(array.shape, lambda *_: (0,) * array.ndim)


def whole_out(shape):
    return pl.BlockSpec(shape, lambda *_: (0,) * len(shape))


def stack_rows(pieces):
    half = len(pieces) // 2
    rows, width = pieces[0].shape

    def kernel(*refs):
        ins, outs, sem = refs[: len(pieces)], refs[len(pieces) : -1], refs[-1]
        copies = [
            pltpu.make_async_copy(
                piece, outs[i // half].at[pl.ds((i % half) * rows, rows)], sem.at[i]
            )
            for i, piece in enumerate(ins)
        ]
        for copy in copies:
            copy.start()
        for copy in copies:
            copy.wait()

    anywhere = pl.BlockSpec(memory_space=pl.ANY)
    return call(
        kernel,
        (),
        pieces,
        [anywhere] * len(pieces),
        [((half * rows, width), BF)] * 2,
        [anywhere] * 2,
        scratch_shapes=[pltpu.SemaphoreType.DMA((len(pieces),))],
    )


def gather_weight(shard):
    shard = gather_groups(shard, 0)
    low, high = stack_rows([shard] + [turn(shard, k) for k in range(1, RING)])
    low_x, low_y = swap(low, "x"), swap(low, "y")
    high_y, high_x = swap(high, "y"), swap(high, "x")
    low_xy, high_xy = swap(low_x, "y"), swap(high_y, "x")
    return [[[low, high], [low_x, high_x]], [[low_y, high_y], [low_xy, high_xy]]]


def flat_pieces(pieces):
    return [pieces[y][x][half] for y in range(2) for x in range(2) for half in range(2)]


def gather_rows(shard):
    if lax.axis_size("r") > 1:
        shard = lax.all_gather(shard, "r", axis=1, tiled=True)
    near = jnp.concatenate([shard] + [turn(shard, k) for k in range(1, RING)], axis=1)
    return jnp.concatenate([near, swap(near, "x")], axis=1)


def row_order(own, other, blocks):
    per = own.shape[0] // blocks
    parts = []
    for b in range(blocks):
        parts += [own[b * per : (b + 1) * per], other[b * per : (b + 1) * per]]
    return jnp.concatenate(parts, axis=0)


def project(own, other, pieces, column, width, block, blocks=1, gate=None, activate=False):
    rows = own.shape[0] * 2
    refs = flat_pieces(pieces)
    first = column // block

    def kernel(*args):
        own_ref, other_ref, weights = args[0], args[1], args[2:10]
        left = row_order(own_ref[...], other_ref[...], blocks)
        for y in range(2):
            weight = jnp.concatenate([ref[...] for ref in weights[4 * y : 4 * y + 4]], axis=0)
            total = mm(left, weight)
            if gate is not None:
                gate_ref, out_ref = args[10], args[11]
                low = total.astype(BF).astype(F32)
                out_ref[y] = (low * gate_ref[y].astype(F32)).astype(BF)
            elif activate:
                act_ref, slope_ref = args[10], args[11]
                cubic = 0.044715 * total * total * total
                inner = GELU * (total + cubic)
                curve = jnp.tanh(inner)
                act_ref[y] = (0.5 * total * (1.0 + curve)).astype(BF)
                slope = 0.5 * (1.0 + curve) + 0.5 * total * (1.0 - curve * curve) * (
                    GELU * (1.0 + 3.0 * 0.044715 * total * total)
                )
                slope_ref[y] = slope.astype(BF)
            else:
                args[10][y] = total.astype(BF)

    spec = pl.BlockSpec((2, rows, block), lambda j: (0, 0, j))
    weight_spec = [pl.BlockSpec((ref.shape[0], block), lambda j: (0, first + j)) for ref in refs]
    extra = [] if gate is None else [gate]
    count = 2 if activate else 1
    out = call(
        kernel,
        (width // block,),
        [own, other] + refs + extra,
        [whole(own), whole(other)] + weight_spec + [spec] * len(extra),
        [((2, rows, width), BF)] * count,
        [spec] * count,
        flops=4 * rows * own.shape[1] * width,
    )
    return out if activate else out[0]


def merge(lefts, pieces, column, blocks=1):
    refs = flat_pieces(pieces)
    columns = lefts[0].shape[2]
    rows = sum(left.shape[1] for left in lefts)
    width = 8 * refs[0].shape[0] // 2
    first = column // columns
    count = len(lefts)

    def kernel(*args):
        left_refs, weights = args[:count], args[count : count + 8]
        own_ref, other_ref = args[count + 8 :]
        sides = [
            jnp.concatenate([ref[...] for ref in weights[4 * y : 4 * y + 4]], axis=0) for y in range(2)
        ]
        per = rows // (2 * blocks)
        for core, out_ref in ((1, other_ref), (0, own_ref)):
            total = None
            for y in range(2):
                parts = []
                for b in range(blocks):
                    begin = (2 * b + core) * per
                    index, within = begin // left_refs[0].shape[1], begin % left_refs[0].shape[1]
                    parts.append(left_refs[index][y, within : within + per])
                piece = mm_nt(jnp.concatenate(parts, axis=0), sides[y])
                total = piece if total is None else total + piece
            out_ref[...] = total.astype(out_ref.dtype)

    weight_spec = [pl.BlockSpec((ref.shape[0], columns), lambda i: (0, first)) for ref in refs]
    return call(
        kernel,
        (1,),
        list(lefts) + refs,
        [whole(left) for left in lefts] + weight_spec,
        [((rows // 2, width), F32), ((rows // 2, width), BF)],
        [whole_out((rows // 2, width))] * 2,
        flops=4 * rows * width * columns,
    )


def outer(lefts, rights, block, blocks=1):
    width = lefts[0][0].shape[1]
    columns = rights[0].shape[2]
    half = width // 2
    count = len(lefts)
    flat = [array for pair in lefts for array in pair]

    def kernel(*args):
        left_refs, right_refs = args[: 2 * count], args[2 * count : 3 * count]
        low11, high11, out10, out01, out00 = args[3 * count :]
        left = jnp.concatenate(
            [row_order(left_refs[2 * i][...], left_refs[2 * i + 1][...], blocks) for i in range(count)], axis=0
        )
        for y in (1, 0):
            right = jnp.concatenate([ref[y] for ref in right_refs], axis=0)
            for x in (1, 0):
                total = mm_tn(left[:, x * half : (x + 1) * half], right).astype(BF)
                if x and y:
                    low11[...] = total[: half // 2]
                    high11[...] = total[half // 2 :]
                else:
                    {(1, 0): out10, (0, 1): out01, (0, 0): out00}[(x, y)][...] = total

    return call(
        kernel,
        (columns // block,),
        flat + list(rights),
        [whole(array) for array in flat]
        + [pl.BlockSpec((2, right.shape[1], block), lambda j: (0, 0, j)) for right in rights],
        [((half // 2, columns), BF)] * 2 + [((half, columns), BF)] * 3,
        [pl.BlockSpec((half // 2, block), lambda j: (0, j))] * 2
        + [pl.BlockSpec((half, block), lambda j: (0, j))] * 3,
        flops=4 * width * columns * sum(right.shape[1] for right in rights),
    )


def add_into(array, piece, half):
    rows, columns = piece.shape

    def kernel(array_ref, piece_ref, out_ref):
        out_ref[...] = (array_ref[...].astype(F32) + piece_ref[...].astype(F32)).astype(BF)

    return call(
        kernel,
        (1,),
        [array, piece],
        [pl.BlockSpec((rows, columns), lambda i: (half, 0)), pl.BlockSpec((rows, columns), lambda i: (0, 0))],
        [(array.shape, BF)],
        [pl.BlockSpec((rows, columns), lambda i: (half, 0))],
        input_output_aliases={0: 0},
    )[0]


def add_split(first, second, third):
    rows, columns = first.shape
    part = rows // RING

    def kernel(a_ref, b_ref, c_ref, *outs):
        for k, out_ref in enumerate(outs):
            piece = slice(k * part, (k + 1) * part)
            total = a_ref[piece].astype(F32) + b_ref[piece].astype(F32) + c_ref[piece].astype(F32)
            out_ref[...] = total.astype(out_ref.dtype)

    return call(
        kernel,
        (),
        [first, second, third],
        [whole(first)] * 3,
        [((part, columns), F32)] + [((part, columns), BF)] * (RING - 1),
        [whole_out((part, columns))] * RING,
    )


def reduce_weight(quarters):
    low11, high11, out10, out01, out00 = quarters
    low_got, high_got = swap(low11, "y"), swap(high11, "x")
    x_got = swap(add_into(out10, low_got, 0), "x")
    y_got = swap(add_into(out01, high_got, 1), "y")
    pieces = add_split(out00, x_got, y_got)
    total = pieces[0]
    for k in range(1, RING):
        total = total + turn(pieces[k], RING - k).astype(F32)
    return scatter_groups(total, 0)


def rms_inverse(values):
    return lax.rsqrt(jnp.mean(values * values, axis=-1, keepdims=True) + EPSILON)


def rms_forward(values, gain):
    return (values * rms_inverse(values) * gain).astype(BF)


def rms_backward(values, gain, grad):
    inverse = rms_inverse(values)
    scaled = values * inverse
    weighted = grad * gain
    grad_values = inverse * (weighted - scaled * jnp.mean(scaled * weighted, axis=-1, keepdims=True))
    return grad_values, jnp.sum(grad * scaled, axis=0)


def pair(own):
    return own, swap(own, "c")


def fold(both):
    own, other = both
    return own + swap(other, "c").astype(F32)


SCALE = HEAD_DIM ** (-0.5)


def key_tiles(b, j):
    tiles = []
    if b > 0:
        tiles += [(b - 1, jj, "after" if jj == j else "all") for jj in range(j, 2)]
    tiles += [(b, jj, "until" if jj == j else "all") for jj in range(j + 1)]
    return tiles


def tile_mask(kind, size, limit):
    rows = lax.broadcasted_iota(jnp.int32, (size, size), 0)
    columns = lax.broadcasted_iota(jnp.int32, (size, size), 1)
    mask = None
    if kind == "after":
        mask = columns > rows
    if kind == "until":
        mask = columns <= rows
    if limit is not None:
        inside = columns < limit
        mask = inside if mask is None else mask & inside
    return mask


def masked_scores(queries, keys, masks):
    scores = mm_nt(queries, keys) * SCALE
    parts, place = [], 0
    for size, mask in masks:
        part = scores[:, place : place + size]
        parts.append(part if mask is None else jnp.where(mask, part, MASKED))
        place += size
    return jnp.concatenate(parts, axis=1)


def attention_plan(b, last, size, core, count, states):
    def start(block, j):
        return pl.multiple_of(block * 2 * size + jnp.bitwise_xor(core, j) * size, size)

    plan = []
    for j in range(2):
        tiles, masks = [], []
        for block, jj, kind in key_tiles(b, j):
            limit = count - jj * size if block == b and last else None
            tiles.append((block, jj))
            masks.append((size, tile_mask(kind, size, limit)))
        plan.append((tiles, masks + [(states, None)]))
    state_masks = [(states, None)]
    for jj in range(2):
        state_masks.append((size, tile_mask("all", size, count - jj * size if last else None)))
    return start, plan, state_masks


def attend_forward(b, blocks, info, tokens, states):
    lanes = tokens.shape[2] // 3
    heads = lanes // HEAD_DIM
    size = BLOCK // 2
    count_states = states.shape[1]

    def one(queries, keys, values, masks):
        scores = masked_scores(queries, keys, masks)
        top = jnp.max(scores, axis=1, keepdims=True)
        weights = jnp.exp(scores - top)
        total = jnp.sum(weights, axis=1, keepdims=True)
        mixed = mm(weights.astype(BF), values) / total
        return mixed.astype(BF), top + jnp.log(total)

    def kernel(info_ref, token_ref, state_ref, mixed_ref, state_mixed_ref, log_ref):
        start, plan, state_masks = attention_plan(
            b, b == blocks - 1, size, info_ref[0], info_ref[1], count_states
        )
        for h in range(heads):
            query, key, value = [slice(p * lanes + h * HEAD_DIM, p * lanes + (h + 1) * HEAD_DIM) for p in range(3)]
            own = slice(h * HEAD_DIM, (h + 1) * HEAD_DIM)

            def token_rows(places, columns):
                return [token_ref[0, pl.ds(start(*place), size), columns] for place in places]

            for j, (tiles, masks) in enumerate(plan):
                keys = jnp.concatenate(token_rows(tiles, key) + [state_ref[0, :, key]], axis=0)
                values = jnp.concatenate(token_rows(tiles, value) + [state_ref[0, :, value]], axis=0)
                mixed, log_total = one(token_ref[0, pl.ds(start(b, j), size), query], keys, values, masks)
                mixed_ref[0, pl.ds(start(0, j), size), own] = mixed
                log_ref[0, pl.ds(start(0, j), size), h : h + 1] = log_total
            tiles = [(b, 0), (b, 1)]
            keys = jnp.concatenate([state_ref[0, :, key]] + token_rows(tiles, key), axis=0)
            values = jnp.concatenate([state_ref[0, :, value]] + token_rows(tiles, value), axis=0)
            for begin in range(0, count_states, size):
                rows = slice(begin, begin + size)
                mixed, log_total = one(state_ref[0, rows, query], keys, values, state_masks)
                state_mixed_ref[0, rows, own] = mixed
                log_ref[0, rows, heads + h : heads + h + 1] = log_total

    rows = (b + 1) * BLOCK
    pairs = 2 * heads * (BLOCK * (BLOCK * (2 if b else 1) + count_states) + count_states * (count_states + BLOCK))
    spec = lambda n, w: pl.BlockSpec((1, n, w), lambda y: (y, 0, 0))
    return call(
        kernel,
        (2,),
        [info, tokens, states],
        [pl.BlockSpec(memory_space=pltpu.SMEM), spec(rows, 3 * lanes), spec(count_states, 3 * lanes)],
        [((2, BLOCK, lanes), BF), ((2, count_states, lanes), BF), ((2, BLOCK, 128), F32)],
        [spec(BLOCK, lanes), spec(count_states, lanes), spec(BLOCK, 128)],
        flops=4 * pairs * HEAD_DIM,
        exps=pairs,
    )


def attend_backward(b, blocks, info, tokens, states, logs, grad_mixed, grad_state_mixed, later):
    lanes = tokens.shape[2] // 3
    heads = lanes // HEAD_DIM
    size = BLOCK // 2
    count_states = states.shape[1]
    is_last = b == blocks - 1

    def one(queries, keys, values, masks, log_total, grad):
        scores = masked_scores(queries, keys, masks)
        probs = jnp.exp(scores - log_total)
        grad_probs = mm_nt(grad, values)
        row_sum = jnp.sum(grad_probs * probs, axis=1, keepdims=True)
        low = (probs * (grad_probs - row_sum)).astype(BF)
        return mm(low, keys) * SCALE, mm_tn(low, queries) * SCALE, mm_tn(probs.astype(BF), grad)

    def kernel(*args):
        info_ref, token_ref, state_ref, log_ref, grad_ref, state_grad_ref = args[:6]
        rest = list(args[6:])
        later_ref = None if is_last else rest.pop(0)
        out_ref, state_out_ref = rest.pop(0), rest.pop(0)
        before_ref = rest.pop(0) if b > 0 else None
        start, plan, state_masks = attention_plan(b, is_last, size, info_ref[0], info_ref[1], count_states)
        for h in range(heads):
            query, key, value = [slice(p * lanes + h * HEAD_DIM, p * lanes + (h + 1) * HEAD_DIM) for p in range(3)]
            own = slice(h * HEAD_DIM, (h + 1) * HEAD_DIM)

            def token_rows(places, columns):
                return [token_ref[0, pl.ds(start(*place), size), columns] for place in places]

            sums = {}

            def gather(places, grads):
                begin = 0
                for place in places:
                    rows = count_states if place == "state" else size
                    part = grads[begin : begin + rows]
                    begin += rows
                    yield place, part

            def collect(name, places, grads):
                for place, part in gather(places, grads):
                    full = (name, place)
                    sums[full] = part if full not in sums else sums[full] + part

            places = ["state", (b, 0), (b, 1)]
            keys = jnp.concatenate([state_ref[0, :, key]] + token_rows(places[1:], key), axis=0)
            values = jnp.concatenate([state_ref[0, :, value]] + token_rows(places[1:], value), axis=0)
            for begin in range(0, count_states, size):
                rows = slice(begin, begin + size)
                dq, dk, dv = one(
                    state_ref[0, rows, query],
                    keys,
                    values,
                    state_masks,
                    log_ref[0, rows, heads + h : heads + h + 1],
                    state_grad_ref[0, rows, own],
                )
                state_out_ref[0, rows, query] = dq.astype(BF)
                collect("k", places, dk)
                collect("v", places, dv)
            for j, (tiles, masks) in enumerate(plan):
                keys = jnp.concatenate(token_rows(tiles, key) + [state_ref[0, :, key]], axis=0)
                values = jnp.concatenate(token_rows(tiles, value) + [state_ref[0, :, value]], axis=0)
                here = pl.ds(start(0, j), size)
                dq, dk, dv = one(
                    token_ref[0, pl.ds(start(b, j), size), query],
                    keys,
                    values,
                    masks,
                    log_ref[0, here, h : h + 1],
                    grad_ref[0, here, own],
                )
                out_ref[0, here, query] = dq.astype(BF)
                collect("k", tiles + ["state"], dk)
                collect("v", tiles + ["state"], dv)
            state_out_ref[0, :, key] = sums[("k", "state")].astype(BF)
            state_out_ref[0, :, value] = sums[("v", "state")].astype(BF)
            for name, columns in (("k", key), ("v", value)):
                shift = slice(columns.start - lanes, columns.stop - lanes)
                for j in range(2):
                    here = pl.ds(start(0, j), size)
                    total = sums[(name, (b, j))]
                    if later_ref is not None:
                        total = total + later_ref[0, here, shift]
                    out_ref[0, here, columns] = total.astype(BF)
                    if before_ref is not None:
                        before_ref[0, here, shift] = sums[(name, (b - 1, j))]

    rows = (b + 1) * BLOCK
    pairs = 2 * heads * (BLOCK * (BLOCK * (2 if b else 1) + count_states) + count_states * (count_states + BLOCK))
    spec = lambda n, w: pl.BlockSpec((1, n, w), lambda y: (y, 0, 0))
    inputs = [info, tokens, states, logs, grad_mixed, grad_state_mixed]
    in_specs = [
        pl.BlockSpec(memory_space=pltpu.SMEM),
        spec(rows, 3 * lanes),
        spec(count_states, 3 * lanes),
        spec(BLOCK, 128),
        pl.BlockSpec((1, BLOCK, lanes), lambda y: (y, b, 0)),
        spec(count_states, lanes),
    ]
    outputs = [((2, BLOCK, 3 * lanes), BF), ((2, count_states, 3 * lanes), BF)]
    out_specs = [spec(BLOCK, 3 * lanes), spec(count_states, 3 * lanes)]
    if not is_last:
        inputs.append(later)
        in_specs.append(spec(BLOCK, 2 * lanes))
    if b > 0:
        outputs.append(((2, BLOCK, 2 * lanes), F32))
        out_specs.append(spec(BLOCK, 2 * lanes))
    out = call(
        kernel, (2,), inputs, in_specs, outputs, out_specs, flops=10 * pairs * HEAD_DIM, exps=pairs
    )
    return out if b > 0 else (out[0], out[1], None)


def body(
    tokens,
    counts,
    token_weights,
    token_output,
    state_weights,
    state_output,
    hidden_up,
    hidden_down,
    norm_gains,
    gate_bias,
    init_state,
    cotangent,
    state_cotangent,
):
    y, c = lax.axis_index("y"), lax.axis_index("c")
    micro, rows_local, width = tokens.shape[0], tokens.shape[2], tokens.shape[3]
    state_rows = init_state.shape[0]
    state_half = state_rows // 2

    def own_rows(array):
        keep = lax.dynamic_index_in_dim(array[:, 0], y, 0, keepdims=False)
        send = lax.dynamic_index_in_dim(array[:, 0], 1 - y, 0, keepdims=False)
        got = swap(send, "y")
        return jnp.where(y == 0, jnp.concatenate([keep, got]), jnp.concatenate([got, keep]))

    def to_owner(rows, wide):
        split = rows.reshape(2, rows_local, width)
        keep = lax.dynamic_index_in_dim(split, y, 0, keepdims=False)
        send = lax.dynamic_index_in_dim(split, 1 - y, 0, keepdims=False)
        got = swap(send.astype(BF), "y").astype(wide)
        keep = keep.astype(wide)
        return jnp.where(y == 0, jnp.stack([keep, got]), jnp.stack([got, keep]))[:, None]

    x_rows = to_local(own_rows(tokens))
    valid_count = lax.dynamic_index_in_dim(counts[:, 0], y, 0, keepdims=False)

    small = jnp.concatenate(
        [
            lax.dynamic_slice_in_dim(init_state, c * state_half, state_half, 0),
            norm_gains,
            gate_bias[None],
            jnp.zeros((12, init_state.shape[1]), BF),
        ],
        axis=0,
    )
    shard_rows = token_output.shape[0]
    flat = lambda array: array.reshape(shard_rows, -1)
    small = gather_rows(small)
    w_token = gather_weight(flat(token_weights))
    w_mid = gather_weight(jnp.concatenate([flat(state_weights), state_output, token_output], axis=1))
    w_up = gather_weight(hidden_up)
    w_down = gather_weight(hidden_down)
    head = token_output.shape[1]
    at_state, at_state_out, at_token_out = 0, 3 * head, 4 * head
    gains = small[state_half : state_half + 3].astype(F32)
    gate_open = jax.nn.sigmoid(small[state_half + 3].astype(F32))
    state_now = small[:state_half].astype(F32)

    dy_rows = to_local(own_rows(cotangent))
    dy_pair = pair(dy_rows)
    grad_final = lax.dynamic_slice(
        state_cotangent, (y, 0, c * state_half, 0), (1, 1, state_half, width)
    )[0, 0]
    grad_final = to_local(grad_final)

    seq_length = 4 * rows_local
    blocks = seq_length // BLOCK
    info = jnp.stack([c, valid_count]).astype(jnp.int32)
    x_values = x_rows.astype(F32)
    normed = pair(rms_forward(x_values, gains[0]))
    token_proj = project(*normed, w_token, 0, 3 * head, 3 * head // 2, blocks=blocks)

    kept = []
    mixed = []
    for b in range(blocks):
        state_norm = pair(rms_forward(state_now, gains[1]))
        state_proj = project(*state_norm, w_mid, at_state, 3 * head, 3 * head)
        mixed_b, state_flat, logs = attend_forward(b, blocks, info, token_proj, state_proj)
        mixed.append(mixed_b)
        update = fold(merge([state_flat], w_mid, at_state_out))
        kept.append((state_now, state_norm, state_proj, logs, state_flat, update))
        state_now = gate_open * state_now + (1.0 - gate_open) * update
    hidden = x_values + fold(merge(mixed, w_mid, at_token_out, blocks=blocks))
    hidden_norm = pair(rms_forward(hidden, gains[2]))
    ff = hidden_up.shape[1]
    activated, slope = project(*hidden_norm, w_up, 0, ff, ff // 2, activate=True)
    result = (hidden + fold(merge([activated], w_down, 0))).astype(BF)
    output = to_owner(from_local(result), BF)

    final_half = from_local(state_now.astype(BF))
    final_pair = jnp.stack([final_half, swap(final_half, "y")])
    final_pair = jnp.where(y == 0, final_pair, final_pair[::-1])
    final_other = swap(final_pair, "c")
    final_state = jnp.where(
        c == 0,
        jnp.concatenate([final_pair, final_other], axis=1),
        jnp.concatenate([final_other, final_pair], axis=1),
    )[:, None]

    grad_hidden_down = reduce_weight(outer([dy_pair], [activated], ff // 2))
    grad_up = project(*dy_pair, w_down, 0, ff, ff // 2, gate=slope)
    grad_hidden_norm = fold(merge([grad_up], w_up, 0))
    grad_hidden_up = reduce_weight(outer([hidden_norm], [grad_up], ff // 2))
    through, gain_hidden = rms_backward(hidden, gains[2], grad_hidden_norm)
    grad_hidden = dy_rows.astype(F32) + through
    branch = pair(grad_hidden.astype(BF))
    grad_mixed = project(*branch, w_mid, at_token_out, head, head, blocks=blocks)
    grad_token_output = reduce_weight(
        outer([branch], [jnp.concatenate(mixed, axis=1)], head, blocks=blocks)
    )

    grad_state = grad_final.astype(F32)
    grad_gate = jnp.zeros((width,), F32)
    gain_state = jnp.zeros((width,), F32)
    proj_grads = [None] * blocks
    update_all, flat_all, norm_all, state_grads = [], [], [], []
    later = None
    for b in reversed(range(blocks)):
        state_before, state_norm, state_proj, logs, state_flat, update = kept[b]
        grad_update = pair(((1.0 - gate_open) * grad_state).astype(BF))
        grad_gate = grad_gate + jnp.sum(grad_state * (state_before - update), axis=0)
        grad_state_mixed = project(*grad_update, w_mid, at_state_out, head, head)
        proj_grads[b], state_grad, later = attend_backward(
            b, blocks, info, token_proj, state_proj, logs, grad_mixed, grad_state_mixed, later
        )
        update_all.append(grad_update)
        flat_all.append(state_flat)
        norm_all.append(state_norm)
        state_grads.append(state_grad)
        partial = merge([state_grad], w_mid, at_state)
        previous, gain_piece = rms_backward(state_before, gains[1], fold(partial))
        gain_state = gain_state + gain_piece
        grad_state = gate_open * grad_state + previous
    grad_gate = grad_gate * gate_open * (1.0 - gate_open)
    grad_state_output = reduce_weight(outer(update_all, flat_all, head))
    grad_state_weights = reduce_weight(outer(norm_all, state_grads, 3 * head)).reshape(-1, 3, head)
    grad_normed = fold(merge(proj_grads, w_token, 0, blocks=blocks))
    grad_token_weights = reduce_weight(
        outer([normed], [jnp.concatenate(proj_grads, axis=1)], 3 * head, blocks=blocks)
    ).reshape(-1, 3, head)
    through, gain_token = rms_backward(x_values, gains[0], grad_normed)
    input_grad = to_owner(from_local(grad_hidden + through), F32)

    vectors = from_local(jnp.stack([gain_token, gain_state, gain_hidden, grad_gate]))
    vectors = lax.psum_scatter(vectors, ("r", "z", "x"), scatter_dimension=1, tiled=True)
    vectors = lax.psum(vectors, ("y", "c"))
    init_grad = from_local(grad_state)
    init_grad = lax.psum_scatter(init_grad, ("r", "z", "x"), scatter_dimension=1, tiled=True)
    init_grad = lax.psum(init_grad, "y")
    init_grad = lax.all_gather(init_grad, "c", axis=0, tiled=True)
    return (
        output,
        final_state,
        input_grad,
        grad_token_weights,
        grad_token_output,
        grad_state_weights,
        grad_state_output,
        grad_hidden_up,
        grad_hidden_down,
        vectors[:3],
        vectors[3],
        init_grad,
    )


def solution(mesh):
    dp, heads = mesh.devices.shape
    fine = Mesh(mesh.devices.reshape(dp // (2 * RING), RING, 2, heads // 2, 2), ("r", "z", "x", "y", "c"))
    d, h = ("r", "z", "x"), ("y", "c")
    return jax.shard_map(
        body,
        mesh=fine,
        in_specs=(
            P(None, d, h, None),
            P(None, d),
            P(d, None, h),
            P(d, h),
            P(d, None, h),
            P(d, h),
            P(d, h),
            P(d, h),
            P(None, d),
            P(d),
            P(None, d),
            P(None, d, h, None),
            P(None, d, None, None),
        ),
        out_specs=(
            P(None, d, h, None),
            P(None, d, None, None),
            P(None, d, h, None),
            P(d, None, h),
            P(d, h),
            P(d, None, h),
            P(d, h),
            P(d, h),
            P(d, h),
            P(None, d),
            P(d),
            P(None, d),
        ),
        check_vma=False,
    )
```

```python
import functools

import jax
import jax.numpy as jnp
from jax import lax
from jax.experimental import pallas as pl
from jax.experimental.pallas import tpu as pltpu
from jax.sharding import Mesh
from jax.sharding import PartitionSpec as P

HEAD_DIM = 128
BLOCK = 512
EPSILON = 1e-06
MASKED = -1e30
GELU = 0.7978845608028654
RING = 4
BF = jnp.bfloat16
F32 = jnp.float32


def swap(array, axis):
    return lax.ppermute(array, axis, [(0, 1), (1, 0)])


def turn(array, steps):
    return lax.ppermute(array, "z", [(i, (i + steps) % RING) for i in range(RING)])


def matmul(left, right, contract):
    return lax.dot_general(
        left, right, (contract, ((), ())), preferred_element_type=jnp.float32
    )


def mm(left, right):
    return matmul(left, right, ((1,), (0,)))


def mm_nt(left, right):
    return matmul(left, right, ((1,), (1,)))


def mm_tn(left, right):
    return matmul(left, right, ((0,), (0,)))


def width_places():
    z, x = lax.axis_index("z"), lax.axis_index("x")
    return [lax.rem(z - k + RING, RING) * 2 + jnp.bitwise_xor(x, dx) for dx in range(2) for k in range(RING)]


def take_pieces(array, places):
    groups = lax.axis_size("r")
    lead, width = array.shape[:-1], array.shape[-1]
    split = array.reshape(lead + (groups, len(places), width // (groups * len(places))))
    axis = len(lead) + 1
    return [lax.dynamic_index_in_dim(split, place, axis, keepdims=False) for place in places]


def to_local(array):
    pieces = take_pieces(array, width_places())
    lead = array.shape[:-1]
    return jnp.concatenate([p.reshape(lead + (-1,)) for p in pieces], axis=-1)


def from_local(array):
    z, x = lax.axis_index("z"), lax.axis_index("x")
    groups = lax.axis_size("r")
    lead, width = array.shape[:-1], array.shape[-1]
    split = array.reshape(lead + (2 * RING, groups, width // (groups * 2 * RING)))
    axis = len(lead)
    pieces = []
    for z_to in range(RING):
        for x_to in range(2):
            place = jnp.bitwise_xor(x, x_to) * RING + lax.rem(z - z_to + RING, RING)
            pieces.append(lax.dynamic_index_in_dim(split, place, axis, keepdims=False))
    return jnp.stack(pieces, axis=axis + 1).reshape(array.shape)


def gather_groups(array, axis):
    if lax.axis_size("r") == 1:
        return array
    return lax.all_gather(array, "r", axis=axis, tiled=True)


def scatter_groups(array, axis):
    if lax.axis_size("r") == 1:
        return array
    return lax.psum_scatter(array, "r", scatter_dimension=axis, tiled=True)


def call(kernel, grid, inputs, in_specs, outputs, out_specs, flops=0, exps=0, **more):
    block_bytes = sum(a.size * a.dtype.itemsize for a in inputs)
    shapes = [jax.ShapeDtypeStruct(shape, dtype) for shape, dtype in outputs]
    out_bytes = sum(s.size * s.dtype.itemsize for s in shapes)
    return pl.pallas_call(
        kernel,
        grid=grid,
        in_specs=in_specs,
        out_specs=out_specs,
        out_shape=shapes,
        compiler_params=pltpu.CompilerParams(vmem_limit_bytes=48 * 2**20),
        cost_estimate=pl.CostEstimate(
            flops=flops, bytes_accessed=block_bytes + out_bytes, transcendentals=exps
        ),
        **more,
    )(*inputs)


def whole(array):
    return pl.BlockSpec(array.shape, lambda *_: (0,) * array.ndim)


def whole_out(shape):
    return pl.BlockSpec(shape, lambda *_: (0,) * len(shape))


def stack_rows(pieces):
    half = len(pieces) // 2
    rows, width = pieces[0].shape

    def kernel(*refs):
        ins, outs = refs[: len(pieces)], refs[len(pieces) :]
        for i, piece in enumerate(ins):
            outs[i // half][(i % half) * rows : (i % half + 1) * rows] = piece[...]

    return call(
        kernel,
        (1,),
        pieces,
        [whole(piece) for piece in pieces],
        [((half * rows, width), BF)] * 2,
        [whole_out((half * rows, width))] * 2,
    )


def gather_weight(shard):
    shard = gather_groups(shard, 0)
    low, high = stack_rows([shard] + [turn(shard, k) for k in range(1, RING)])
    low_x, low_y = swap(low, "x"), swap(low, "y")
    high_y, high_x = swap(high, "y"), swap(high, "x")
    low_xy, high_xy = swap(low_x, "y"), swap(high_y, "x")
    return [[[low, high], [low_x, high_x]], [[low_y, high_y], [low_xy, high_xy]]]


def flat_pieces(pieces):
    return [pieces[y][x][half] for y in range(2) for x in range(2) for half in range(2)]


def gather_rows(shard):
    if lax.axis_size("r") > 1:
        shard = lax.all_gather(shard, "r", axis=1, tiled=True)
    near = jnp.concatenate([shard] + [turn(shard, k) for k in range(1, RING)], axis=1)
    return jnp.concatenate([near, swap(near, "x")], axis=1)


def row_order(own, other, blocks):
    per = own.shape[0] // blocks
    parts = []
    for b in range(blocks):
        parts += [own[b * per : (b + 1) * per], other[b * per : (b + 1) * per]]
    return jnp.concatenate(parts, axis=0)


def project(own, other, pieces, column, width, block, blocks=1, gate=None, activate=False):
    rows = own.shape[0] * 2
    refs = flat_pieces(pieces)
    first = column // block

    def kernel(*args):
        own_ref, other_ref, weights = args[0], args[1], args[2:10]
        left = row_order(own_ref[...], other_ref[...], blocks)
        for y in range(2):
            weight = jnp.concatenate([ref[...] for ref in weights[4 * y : 4 * y + 4]], axis=0)
            total = mm(left, weight)
            if gate is not None:
                gate_ref, out_ref = args[10], args[11]
                low = total.astype(BF).astype(F32)
                out_ref[y] = (low * gate_ref[y].astype(F32)).astype(BF)
            elif activate:
                act_ref, slope_ref = args[10], args[11]
                cubic = 0.044715 * total * total * total
                inner = GELU * (total + cubic)
                curve = jnp.tanh(inner)
                act_ref[y] = (0.5 * total * (1.0 + curve)).astype(BF)
                slope = 0.5 * (1.0 + curve) + 0.5 * total * (1.0 - curve * curve) * (
                    GELU * (1.0 + 3.0 * 0.044715 * total * total)
                )
                slope_ref[y] = slope.astype(BF)
            else:
                args[10][y] = total.astype(BF)

    spec = pl.BlockSpec((2, rows, block), lambda j: (0, 0, j))
    weight_spec = [pl.BlockSpec((ref.shape[0], block), lambda j: (0, first + j)) for ref in refs]
    extra = [] if gate is None else [gate]
    count = 2 if activate else 1
    out = call(
        kernel,
        (width // block,),
        [own, other] + refs + extra,
        [whole(own), whole(other)] + weight_spec + [spec] * len(extra),
        [((2, rows, width), BF)] * count,
        [spec] * count,
        flops=4 * rows * own.shape[1] * width,
    )
    return out if activate else out[0]


def merge(lefts, pieces, column, blocks=1):
    refs = flat_pieces(pieces)
    columns = lefts[0].shape[2]
    rows = sum(left.shape[1] for left in lefts)
    width = 8 * refs[0].shape[0] // 2
    first = column // columns
    count = len(lefts)

    def kernel(*args):
        left_refs, weights = args[:count], args[count : count + 8]
        own_ref, other_ref = args[count + 8 :]
        sides = [
            jnp.concatenate([ref[...] for ref in weights[4 * y : 4 * y + 4]], axis=0) for y in range(2)
        ]
        per = rows // (2 * blocks)
        for core, out_ref in ((1, other_ref), (0, own_ref)):
            total = None
            for y in range(2):
                parts = []
                for b in range(blocks):
                    begin = (2 * b + core) * per
                    index, within = begin // left_refs[0].shape[1], begin % left_refs[0].shape[1]
                    parts.append(left_refs[index][y, within : within + per])
                piece = mm_nt(jnp.concatenate(parts, axis=0), sides[y])
                total = piece if total is None else total + piece
            out_ref[...] = total.astype(out_ref.dtype)

    weight_spec = [pl.BlockSpec((ref.shape[0], columns), lambda i: (0, first)) for ref in refs]
    return call(
        kernel,
        (1,),
        list(lefts) + refs,
        [whole(left) for left in lefts] + weight_spec,
        [((rows // 2, width), F32), ((rows // 2, width), BF)],
        [whole_out((rows // 2, width))] * 2,
        flops=4 * rows * width * columns,
    )


def outer(lefts, rights, block, blocks=1):
    width = lefts[0][0].shape[1]
    columns = rights[0].shape[2]
    half = width // 2
    count = len(lefts)
    flat = [array for pair in lefts for array in pair]

    def kernel(*args):
        left_refs, right_refs = args[: 2 * count], args[2 * count : 3 * count]
        low11, high11, out10, out01, out00 = args[3 * count :]
        left = jnp.concatenate(
            [row_order(left_refs[2 * i][...], left_refs[2 * i + 1][...], blocks) for i in range(count)], axis=0
        )
        for y in (1, 0):
            right = jnp.concatenate([ref[y] for ref in right_refs], axis=0)
            for x in (1, 0):
                total = mm_tn(left[:, x * half : (x + 1) * half], right).astype(BF)
                if x and y:
                    low11[...] = total[: half // 2]
                    high11[...] = total[half // 2 :]
                else:
                    {(1, 0): out10, (0, 1): out01, (0, 0): out00}[(x, y)][...] = total

    return call(
        kernel,
        (columns // block,),
        flat + list(rights),
        [whole(array) for array in flat]
        + [pl.BlockSpec((2, right.shape[1], block), lambda j: (0, 0, j)) for right in rights],
        [((half // 2, columns), BF)] * 2 + [((half, columns), BF)] * 3,
        [pl.BlockSpec((half // 2, block), lambda j: (0, j))] * 2
        + [pl.BlockSpec((half, block), lambda j: (0, j))] * 3,
        flops=4 * width * columns * sum(right.shape[1] for right in rights),
    )


def add_into(array, piece, half):
    rows, columns = piece.shape

    def kernel(array_ref, piece_ref, out_ref):
        out_ref[...] = (array_ref[...].astype(F32) + piece_ref[...].astype(F32)).astype(BF)

    return call(
        kernel,
        (1,),
        [array, piece],
        [pl.BlockSpec((rows, columns), lambda i: (half, 0)), pl.BlockSpec((rows, columns), lambda i: (0, 0))],
        [(array.shape, BF)],
        [pl.BlockSpec((rows, columns), lambda i: (half, 0))],
        input_output_aliases={0: 0},
    )[0]


def add_split(first, second, third):
    rows, columns = first.shape
    part = rows // RING

    def kernel(a_ref, b_ref, c_ref, *outs):
        for k, out_ref in enumerate(outs):
            piece = slice(k * part, (k + 1) * part)
            total = a_ref[piece].astype(F32) + b_ref[piece].astype(F32) + c_ref[piece].astype(F32)
            out_ref[...] = total.astype(out_ref.dtype)

    return call(
        kernel,
        (),
        [first, second, third],
        [whole(first)] * 3,
        [((part, columns), F32)] + [((part, columns), BF)] * (RING - 1),
        [whole_out((part, columns))] * RING,
    )


def reduce_weight(quarters):
    low11, high11, out10, out01, out00 = quarters
    low_got, high_got = swap(low11, "y"), swap(high11, "x")
    x_got = swap(add_into(out10, low_got, 0), "x")
    y_got = swap(add_into(out01, high_got, 1), "y")
    pieces = add_split(out00, x_got, y_got)
    total = pieces[0]
    for k in range(1, RING):
        total = total + turn(pieces[k], RING - k).astype(F32)
    return scatter_groups(total, 0)


def pair(own):
    return own, swap(own, "c")


INFO = 3
PIECES = 2 * RING


def smem():
    return pl.BlockSpec(memory_space=pltpu.SMEM)


def lanes_at(info_ref, index, width):
    size = width // PIECES
    return pl.ds(pl.multiple_of(info_ref[index] * size, size), size)


def reorder_in(info_ref, source, target, rows=slice(None)):
    width = source.shape[-1]
    size = width // PIECES
    for k in range(PIECES):
        target[rows, k * size : (k + 1) * size] = source[:, lanes_at(info_ref, INFO + k, width)].astype(target.dtype)


def reorder_out(info_ref, source, target, rows=slice(None)):
    width = source.shape[-1]
    size = width // PIECES
    for k in range(PIECES):
        part = source[rows, lanes_at(info_ref, INFO + PIECES + k, width)]
        target[:, k * size : (k + 1) * size] = part.astype(target.dtype)


def inverse_rms(values):
    return lax.rsqrt(jnp.mean(values * values, axis=-1, keepdims=True) + EPSILON)


def rms_back(values, gain, grad):
    inverse = inverse_rms(values)
    scaled = values * inverse
    weighted = grad * gain
    back = inverse * (weighted - scaled * jnp.mean(scaled * weighted, axis=-1, keepdims=True))
    return back, jnp.sum(grad * scaled, axis=0, keepdims=True)


def rowwise(kernel, inputs, outputs, scratch=()):
    return call(
        kernel,
        (1,),
        inputs,
        [smem()] + [whole(array) for array in inputs[1:]],
        outputs,
        [whole_out(shape) for shape, _ in outputs],
        scratch_shapes=[pltpu.VMEM(shape, dtype) for shape, dtype in scratch],
    )


def own_rows(info, keep, got):
    rows, width = keep.shape

    def kernel(info_ref, keep_ref, got_ref, out_ref):
        y = info_ref[2]
        reorder_in(info_ref, keep_ref, out_ref, pl.ds(pl.multiple_of(y * rows, rows), rows))
        reorder_in(info_ref, got_ref, out_ref, pl.ds(pl.multiple_of((1 - y) * rows, rows), rows))

    return rowwise(kernel, [info, keep, got], [((2 * rows, width), BF)])[0]


def local_rows(info, array):
    def kernel(info_ref, in_ref, out_ref):
        reorder_in(info_ref, in_ref, out_ref)

    return rowwise(kernel, [info, array], [(array.shape, array.dtype)])[0]


def norm_rows(info, values, gain):
    def kernel(info_ref, in_ref, gain_ref, out_ref):
        rows = in_ref[...].astype(F32)
        out_ref[...] = (rows * inverse_rms(rows) * gain_ref[...]).astype(BF)

    return rowwise(kernel, [info, values, gain], [(values.shape, BF)])[0]


def add_norm(info, rows, both, gain):
    own, other = both

    def kernel(info_ref, row_ref, own_ref, got_ref, gain_ref, hidden_ref, norm_ref):
        hidden = row_ref[...].astype(F32) + (own_ref[...] + got_ref[...].astype(F32))
        hidden_ref[...] = hidden
        norm_ref[...] = (hidden * inverse_rms(hidden) * gain_ref[...]).astype(BF)

    return rowwise(kernel, [info, rows, own, swap(other, "c"), gain], [(rows.shape, F32), (rows.shape, BF)])


def add_out(info, hidden, both):
    own, other = both
    rows, width = hidden.shape
    half = rows // 2

    def kernel(info_ref, hidden_ref, own_ref, got_ref, keep_ref, send_ref, scratch):
        y = info_ref[2]
        scratch[...] = hidden_ref[...] + (own_ref[...] + got_ref[...].astype(F32))
        reorder_out(info_ref, scratch, keep_ref, pl.ds(pl.multiple_of(y * half, half), half))
        reorder_out(info_ref, scratch, send_ref, pl.ds(pl.multiple_of((1 - y) * half, half), half))

    return rowwise(
        kernel,
        [info, hidden, own, swap(other, "c")],
        [((half, width), BF)] * 2,
        [((rows, width), F32)],
    )


def step_state(info, state, both, gate, gain):
    own, other = both

    def kernel(info_ref, state_ref, own_ref, got_ref, gate_ref, gain_ref, next_ref, norm_ref, update_ref):
        update = own_ref[...] + got_ref[...].astype(F32)
        update_ref[...] = update
        after = gate_ref[...] * state_ref[...] + (1.0 - gate_ref[...]) * update
        next_ref[...] = after
        norm_ref[...] = (after * inverse_rms(after) * gain_ref[...]).astype(BF)

    return rowwise(
        kernel,
        [info, state, own, swap(other, "c"), gate, gain],
        [(state.shape, F32), (state.shape, BF), (state.shape, F32)],
    )


def last_state(info, state, both, gate):
    own, other = both

    def kernel(info_ref, state_ref, own_ref, got_ref, gate_ref, final_ref, update_ref, scratch):
        update = own_ref[...] + got_ref[...].astype(F32)
        update_ref[...] = update
        scratch[...] = gate_ref[...] * state_ref[...] + (1.0 - gate_ref[...]) * update
        reorder_out(info_ref, scratch, final_ref)

    return rowwise(
        kernel,
        [info, state, own, swap(other, "c"), gate],
        [(state.shape, BF), (state.shape, F32)],
        [(state.shape, F32)],
    )


def back_hidden(info, hidden, both, gain, dy):
    own, other = both

    def kernel(info_ref, hidden_ref, own_ref, got_ref, gain_ref, dy_ref, grad_ref, branch_ref, gain_grad_ref):
        grad = own_ref[...] + got_ref[...].astype(F32)
        back, gain_grad_ref[...] = rms_back(hidden_ref[...], gain_ref[...], grad)
        total = dy_ref[...].astype(F32) + back
        grad_ref[...] = total
        branch_ref[...] = total.astype(BF)

    return rowwise(
        kernel,
        [info, hidden, own, swap(other, "c"), gain, dy],
        [(hidden.shape, F32), (hidden.shape, BF), ((1, hidden.shape[1]), F32)],
    )


def back_update(info, grad, gate):
    def kernel(info_ref, grad_ref, gate_ref, out_ref):
        out_ref[...] = ((1.0 - gate_ref[...]) * grad_ref[...].astype(F32)).astype(BF)

    return rowwise(kernel, [info, grad, gate], [(grad.shape, BF)])[0]


def back_state(info, grad, state, update, both, gate, gain):
    own, other = both
    width = state.shape[1]

    def kernel(
        info_ref, grad_ref, state_ref, update_ref, own_ref, got_ref, gate_ref, gain_ref, out_ref, low_ref, gain_grad_ref, gate_grad_ref
    ):
        gate_open = gate_ref[...]
        grad_now = grad_ref[...].astype(F32)
        values = state_ref[...]
        gate_grad_ref[...] = jnp.sum(grad_now * (values - update_ref[...]), axis=0, keepdims=True) * (
            gate_open * (1.0 - gate_open)
        )
        back, gain_grad_ref[...] = rms_back(values, gain_ref[...], own_ref[...] + got_ref[...].astype(F32))
        total = gate_open * grad_now + back
        out_ref[...] = total
        low_ref[...] = ((1.0 - gate_open) * total).astype(BF)

    return rowwise(
        kernel,
        [info, grad, state, update, own, swap(other, "c"), gate, gain],
        [(state.shape, F32), (state.shape, BF), ((1, width), F32), ((1, width), F32)],
    )


def back_input(info, values, both, gain, grad_hidden):
    own, other = both
    rows, width = values.shape
    half = rows // 2

    def kernel(info_ref, value_ref, own_ref, got_ref, gain_ref, grad_ref, keep_ref, send_ref, gain_grad_ref, scratch):
        y = info_ref[2]
        grad = own_ref[...] + got_ref[...].astype(F32)
        back, gain_grad_ref[...] = rms_back(value_ref[...].astype(F32), gain_ref[...], grad)
        scratch[...] = grad_ref[...] + back
        reorder_out(info_ref, scratch, keep_ref, pl.ds(pl.multiple_of(y * half, half), half))
        reorder_out(info_ref, scratch, send_ref, pl.ds(pl.multiple_of((1 - y) * half, half), half))

    return rowwise(
        kernel,
        [info, values, own, swap(other, "c"), gain, grad_hidden],
        [((half, width), F32), ((half, width), BF), ((1, width), F32)],
        [((rows, width), F32)],
    )


def place_rows(info, keep, got):
    shape = (2,) + keep.shape

    def kernel(info_ref, keep_ref, got_ref, out_ref):
        y = info_ref[2]
        out_ref[y] = keep_ref[...]
        out_ref[1 - y] = got_ref[...].astype(keep.dtype)

    return rowwise(kernel, [info, keep, got], [(shape, keep.dtype)])[0]


def place_state(info, near, near_c, far, far_c):
    rows, width = near.shape

    def kernel(info_ref, near_ref, near_c_ref, far_ref, far_c_ref, out_ref):
        c, y = info_ref[0], info_ref[2]
        here = pl.ds(pl.multiple_of(c * rows, rows), rows)
        there = pl.ds(pl.multiple_of((1 - c) * rows, rows), rows)
        out_ref[y, here] = near_ref[...]
        out_ref[y, there] = near_c_ref[...]
        out_ref[1 - y, here] = far_ref[...]
        out_ref[1 - y, there] = far_c_ref[...]

    return rowwise(kernel, [info, near, near_c, far, far_c], [((2, 2 * rows, width), near.dtype)])[0]


SCALE = HEAD_DIM ** (-0.5)


def key_tiles(b, j):
    tiles = []
    if b > 0:
        tiles += [(b - 1, jj, "after" if jj == j else "all") for jj in range(j, 2)]
    tiles += [(b, jj, "until" if jj == j else "all") for jj in range(j + 1)]
    return tiles


def tile_mask(kind, size, limit):
    rows = lax.broadcasted_iota(jnp.int32, (size, size), 0)
    columns = lax.broadcasted_iota(jnp.int32, (size, size), 1)
    mask = None
    if kind == "after":
        mask = columns > rows
    if kind == "until":
        mask = columns <= rows
    if limit is not None:
        inside = columns < limit
        mask = inside if mask is None else mask & inside
    return mask


def masked_scores(queries, keys, masks):
    scores = mm_nt(queries, keys) * SCALE
    parts, place = [], 0
    for size, mask in masks:
        part = scores[:, place : place + size]
        parts.append(part if mask is None else jnp.where(mask, part, MASKED))
        place += size
    return jnp.concatenate(parts, axis=1)


def attention_plan(b, last, size, core, count, states):
    def start(block, j):
        return pl.multiple_of(block * 2 * size + jnp.bitwise_xor(core, j) * size, size)

    plan = []
    for j in range(2):
        tiles, masks = [], []
        for block, jj, kind in key_tiles(b, j):
            limit = count - jj * size if block == b and last else None
            tiles.append((block, jj))
            masks.append((size, tile_mask(kind, size, limit)))
        plan.append((tiles, masks + [(states, None)]))
    state_masks = [(states, None)]
    for jj in range(2):
        state_masks.append((size, tile_mask("all", size, count - jj * size if last else None)))
    return start, plan, state_masks


def attend_forward(b, blocks, info, tokens, states):
    lanes = tokens.shape[2] // 3
    heads = lanes // HEAD_DIM
    size = BLOCK // 2
    count_states = states.shape[1]

    def one(queries, keys, values, masks):
        scores = masked_scores(queries, keys, masks)
        top = jnp.max(scores, axis=1, keepdims=True)
        weights = jnp.exp(scores - top)
        total = jnp.sum(weights, axis=1, keepdims=True)
        mixed = mm(weights.astype(BF), values) / total
        return mixed.astype(BF), top + jnp.log(total)

    def kernel(info_ref, token_ref, state_ref, mixed_ref, state_mixed_ref, log_ref):
        start, plan, state_masks = attention_plan(
            b, b == blocks - 1, size, info_ref[0], info_ref[1], count_states
        )
        for h in range(heads):
            query, key, value = [slice(p * lanes + h * HEAD_DIM, p * lanes + (h + 1) * HEAD_DIM) for p in range(3)]
            own = slice(h * HEAD_DIM, (h + 1) * HEAD_DIM)

            def token_rows(places, columns):
                return [token_ref[0, pl.ds(start(*place), size), columns] for place in places]

            for j, (tiles, masks) in enumerate(plan):
                keys = jnp.concatenate(token_rows(tiles, key) + [state_ref[0, :, key]], axis=0)
                values = jnp.concatenate(token_rows(tiles, value) + [state_ref[0, :, value]], axis=0)
                mixed, log_total = one(token_ref[0, pl.ds(start(b, j), size), query], keys, values, masks)
                mixed_ref[0, pl.ds(start(0, j), size), own] = mixed
                log_ref[0, pl.ds(start(0, j), size), h : h + 1] = log_total
            tiles = [(b, 0), (b, 1)]
            keys = jnp.concatenate([state_ref[0, :, key]] + token_rows(tiles, key), axis=0)
            values = jnp.concatenate([state_ref[0, :, value]] + token_rows(tiles, value), axis=0)
            for begin in range(0, count_states, size):
                rows = slice(begin, begin + size)
                mixed, log_total = one(state_ref[0, rows, query], keys, values, state_masks)
                state_mixed_ref[0, rows, own] = mixed
                log_ref[0, rows, heads + h : heads + h + 1] = log_total

    rows = (b + 1) * BLOCK
    pairs = 2 * heads * (BLOCK * (BLOCK * (2 if b else 1) + count_states) + count_states * (count_states + BLOCK))
    spec = lambda n, w: pl.BlockSpec((1, n, w), lambda y: (y, 0, 0))
    return call(
        kernel,
        (2,),
        [info, tokens, states],
        [pl.BlockSpec(memory_space=pltpu.SMEM), spec(rows, 3 * lanes), spec(count_states, 3 * lanes)],
        [((2, BLOCK, lanes), BF), ((2, count_states, lanes), BF), ((2, BLOCK, 128), F32)],
        [spec(BLOCK, lanes), spec(count_states, lanes), spec(BLOCK, 128)],
        flops=4 * pairs * HEAD_DIM,
        exps=pairs,
    )


def attend_backward(b, blocks, info, tokens, states, logs, grad_mixed, grad_state_mixed, later):
    lanes = tokens.shape[2] // 3
    heads = lanes // HEAD_DIM
    size = BLOCK // 2
    count_states = states.shape[1]
    is_last = b == blocks - 1

    def one(queries, keys, values, masks, log_total, grad):
        scores = masked_scores(queries, keys, masks)
        probs = jnp.exp(scores - log_total)
        grad_probs = mm_nt(grad, values)
        row_sum = jnp.sum(grad_probs * probs, axis=1, keepdims=True)
        low = (probs * (grad_probs - row_sum)).astype(BF)
        return mm(low, keys) * SCALE, mm_tn(low, queries) * SCALE, mm_tn(probs.astype(BF), grad)

    def kernel(*args):
        info_ref, token_ref, state_ref, log_ref, grad_ref, state_grad_ref = args[:6]
        rest = list(args[6:])
        later_ref = None if is_last else rest.pop(0)
        out_ref, state_out_ref = rest.pop(0), rest.pop(0)
        before_ref = rest.pop(0) if b > 0 else None
        start, plan, state_masks = attention_plan(b, is_last, size, info_ref[0], info_ref[1], count_states)
        for h in range(heads):
            query, key, value = [slice(p * lanes + h * HEAD_DIM, p * lanes + (h + 1) * HEAD_DIM) for p in range(3)]
            own = slice(h * HEAD_DIM, (h + 1) * HEAD_DIM)

            def token_rows(places, columns):
                return [token_ref[0, pl.ds(start(*place), size), columns] for place in places]

            sums = {}

            def gather(places, grads):
                begin = 0
                for place in places:
                    rows = count_states if place == "state" else size
                    part = grads[begin : begin + rows]
                    begin += rows
                    yield place, part

            def collect(name, places, grads):
                for place, part in gather(places, grads):
                    full = (name, place)
                    sums[full] = part if full not in sums else sums[full] + part

            places = ["state", (b, 0), (b, 1)]
            keys = jnp.concatenate([state_ref[0, :, key]] + token_rows(places[1:], key), axis=0)
            values = jnp.concatenate([state_ref[0, :, value]] + token_rows(places[1:], value), axis=0)
            for begin in range(0, count_states, size):
                rows = slice(begin, begin + size)
                dq, dk, dv = one(
                    state_ref[0, rows, query],
                    keys,
                    values,
                    state_masks,
                    log_ref[0, rows, heads + h : heads + h + 1],
                    state_grad_ref[0, rows, own],
                )
                state_out_ref[0, rows, query] = dq.astype(BF)
                collect("k", places, dk)
                collect("v", places, dv)
            for j, (tiles, masks) in enumerate(plan):
                keys = jnp.concatenate(token_rows(tiles, key) + [state_ref[0, :, key]], axis=0)
                values = jnp.concatenate(token_rows(tiles, value) + [state_ref[0, :, value]], axis=0)
                here = pl.ds(start(0, j), size)
                dq, dk, dv = one(
                    token_ref[0, pl.ds(start(b, j), size), query],
                    keys,
                    values,
                    masks,
                    log_ref[0, here, h : h + 1],
                    grad_ref[0, here, own],
                )
                out_ref[0, here, query] = dq.astype(BF)
                collect("k", tiles + ["state"], dk)
                collect("v", tiles + ["state"], dv)
            state_out_ref[0, :, key] = sums[("k", "state")].astype(BF)
            state_out_ref[0, :, value] = sums[("v", "state")].astype(BF)
            for name, columns in (("k", key), ("v", value)):
                shift = slice(columns.start - lanes, columns.stop - lanes)
                for j in range(2):
                    here = pl.ds(start(0, j), size)
                    total = sums[(name, (b, j))]
                    if later_ref is not None:
                        total = total + later_ref[0, here, shift]
                    out_ref[0, here, columns] = total.astype(BF)
                    if before_ref is not None:
                        before_ref[0, here, shift] = sums[(name, (b - 1, j))]

    rows = (b + 1) * BLOCK
    pairs = 2 * heads * (BLOCK * (BLOCK * (2 if b else 1) + count_states) + count_states * (count_states + BLOCK))
    spec = lambda n, w: pl.BlockSpec((1, n, w), lambda y: (y, 0, 0))
    inputs = [info, tokens, states, logs, grad_mixed, grad_state_mixed]
    in_specs = [
        pl.BlockSpec(memory_space=pltpu.SMEM),
        spec(rows, 3 * lanes),
        spec(count_states, 3 * lanes),
        spec(BLOCK, 128),
        pl.BlockSpec((1, BLOCK, lanes), lambda y: (y, b, 0)),
        spec(count_states, lanes),
    ]
    outputs = [((2, BLOCK, 3 * lanes), BF), ((2, count_states, 3 * lanes), BF)]
    out_specs = [spec(BLOCK, 3 * lanes), spec(count_states, 3 * lanes)]
    if not is_last:
        inputs.append(later)
        in_specs.append(spec(BLOCK, 2 * lanes))
    if b > 0:
        outputs.append(((2, BLOCK, 2 * lanes), F32))
        out_specs.append(spec(BLOCK, 2 * lanes))
    out = call(
        kernel, (2,), inputs, in_specs, outputs, out_specs, flops=10 * pairs * HEAD_DIM, exps=pairs
    )
    return out if b > 0 else (out[0], out[1], None)


def body(
    tokens,
    counts,
    token_weights,
    token_output,
    state_weights,
    state_output,
    hidden_up,
    hidden_down,
    norm_gains,
    gate_bias,
    init_state,
    cotangent,
    state_cotangent,
):
    y, c = lax.axis_index("y"), lax.axis_index("c")
    width = tokens.shape[3]
    state_half = init_state.shape[0] // 2
    blocks = 4 * tokens.shape[2] // BLOCK
    valid_count = lax.dynamic_index_in_dim(counts[:, 0], y, 0, keepdims=False)
    if lax.axis_size("r") == 1:
        z, x = lax.axis_index("z"), lax.axis_index("x")
        places = width_places()
        back = [
            jnp.bitwise_xor(x, x_to) * RING + lax.rem(z - z_to + RING, RING) for z_to in range(RING) for x_to in range(2)
        ]
        before, after = (lambda array: array), (lambda array: array)
    else:
        places = back = list(range(PIECES))
        before, after = to_local, from_local
    info = jnp.stack([jnp.asarray(v, jnp.int32) for v in [c, valid_count, y] + places + back])

    def micro(array, index):
        return lax.dynamic_index_in_dim(array[:, 0], index, 0, keepdims=False)

    shard_rows = token_output.shape[0]
    flat = lambda array: array.reshape(shard_rows, -1)
    token_got = swap(micro(tokens, 1 - y), "y")
    small = jnp.concatenate(
        [
            lax.dynamic_slice_in_dim(init_state, c * state_half, state_half, 0),
            norm_gains,
            gate_bias[None],
            jnp.zeros((12, init_state.shape[1]), BF),
        ],
        axis=0,
    )
    small = gather_rows(small)
    w_token = gather_weight(flat(token_weights))
    w_mid = gather_weight(jnp.concatenate([flat(state_weights), state_output, token_output], axis=1))
    dy_got = swap(micro(cotangent, 1 - y), "y")
    w_up = gather_weight(hidden_up)
    w_down = gather_weight(hidden_down)
    head = token_output.shape[1]
    at_state, at_state_out, at_token_out = 0, 3 * head, 4 * head
    gains = [small[state_half + i : state_half + i + 1].astype(F32) for i in range(3)]
    gate_open = jax.nn.sigmoid(small[state_half + 3 : state_half + 4].astype(F32))
    state_now = small[:state_half].astype(F32)

    x_rows = own_rows(info, before(micro(tokens, y)), before(token_got))
    normed = pair(norm_rows(info, x_rows, gains[0]))
    state_norm = pair(norm_rows(info, state_now, gains[1]))
    dy_rows = own_rows(info, before(micro(cotangent, y)), before(dy_got))
    dy_pair = pair(dy_rows)
    grad_final = lax.dynamic_slice(
        state_cotangent, (y, 0, c * state_half, 0), (1, 1, state_half, width)
    )[0, 0]
    grad_final = local_rows(info, before(grad_final))

    token_proj = project(*normed, w_token, 0, 3 * head, 3 * head // 2, blocks=blocks)
    kept = []
    mixed = []
    for b in range(blocks):
        state_proj = project(*state_norm, w_mid, at_state, 3 * head, 3 * head)
        mixed_b, state_flat, logs = attend_forward(b, blocks, info, token_proj, state_proj)
        mixed.append(mixed_b)
        both = merge([state_flat], w_mid, at_state_out)
        if b < blocks - 1:
            state_next, next_norm, update = step_state(info, state_now, both, gate_open, gains[1])
        else:
            final_rows, update = last_state(info, state_now, both, gate_open)
            state_next, next_norm = None, None
        kept.append((state_now, state_norm, state_proj, logs, state_flat, update))
        state_now = state_next
        state_norm = None if next_norm is None else pair(next_norm)
    hidden, hidden_own = add_norm(info, x_rows, merge(mixed, w_mid, at_token_out, blocks=blocks), gains[2])
    hidden_norm = pair(hidden_own)
    ff = hidden_up.shape[1]
    activated, slope = project(*hidden_norm, w_up, 0, ff, ff // 2, activate=True)
    keep, send = add_out(info, hidden, merge([activated], w_down, 0))
    output = place_rows(info, after(keep), swap(after(send), "y"))[:, None]
    final_rows = after(final_rows)
    final_far = swap(final_rows, "y")
    final_state = place_state(info, final_rows, swap(final_rows, "c"), final_far, swap(final_far, "c"))[:, None]

    grad_up = project(*dy_pair, w_down, 0, ff, ff // 2, gate=slope)
    grad_hidden_down = reduce_weight(outer([dy_pair], [activated], ff // 2))
    both = merge([grad_up], w_up, 0)
    grad_hidden_up = reduce_weight(outer([hidden_norm], [grad_up], ff // 2))
    grad_hidden, branch, gain_hidden = back_hidden(info, hidden, both, gains[2], dy_rows)
    branch = pair(branch)
    grad_mixed = project(*branch, w_mid, at_token_out, head, head, blocks=blocks)
    grad_token_output = reduce_weight(
        outer([branch], [jnp.concatenate(mixed, axis=1)], head, blocks=blocks)
    )

    grad_state = grad_final
    grad_update = pair(back_update(info, grad_final, gate_open))
    gate_sums, gain_sums = [], []
    proj_grads = [None] * blocks
    update_all, flat_all, norm_all, state_grads = [], [], [], []
    later = None
    for b in reversed(range(blocks)):
        state_before, state_norm, state_proj, logs, state_flat, update = kept[b]
        grad_state_mixed = project(*grad_update, w_mid, at_state_out, head, head)
        proj_grads[b], state_grad, later = attend_backward(
            b, blocks, info, token_proj, state_proj, logs, grad_mixed, grad_state_mixed, later
        )
        update_all.append(grad_update)
        flat_all.append(state_flat)
        norm_all.append(state_norm)
        state_grads.append(state_grad)
        both = merge([state_grad], w_mid, at_state)
        grad_state, low, gain_sum, gate_sum = back_state(
            info, grad_state, state_before, update, both, gate_open, gains[1]
        )
        grad_update = pair(low) if b > 0 else None
        gain_sums.append(gain_sum)
        gate_sums.append(gate_sum)
    both = merge(proj_grads, w_token, 0, blocks=blocks)
    grad_token_weights = reduce_weight(
        outer([normed], [jnp.concatenate(proj_grads, axis=1)], 3 * head, blocks=blocks)
    ).reshape(-1, 3, head)
    keep, send, gain_token = back_input(info, x_rows, both, gains[0], grad_hidden)
    input_grad = place_rows(info, after(keep), swap(after(send), "y"))[:, None]
    grad_state_weights = reduce_weight(outer(norm_all, state_grads, 3 * head)).reshape(-1, 3, head)
    grad_state_output = reduce_weight(outer(update_all, flat_all, head))

    vectors = jnp.concatenate(
        [gain_token, sum(gain_sums), gain_hidden, sum(gate_sums), jnp.zeros((12, width), F32)], axis=0
    )
    rows = jnp.concatenate([grad_state, vectors], axis=0).astype(BF)
    half = width // 2
    total = (rows[:, :half].astype(F32) + swap(rows[:, half:], "x").astype(F32)).astype(BF)
    size = half // RING
    near = total[:, :size].astype(F32)
    for k in range(1, RING):
        near = near + turn(total[:, k * size : (k + 1) * size], RING - k).astype(F32)
    if lax.axis_size("r") > 1:
        near = lax.psum_scatter(near, "r", scatter_dimension=1, tiled=True)
    near = near + swap(near, "y")
    far = swap(near, "c")
    states, others = near[:state_half], far[:state_half]
    init_grad = jnp.where(c == 0, jnp.concatenate([states, others]), jnp.concatenate([others, states]))
    vectors = near[state_half:] + far[state_half:]
    return (
        output,
        final_state,
        input_grad,
        grad_token_weights,
        grad_token_output,
        grad_state_weights,
        grad_state_output,
        grad_hidden_up,
        grad_hidden_down,
        vectors[:3],
        vectors[3],
        init_grad,
    )


def solution(mesh):
    dp, heads = mesh.devices.shape
    fine = Mesh(mesh.devices.reshape(dp // (2 * RING), RING, 2, heads // 2, 2), ("r", "z", "x", "y", "c"))
    d, h = ("r", "z", "x"), ("y", "c")
    return jax.shard_map(
        body,
        mesh=fine,
        in_specs=(
            P(None, d, h, None),
            P(None, d),
            P(d, None, h),
            P(d, h),
            P(d, None, h),
            P(d, h),
            P(d, h),
            P(d, h),
            P(None, d),
            P(d),
            P(None, d),
            P(None, d, h, None),
            P(None, d, None, None),
        ),
        out_specs=(
            P(None, d, h, None),
            P(None, d, None, None),
            P(None, d, h, None),
            P(d, None, h),
            P(d, h),
            P(d, None, h),
            P(d, h),
            P(d, h),
            P(d, h),
            P(None, d),
            P(d),
            P(None, d),
        ),
        check_vma=False,
    )
```

```python
import functools

import jax
import jax.numpy as jnp
from jax import lax
from jax.experimental import pallas as pl
from jax.experimental.pallas import tpu as pltpu
from jax.sharding import Mesh
from jax.sharding import PartitionSpec as P

HEAD_DIM = 128
BLOCK = 512
EPSILON = 1e-06
MASKED = -1e30
COST = 1
GELU = 0.7978845608028654
RING = 4
BF = jnp.bfloat16
F32 = jnp.float32


def swap(array, axis):
    return lax.ppermute(array, axis, [(0, 1), (1, 0)])


def swap_z(array, bit):
    return lax.ppermute(array, "z", [(i, i ^ bit) for i in range(RING)])


def matmul(left, right, contract):
    return lax.dot_general(
        left, right, (contract, ((), ())), preferred_element_type=jnp.float32
    )


def mm(left, right):
    return matmul(left, right, ((1,), (0,)))


def mm_nt(left, right):
    return matmul(left, right, ((1,), (1,)))


def mm_tn(left, right):
    return matmul(left, right, ((0,), (0,)))


RING_BITS = (0, 2, 1, 3)


def width_places():
    z, x = lax.axis_index("z"), lax.axis_index("x")
    return [jnp.bitwise_xor(z, RING_BITS[k]) * 2 + jnp.bitwise_xor(x, dx) for dx in range(2) for k in range(RING)]


def width_places_back():
    z, x = lax.axis_index("z"), lax.axis_index("x")
    places = []
    for z_to in range(RING):
        apart = jnp.bitwise_xor(z, z_to)
        k = lax.rem(apart, 2) * 2 + lax.div(apart, 2)
        places += [jnp.bitwise_xor(x, x_to) * RING + k for x_to in range(2)]
    return places


def take_pieces(array, places):
    groups = lax.axis_size("r")
    lead, width = array.shape[:-1], array.shape[-1]
    split = array.reshape(lead + (groups, len(places), width // (groups * len(places))))
    axis = len(lead) + 1
    return [lax.dynamic_index_in_dim(split, place, axis, keepdims=False) for place in places]


def to_local(array):
    pieces = take_pieces(array, width_places())
    lead = array.shape[:-1]
    return jnp.concatenate([p.reshape(lead + (-1,)) for p in pieces], axis=-1)


def from_local(array):
    groups = lax.axis_size("r")
    lead, width = array.shape[:-1], array.shape[-1]
    split = array.reshape(lead + (2 * RING, groups, width // (groups * 2 * RING)))
    axis = len(lead)
    pieces = [lax.dynamic_index_in_dim(split, place, axis, keepdims=False) for place in width_places_back()]
    return jnp.stack(pieces, axis=axis + 1).reshape(array.shape)


def gather_groups(array, axis):
    if lax.axis_size("r") == 1:
        return array
    return lax.all_gather(array, "r", axis=axis, tiled=True)


def scatter_groups(array, axis):
    if lax.axis_size("r") == 1:
        return array
    return lax.psum_scatter(array, "r", scatter_dimension=axis, tiled=True)


class Order:
    def __init__(self):
        self.last = []


ORDER = Order()


def call(kernel, grid, inputs, in_specs, outputs, out_specs, flops=0, exps=0, deps=(), vmem=16, **more):
    block_bytes = sum(a.size * a.dtype.itemsize for a in inputs)
    shapes = [jax.ShapeDtypeStruct(shape, dtype) for shape, dtype in outputs]
    out_bytes = sum(s.size * s.dtype.itemsize for s in shapes)
    given = len(inputs)
    deps = [array for array in list(deps) + ORDER.last if all(array is not other for other in inputs)]

    def run(*refs):
        kernel(*refs[:given], *refs[given + len(deps) :])

    out = pl.pallas_call(
        run,
        grid=grid,
        in_specs=list(in_specs) + [pl.BlockSpec(memory_space=pl.ANY)] * len(deps),
        out_specs=out_specs,
        out_shape=shapes,
        compiler_params=pltpu.CompilerParams(vmem_limit_bytes=vmem * 2**20),
        cost_estimate=pl.CostEstimate(
            flops=int(flops * COST), bytes_accessed=int((block_bytes + out_bytes) * COST), transcendentals=int(exps * COST)
        ),
        **more,
    )(*inputs, *deps)
    ORDER.last = [min(out, key=lambda array: array.size)]
    return out


def whole(array):
    return pl.BlockSpec(array.shape, lambda *_: (0,) * array.ndim)


def whole_out(shape):
    return pl.BlockSpec(shape, lambda *_: (0,) * len(shape))


def stack_rows(first, second, deps=()):
    rows, width = first.shape

    def kernel(first_ref, second_ref, out_ref):
        out_ref[:rows] = first_ref[...]
        out_ref[rows:] = second_ref[...]

    return call(
        kernel,
        (1,),
        [first, second],
        [whole(first)] * 2,
        [((2 * rows, width), BF)],
        [whole_out((2 * rows, width))],
        deps=deps,
    )[0]


def join_columns(arrays, deps):
    rows = arrays[0].shape[0]
    width = sum(array.shape[1] for array in arrays)

    def kernel(*refs):
        place = 0
        for ref in refs[:-1]:
            refs[-1][:, place : place + ref.shape[1]] = ref[...]
            place += ref.shape[1]

    return call(
        kernel,
        (1,),
        arrays,
        [whole(array) for array in arrays],
        [((rows, width), BF)],
        [whole_out((rows, width))],
        deps=deps,
    )[0]


class Gather:
    def __init__(self, shard):
        self.shard = gather_groups(shard, 0)
        self.got = swap_z(self.shard, 2)

    def spread(self, deps=(), by_x=False):
        low = stack_rows(self.shard, self.got, deps)
        low_x, low_y = swap(low, "x"), swap(low, "y")
        high = swap_z(low, 1)
        high_y, high_x = swap(high, "y"), swap(high, "x")
        low_xy = swap(low_y, "x") if by_x else swap(low_x, "y")
        high_xy = swap(high_y, "x")
        self.pieces = [[[low, high], [low_x, high_x]], [[low_y, high_y], [low_xy, high_xy]]]
        self.ring, self.low, self.high, self.far = [high], [low_x, low_y], [high_x, high_y], [low_xy, high_xy]
        return self.pieces


def flat_pieces(pieces):
    return [pieces[y][x][half] for y in range(2) for x in range(2) for half in range(2)]


def spread_rows(info, near, far):
    size = near.shape[1]
    rows = near.shape[0] // RING

    def kernel(near_ref, far_ref, out_ref):
        for k in range(RING):
            out_ref[:, k * size : (k + 1) * size] = near_ref[k * rows : (k + 1) * rows]
            out_ref[:, (RING + k) * size : (RING + k + 1) * size] = far_ref[k * rows : (k + 1) * rows]

    return call(
        kernel,
        (1,),
        [near, far],
        [whole(near), whole(far)],
        [((rows, 2 * RING * size), near.dtype)],
        [whole_out((rows, 2 * RING * size))],
    )[0]


def row_order(own, other, blocks):
    per = own.shape[0] // blocks
    parts = []
    for b in range(blocks):
        parts += [own[b * per : (b + 1) * per], other[b * per : (b + 1) * per]]
    return jnp.concatenate(parts, axis=0)


def project(own, other, pieces, column, width, block, blocks=1, gate=None, activate=False, deps=()):
    rows = own.shape[0] * 2
    refs = flat_pieces(pieces)
    first = column // block

    def kernel(*args):
        own_ref, other_ref, weights = args[0], args[1], args[2:10]
        left = row_order(own_ref[...], other_ref[...], blocks)
        for y in range(2):
            weight = jnp.concatenate([ref[...] for ref in weights[4 * y : 4 * y + 4]], axis=0)
            total = mm(left, weight)
            if gate is not None:
                gate_ref, out_ref = args[10], args[11]
                low = total.astype(BF).astype(F32)
                out_ref[y] = (low * gate_ref[y].astype(F32)).astype(BF)
            elif activate:
                act_ref, slope_ref = args[10], args[11]
                square = total * total
                curve = jnp.tanh(total * (GELU * 0.044715 * square + GELU))
                share = 0.5 * curve + 0.5
                act = total * share
                act_ref[y] = act.astype(BF)
                slope = share + act * (1.0 - curve) * (GELU * 0.134145 * square + GELU)
                slope_ref[y] = slope.astype(BF)
            else:
                args[10][y] = total.astype(BF)

    spec = pl.BlockSpec((2, rows, block), lambda j: (0, 0, j))
    weight_spec = [pl.BlockSpec((ref.shape[0], block), lambda j: (0, first + j)) for ref in refs]
    extra = [] if gate is None else [gate]
    count = 2 if activate else 1
    out = call(
        kernel,
        (width // block,),
        [own, other] + refs + extra,
        [whole(own), whole(other)] + weight_spec + [spec] * len(extra),
        [((2, rows, width), BF)] * count,
        [spec] * count,
        flops=4 * rows * own.shape[1] * width,
        deps=deps,
    )
    return out if activate else out[0]


def merge(lefts, pieces, column, blocks=1, deps=()):
    refs = flat_pieces(pieces)
    columns = sum(part.shape[2] for part in lefts[0])
    per = lefts[0][0].shape[1] // 2
    rows = per * len(lefts)
    width = 8 * refs[0].shape[0] // 2
    first = column // columns
    parts_count = len(lefts[0])
    flat = [part for left in lefts for part in left]

    def kernel(*args):
        left_refs, weights = args[: len(flat)], args[len(flat) : len(flat) + 8]
        own_ref, other_ref = args[len(flat) + 8 :]
        sides = [
            jnp.concatenate([ref[...] for ref in weights[4 * y : 4 * y + 4]], axis=0) for y in range(2)
        ]
        for core, out_ref in ((1, other_ref), (0, own_ref)):
            total = None
            for y in range(2):
                left = []
                for b in range(len(lefts)):
                    here = left_refs[b * parts_count : (b + 1) * parts_count]
                    left.append(jnp.concatenate([ref[y, core * per : (core + 1) * per] for ref in here], axis=1))
                piece = mm_nt(jnp.concatenate(left, axis=0), sides[y])
                total = piece if total is None else total + piece
            out_ref[...] = total.astype(out_ref.dtype)

    weight_spec = [pl.BlockSpec((ref.shape[0], columns), lambda i: (0, first)) for ref in refs]
    return call(
        kernel,
        (1,),
        flat + refs,
        [whole(left) for left in flat] + weight_spec,
        [((rows, width), F32), ((rows, width), BF)],
        [whole_out((rows, width))] * 2,
        flops=8 * rows * width * columns,
        deps=deps,
    )


def outer(segments, block=None, vmem=16, deps=(), into=None, share=1):
    width = segments[0][0][0][0].shape[1]
    sizes = [rights[0].shape[2] for lefts, rights, blocks in segments]
    columns = sum(sizes)
    block = columns if block is None else block
    half = width // 2
    inputs, in_specs, flops = [], [], 0
    for lefts, rights, blocks in segments:
        flat = [array for pair_ in lefts for array in pair_]
        inputs += flat + list(rights)
        in_specs += [whole(array) for array in flat]
        wide = min(block, rights[0].shape[2])
        in_specs += [pl.BlockSpec((2, right.shape[1], wide), lambda j: (0, 0, j)) for right in rights]
        flops += 4 * width * rights[0].shape[2] * sum(right.shape[1] for right in rights)

    def kernel(*args):
        low11, high11, out10, out01, out00 = args[-5:]
        place, column = 0, 0
        for lefts, rights, blocks in segments:
            left_refs = args[place : place + 2 * len(lefts)]
            right_refs = args[place + 2 * len(lefts) : place + 2 * len(lefts) + len(rights)]
            place += 2 * len(lefts) + len(rights)
            left = jnp.concatenate(
                [row_order(left_refs[2 * i][...], left_refs[2 * i + 1][...], blocks) for i in range(len(lefts))], axis=0
            )
            here = slice(column, column + right_refs[0].shape[2])
            column += right_refs[0].shape[2]
            for y in (1, 0):
                right = jnp.concatenate([ref[y] for ref in right_refs], axis=0)
                for x in (1, 0):
                    total = mm_tn(left[:, x * half : (x + 1) * half], right).astype(BF)
                    if x and y:
                        low11[:, here] = total[: half // 2]
                        high11[:, here] = total[half // 2 :]
                    else:
                        {(1, 0): out10, (0, 1): out01, (0, 0): out00}[(x, y)][:, here] = total

    first = 0 if into is None else columns // block
    aliases = {}
    if into is not None:
        aliases = {len(inputs) + i: i for i in range(5)}
        inputs += list(into)
        in_specs += [pl.BlockSpec(memory_space=pl.ANY)] * 5
    return call(
        kernel,
        (columns // block,),
        inputs,
        in_specs,
        [((half // 2, share * columns), BF)] * 2 + [((half, share * columns), BF)] * 3,
        [pl.BlockSpec((half // 2, block), lambda j: (0, first + j))] * 2
        + [pl.BlockSpec((half, block), lambda j: (0, first + j))] * 3,
        flops=flops,
        vmem=vmem,
        deps=deps,
        input_output_aliases=aliases,
    )


def add_into(array, piece, half, deps=()):
    rows, columns = piece.shape

    def kernel(array_ref, piece_ref, out_ref):
        out_ref[...] = (array_ref[...].astype(F32) + piece_ref[...].astype(F32)).astype(BF)

    return call(
        kernel,
        (1,),
        [array, piece],
        [pl.BlockSpec((rows, columns), lambda i: (half, 0)), pl.BlockSpec((rows, columns), lambda i: (0, 0))],
        [(array.shape, BF)],
        [pl.BlockSpec((rows, columns), lambda i: (half, 0))],
        input_output_aliases={0: 0},
        deps=deps,
        vmem=28,
    )[0]


def add_split(arrays, deps=()):
    rows, columns = arrays[0].shape
    part = rows // 2

    def kernel(*refs):
        for half, out_ref in enumerate(refs[len(arrays) :]):
            piece = slice(half * part, (half + 1) * part)
            total = refs[0][piece].astype(F32)
            for ref in refs[1 : len(arrays)]:
                total = total + ref[piece].astype(F32)
            out_ref[...] = total.astype(out_ref.dtype)

    return call(
        kernel,
        (1,),
        arrays,
        [whole(array) for array in arrays],
        [((part, columns), F32), ((part, columns), BF)],
        [whole_out((part, columns))] * 2,
        deps=deps,
        vmem=28,
    )


class Reduce:
    def __init__(self, quarters, by_x=False):
        low11, high11, self.out10, self.out01, self.out00 = quarters
        self.by_x = by_x
        self.low_got, self.high_got = swap(low11, "x" if by_x else "y"), swap(high11, "x")
        self.first = [self.low_got, self.high_got]

    def second(self, deps=()):
        if self.by_x:
            self.out01 = add_into(self.out01, self.low_got, 0, deps)
        else:
            self.out10 = add_into(self.out10, self.low_got, 0, deps)
        self.x_got = swap(self.out10, "x")
        self.y_got = swap(add_into(self.out01, self.high_got, 1, deps), "y")
        self.next = [self.x_got, self.y_got]

    def third(self, deps=()):
        self.near, far = add_split([self.out00, self.x_got, self.y_got], deps)
        self.got = swap_z(far, 1)

    def fourth(self, deps=()):
        self.near, far = add_split([self.near, self.got], deps)
        self.got = swap_z(far, 2)

    def total(self):
        return scatter_groups(self.near + self.got.astype(F32), 0)


def pair(own):
    return own, swap(own, "c")


INFO = 3
PIECES = 2 * RING
SMALL = 16


def smem():
    return pl.BlockSpec(memory_space=pltpu.SMEM)


def lanes_at(info_ref, index, width):
    size = width // PIECES
    return pl.ds(pl.multiple_of(info_ref[index] * size, size), size)


def reorder_in(info_ref, source, target, rows=slice(None)):
    width = source.shape[-1]
    size = width // PIECES
    for k in range(PIECES):
        target[rows, k * size : (k + 1) * size] = source[:, lanes_at(info_ref, INFO + k, width)].astype(target.dtype)


def reorder_out(info_ref, source, target, rows=slice(None)):
    width = source.shape[-1]
    size = width // PIECES
    for k in range(PIECES):
        part = source[rows, lanes_at(info_ref, INFO + PIECES + k, width)]
        target[:, k * size : (k + 1) * size] = part.astype(target.dtype)


def inverse_rms(values):
    return lax.rsqrt(jnp.mean(values * values, axis=-1, keepdims=True) + EPSILON)


def rms_back(values, gain, grad):
    inverse = inverse_rms(values)
    scaled = values * inverse
    weighted = grad * gain
    back = inverse * (weighted - scaled * jnp.mean(scaled * weighted, axis=-1, keepdims=True))
    return back, jnp.sum(grad * scaled, axis=0, keepdims=True)


def rowwise(kernel, inputs, outputs, scratch=(), deps=()):
    return call(
        kernel,
        (1,),
        inputs,
        [smem()] + [whole(array) for array in inputs[1:]],
        outputs,
        [whole_out(shape) for shape, _ in outputs],
        scratch_shapes=[pltpu.VMEM(shape, dtype) for shape, dtype in scratch],
        deps=deps,
    )


def own_rows(info, keep, got):
    rows, width = keep.shape

    def kernel(info_ref, keep_ref, got_ref, out_ref):
        y = info_ref[2]
        reorder_in(info_ref, keep_ref, out_ref, pl.ds(pl.multiple_of(y * rows, rows), rows))
        reorder_in(info_ref, got_ref, out_ref, pl.ds(pl.multiple_of((1 - y) * rows, rows), rows))

    return rowwise(kernel, [info, keep, got], [((2 * rows, width), BF)])[0]


def local_rows(info, array):
    def kernel(info_ref, in_ref, out_ref):
        reorder_in(info_ref, in_ref, out_ref)

    return rowwise(kernel, [info, array], [(array.shape, array.dtype)])[0]


def norm_rows(info, values, gain, deps=()):
    def kernel(info_ref, in_ref, gain_ref, out_ref):
        rows = in_ref[...].astype(F32)
        out_ref[...] = (rows * inverse_rms(rows) * gain_ref[...]).astype(BF)

    return rowwise(kernel, [info, values, gain], [(values.shape, BF)], deps=deps)[0]


def add_norm(info, rows, both, gain):
    own, other = both

    def kernel(info_ref, row_ref, own_ref, got_ref, gain_ref, hidden_ref, norm_ref):
        hidden = row_ref[...].astype(F32) + (own_ref[...] + got_ref[...].astype(F32))
        hidden_ref[...] = hidden
        norm_ref[...] = (hidden * inverse_rms(hidden) * gain_ref[...]).astype(BF)

    return rowwise(kernel, [info, rows, own, swap(other, "c"), gain], [(rows.shape, F32), (rows.shape, BF)])


def add_out(info, hidden, both):
    own, other = both
    rows, width = hidden.shape
    half = rows // 2

    def kernel(info_ref, hidden_ref, own_ref, got_ref, keep_ref, send_ref, scratch):
        y = info_ref[2]
        scratch[...] = hidden_ref[...] + (own_ref[...] + got_ref[...].astype(F32))
        reorder_out(info_ref, scratch, keep_ref, pl.ds(pl.multiple_of(y * half, half), half))
        reorder_out(info_ref, scratch, send_ref, pl.ds(pl.multiple_of((1 - y) * half, half), half))

    return rowwise(
        kernel,
        [info, hidden, own, swap(other, "c")],
        [((half, width), BF)] * 2,
        [((rows, width), F32)],
    )


def step_state(info, state, both, gate, gain):
    own, other = both

    def kernel(info_ref, state_ref, own_ref, got_ref, gate_ref, gain_ref, next_ref, norm_ref, update_ref):
        update = own_ref[...] + got_ref[...].astype(F32)
        update_ref[...] = update
        after = gate_ref[...] * state_ref[...] + (1.0 - gate_ref[...]) * update
        next_ref[...] = after
        norm_ref[...] = (after * inverse_rms(after) * gain_ref[...]).astype(BF)

    return rowwise(
        kernel,
        [info, state, own, swap(other, "c"), gate, gain],
        [(state.shape, F32), (state.shape, BF), (state.shape, F32)],
    )


def last_state(info, state, both, gate):
    own, other = both

    def kernel(info_ref, state_ref, own_ref, got_ref, gate_ref, final_ref, update_ref, scratch):
        update = own_ref[...] + got_ref[...].astype(F32)
        update_ref[...] = update
        scratch[...] = gate_ref[...] * state_ref[...] + (1.0 - gate_ref[...]) * update
        reorder_out(info_ref, scratch, final_ref)

    return rowwise(
        kernel,
        [info, state, own, swap(other, "c"), gate],
        [(state.shape, BF), (state.shape, F32)],
        [(state.shape, F32)],
    )


def back_hidden(info, hidden, both, gain, dy):
    own, other = both

    def kernel(info_ref, hidden_ref, own_ref, got_ref, gain_ref, dy_ref, grad_ref, branch_ref, gain_grad_ref):
        grad = own_ref[...] + got_ref[...].astype(F32)
        back, gain_grad_ref[...] = rms_back(hidden_ref[...], gain_ref[...], grad)
        total = dy_ref[...].astype(F32) + back
        grad_ref[...] = total
        branch_ref[...] = total.astype(BF)

    return rowwise(
        kernel,
        [info, hidden, own, swap(other, "c"), gain, dy],
        [(hidden.shape, F32), (hidden.shape, BF), ((1, hidden.shape[1]), F32)],
    )


def back_update(info, grad, gate):
    def kernel(info_ref, grad_ref, gate_ref, out_ref):
        out_ref[...] = ((1.0 - gate_ref[...]) * grad_ref[...].astype(F32)).astype(BF)

    return rowwise(kernel, [info, grad, gate], [(grad.shape, BF)])[0]


def back_state(info, grad, state, update, both, gate, gain):
    own, other = both
    width = state.shape[1]

    def kernel(
        info_ref, grad_ref, state_ref, update_ref, own_ref, got_ref, gate_ref, gain_ref, out_ref, low_ref, gain_grad_ref, gate_grad_ref
    ):
        gate_open = gate_ref[...]
        grad_now = grad_ref[...].astype(F32)
        values = state_ref[...]
        gate_grad_ref[...] = jnp.sum(grad_now * (values - update_ref[...]), axis=0, keepdims=True) * (
            gate_open * (1.0 - gate_open)
        )
        back, gain_grad_ref[...] = rms_back(values, gain_ref[...], own_ref[...] + got_ref[...].astype(F32))
        total = gate_open * grad_now + back
        out_ref[...] = total
        low_ref[...] = ((1.0 - gate_open) * total).astype(BF)

    return rowwise(
        kernel,
        [info, grad, state, update, own, swap(other, "c"), gate, gain],
        [(state.shape, F32), (state.shape, BF), ((1, width), F32), ((1, width), F32)],
    )


def back_input(info, values, both, gain, grad_hidden):
    own, other = both
    rows, width = values.shape
    half = rows // 2

    def kernel(info_ref, value_ref, own_ref, got_ref, gain_ref, grad_ref, keep_ref, send_ref, gain_grad_ref, scratch):
        y = info_ref[2]
        grad = own_ref[...] + got_ref[...].astype(F32)
        back, gain_grad_ref[...] = rms_back(value_ref[...].astype(F32), gain_ref[...], grad)
        scratch[...] = grad_ref[...] + back
        reorder_out(info_ref, scratch, keep_ref, pl.ds(pl.multiple_of(y * half, half), half))
        reorder_out(info_ref, scratch, send_ref, pl.ds(pl.multiple_of((1 - y) * half, half), half))

    return rowwise(
        kernel,
        [info, values, own, swap(other, "c"), gain, grad_hidden],
        [((half, width), F32), ((half, width), BF), ((1, width), F32)],
        [((rows, width), F32)],
    )


def pack_small(info, states, vectors):
    rows, width = states.shape
    half = width // 2
    counts = [len(group) for group in vectors]
    flat = [vector for group in vectors for vector in group]
    pad = SMALL - len(vectors)

    def kernel(info_ref, state_ref, *refs):
        near_ref, far_ref = refs[len(flat) :]
        parts, place = [], 0
        for count in counts:
            parts.append(sum(ref[...] for ref in refs[place : place + count]))
            place += count
        tail = jnp.concatenate(parts + [jnp.zeros((pad, width), F32)], axis=0)
        near_ref[:rows] = state_ref[:, :half]
        near_ref[rows:] = tail[:, :half]
        far_ref[:rows] = state_ref[:, half:].astype(BF)
        far_ref[rows:] = tail[:, half:].astype(BF)

    shape = (rows + SMALL, half)
    return rowwise(kernel, [info, states] + flat, [(shape, F32), (shape, BF)])


def add_small(info, near, got):
    rows, width = near.shape
    half = width // 2

    def kernel(info_ref, near_ref, got_ref, near_out, far_out):
        total = near_ref[...] + got_ref[...].astype(F32)
        near_out[...] = total[:, :half]
        far_out[...] = total[:, half:].astype(BF)

    return rowwise(kernel, [info, near, got], [((rows, half), F32), ((rows, half), BF)])


def add_pair(info, near, got):
    def kernel(info_ref, near_ref, got_ref, out_ref):
        out_ref[...] = near_ref[...] + got_ref[...].astype(F32)

    return rowwise(kernel, [info, near, got], [(near.shape, F32)])[0]


def place_small(info, near, far, states):
    size = near.shape[1]

    def kernel(info_ref, near_ref, far_ref, state_ref, gain_ref, gate_ref):
        c = info_ref[0]
        state_ref[pl.ds(pl.multiple_of(c * states, states), states)] = near_ref[:states]
        state_ref[pl.ds(pl.multiple_of((1 - c) * states, states), states)] = far_ref[:states]
        total = near_ref[states:] + far_ref[states:]
        gain_ref[...] = total[:3]
        gate_ref[...] = total[3:4]

    return rowwise(kernel, [info, near, far], [((2 * states, size), F32), ((3, size), F32), ((1, size), F32)])


def place_rows(info, keep, got):
    shape = (2,) + keep.shape

    def kernel(info_ref, keep_ref, got_ref, out_ref):
        y = info_ref[2]
        out_ref[y] = keep_ref[...]
        out_ref[1 - y] = got_ref[...].astype(keep.dtype)

    return rowwise(kernel, [info, keep, got], [(shape, keep.dtype)])[0]


def place_state(info, near, near_c, far, far_c):
    rows, width = near.shape

    def kernel(info_ref, near_ref, near_c_ref, far_ref, far_c_ref, out_ref):
        c, y = info_ref[0], info_ref[2]
        here = pl.ds(pl.multiple_of(c * rows, rows), rows)
        there = pl.ds(pl.multiple_of((1 - c) * rows, rows), rows)
        out_ref[y, here] = near_ref[...]
        out_ref[y, there] = near_c_ref[...]
        out_ref[1 - y, here] = far_ref[...]
        out_ref[1 - y, there] = far_c_ref[...]

    return rowwise(kernel, [info, near, near_c, far, far_c], [((2, 2 * rows, width), near.dtype)])[0]


SCALE = HEAD_DIM ** (-0.5)


def key_tiles(b, j):
    tiles = []
    if b > 0:
        tiles += [(b - 1, jj, "after" if jj == j else "all") for jj in range(j, 2)]
    tiles += [(b, jj, "until" if jj == j else "all") for jj in range(j + 1)]
    return tiles


def tile_mask(kind, size, limit):
    rows = lax.broadcasted_iota(jnp.int32, (size, size), 0)
    columns = lax.broadcasted_iota(jnp.int32, (size, size), 1)
    mask = None
    if kind == "after":
        mask = columns > rows
    if kind == "until":
        mask = columns <= rows
    if limit is not None:
        inside = columns < limit
        mask = inside if mask is None else mask & inside
    return mask


def masked_scores(queries, keys, masks):
    scores = mm_nt(queries, keys) * SCALE
    parts, place = [], 0
    for size, mask in masks:
        part = scores[:, place : place + size]
        parts.append(part if mask is None else jnp.where(mask, part, MASKED))
        place += size
    return jnp.concatenate(parts, axis=1)


def attention_plan(b, last, size, core, count, states):
    def start(block, j):
        return pl.multiple_of(block * 2 * size + jnp.bitwise_xor(core, j) * size, size)

    plan = []
    for j in range(2):
        tiles, masks = [], []
        for block, jj, kind in key_tiles(b, j):
            limit = count - jj * size if block == b and last else None
            tiles.append((block, jj))
            masks.append((size, tile_mask(kind, size, limit)))
        plan.append((tiles, masks + [(states, None)]))
    state_masks = [(states, None)]
    for jj in range(2):
        state_masks.append((size, tile_mask("all", size, count - jj * size if last else None)))
    return start, plan, state_masks


def block_spec(rows, width):
    return pl.BlockSpec((1, rows, width), lambda y: (y, 0, 0))


def head_slices(lanes, h):
    return [slice(p * lanes + h * HEAD_DIM, p * lanes + (h + 1) * HEAD_DIM) for p in range(3)]


def attend_rows(queries, keys, values, masks):
    scores = masked_scores(queries, keys, masks)
    top = jnp.max(scores, axis=1, keepdims=True)
    weights = jnp.exp(scores - top)
    total = jnp.sum(weights, axis=1, keepdims=True)
    mixed = mm(weights.astype(BF), values) / total
    return mixed.astype(BF), top + jnp.log(total)


def attend_rows_back(queries, keys, values, masks, log_total, grad):
    scores = masked_scores(queries, keys, masks)
    probs = jnp.exp(scores - log_total)
    grad_probs = mm_nt(grad, values)
    row_sum = jnp.sum(grad_probs * probs, axis=1, keepdims=True)
    low = (probs * (grad_probs - row_sum)).astype(BF)
    return mm(low, keys) * SCALE, mm_tn(low, queries) * SCALE, mm_tn(probs.astype(BF), grad)


def token_pairs(b, heads, states):
    return 2 * heads * BLOCK * (BLOCK * (1.25 if b else 0.75) + states)


def forward_tokens(b, blocks, info, tokens, states, deps=()):
    lanes = tokens.shape[2] // 3
    heads = lanes // HEAD_DIM
    size = BLOCK // 2
    count_states = states.shape[1]

    def kernel(info_ref, token_ref, state_ref, mixed_ref, log_ref):
        start, plan, state_masks = attention_plan(
            b, b == blocks - 1, size, info_ref[0], info_ref[1], count_states
        )
        for h in range(heads):
            query, key, value = head_slices(lanes, h)
            for j, (tiles, masks) in enumerate(plan):
                rows = [pl.ds(start(*place), size) for place in tiles]
                keys = jnp.concatenate([token_ref[0, at, key] for at in rows] + [state_ref[0, :, key]], axis=0)
                values = jnp.concatenate([token_ref[0, at, value] for at in rows] + [state_ref[0, :, value]], axis=0)
                here = pl.ds(start(0, j), size)
                mixed_ref[0, here, query], log_ref[0, here, h : h + 1] = attend_rows(
                    token_ref[0, pl.ds(start(b, j), size), query], keys, values, masks
                )

    pairs = int(token_pairs(b, heads, count_states))
    return call(
        kernel,
        (2,),
        [info, tokens, states],
        [smem(), block_spec((b + 1) * BLOCK, 3 * lanes), block_spec(count_states, 3 * lanes)],
        [((2, BLOCK, lanes), BF), ((2, BLOCK, 128), F32)],
        [block_spec(BLOCK, lanes), block_spec(BLOCK, 128)],
        flops=4 * pairs * HEAD_DIM,
        exps=pairs,
        deps=deps,
    )


def forward_states(b, blocks, info, tokens, states, deps=()):
    lanes = tokens.shape[2] // 3
    heads = lanes // HEAD_DIM
    size = BLOCK // 2
    count_states = states.shape[1]

    def kernel(info_ref, token_ref, state_ref, mixed_ref, log_ref):
        start, plan, state_masks = attention_plan(
            0, b == blocks - 1, size, info_ref[0], info_ref[1], count_states
        )
        for h in range(heads):
            query, key, value = head_slices(lanes, h)
            rows = [pl.ds(start(0, j), size) for j in range(2)]
            keys = jnp.concatenate([state_ref[0, :, key]] + [token_ref[0, at, key] for at in rows], axis=0)
            values = jnp.concatenate([state_ref[0, :, value]] + [token_ref[0, at, value] for at in rows], axis=0)
            for begin in range(0, count_states, size):
                here = slice(begin, begin + size)
                mixed_ref[0, here, query], log_ref[0, here, h : h + 1] = attend_rows(
                    state_ref[0, here, query], keys, values, state_masks
                )

    pairs = 2 * heads * count_states * (count_states + BLOCK)
    return call(
        kernel,
        (2,),
        [info, tokens, states],
        [smem(), pl.BlockSpec((1, BLOCK, 3 * lanes), lambda y: (y, b, 0)), block_spec(count_states, 3 * lanes)],
        [((2, count_states, lanes), BF), ((2, count_states, 128), F32)],
        [block_spec(count_states, lanes), block_spec(count_states, 128)],
        flops=4 * pairs * HEAD_DIM,
        exps=pairs,
        deps=deps,
    )


def add_part(sums, place, part):
    sums[place] = part if place not in sums else sums[place] + part


def backward_tokens(b, blocks, info, tokens, states, logs, grad_mixed, deps=()):
    lanes = tokens.shape[2] // 3
    heads = lanes // HEAD_DIM
    size = BLOCK // 2
    count_states = states.shape[1]

    def kernel(info_ref, token_ref, state_ref, log_ref, grad_ref, query_ref, own_ref, state_out_ref, *before_ref):
        start, plan, state_masks = attention_plan(
            b, b == blocks - 1, size, info_ref[0], info_ref[1], count_states
        )
        for h in range(heads):
            query, key, value = head_slices(lanes, h)
            sums = ({}, {})
            for j, (tiles, masks) in enumerate(plan):
                rows = [pl.ds(start(*place), size) for place in tiles]
                keys = jnp.concatenate([token_ref[0, at, key] for at in rows] + [state_ref[0, :, key]], axis=0)
                values = jnp.concatenate([token_ref[0, at, value] for at in rows] + [state_ref[0, :, value]], axis=0)
                here = pl.ds(start(0, j), size)
                dq, dk, dv = attend_rows_back(
                    token_ref[0, pl.ds(start(b, j), size), query],
                    keys,
                    values,
                    masks,
                    log_ref[0, here, h : h + 1],
                    grad_ref[0, here, query],
                )
                query_ref[0, here, query] = dq.astype(BF)
                for which, grads in enumerate((dk, dv)):
                    for i, place in enumerate(tiles):
                        add_part(sums[which], place, grads[i * size : (i + 1) * size])
                    add_part(sums[which], "state", grads[len(tiles) * size :])
            for which in range(2):
                columns = slice(which * lanes + h * HEAD_DIM, which * lanes + (h + 1) * HEAD_DIM)
                state_out_ref[0, :, columns] = sums[which]["state"]
                for j in range(2):
                    here = pl.ds(start(0, j), size)
                    own_ref[0, here, columns] = sums[which][(b, j)]
                    if b > 0:
                        before_ref[0][0, here, columns] = sums[which][(b - 1, j)]

    pairs = int(token_pairs(b, heads, count_states))
    outputs = [((2, BLOCK, lanes), BF), ((2, BLOCK, 2 * lanes), F32), ((2, count_states, 2 * lanes), F32)]
    out_specs = [block_spec(BLOCK, lanes), block_spec(BLOCK, 2 * lanes), block_spec(count_states, 2 * lanes)]
    if b > 0:
        outputs.append(((2, BLOCK, 2 * lanes), F32))
        out_specs.append(block_spec(BLOCK, 2 * lanes))
    return call(
        kernel,
        (2,),
        [info, tokens, states, logs, grad_mixed],
        [
            smem(),
            block_spec((b + 1) * BLOCK, 3 * lanes),
            block_spec(count_states, 3 * lanes),
            block_spec(BLOCK, 128),
            pl.BlockSpec((1, BLOCK, lanes), lambda y: (y, b, 0)),
        ],
        outputs,
        out_specs,
        flops=10 * pairs * HEAD_DIM,
        exps=pairs,
        deps=deps,
    )


def backward_states(b, blocks, info, tokens, states, logs, grad_mixed, token_sums, state_sums, deps=()):
    lanes = tokens.shape[2] // 3
    heads = lanes // HEAD_DIM
    size = BLOCK // 2
    count_states = states.shape[1]
    count = len(token_sums)

    def kernel(info_ref, token_ref, state_ref, log_ref, grad_ref, sum_ref, *rest):
        token_sum_refs, (state_out_ref, token_out_ref) = rest[:count], rest[count:]
        start, plan, state_masks = attention_plan(
            0, b == blocks - 1, size, info_ref[0], info_ref[1], count_states
        )
        for h in range(heads):
            query, key, value = head_slices(lanes, h)
            rows = [pl.ds(start(0, j), size) for j in range(2)]
            keys = jnp.concatenate([state_ref[0, :, key]] + [token_ref[0, at, key] for at in rows], axis=0)
            values = jnp.concatenate([state_ref[0, :, value]] + [token_ref[0, at, value] for at in rows], axis=0)
            sums = [None, None]
            for begin in range(0, count_states, size):
                here = slice(begin, begin + size)
                dq, dk, dv = attend_rows_back(
                    state_ref[0, here, query],
                    keys,
                    values,
                    state_masks,
                    log_ref[0, here, h : h + 1],
                    grad_ref[0, here, query],
                )
                state_out_ref[0, here, query] = dq.astype(BF)
                sums = [part if old is None else old + part for old, part in zip(sums, (dk, dv))]
            for which, to in ((0, key), (1, value)):
                columns = slice(which * lanes + h * HEAD_DIM, which * lanes + (h + 1) * HEAD_DIM)
                state_out_ref[0, :, to] = (sums[which][:count_states] + sum_ref[0, :, columns]).astype(BF)
                for j in range(2):
                    total = sums[which][count_states + j * size : count_states + (j + 1) * size]
                    for ref in token_sum_refs:
                        total = total + ref[0, rows[j], columns]
                    token_out_ref[0, rows[j], columns] = total.astype(BF)

    pairs = 2 * heads * count_states * (count_states + BLOCK)
    return call(
        kernel,
        (2,),
        [info, tokens, states, logs, grad_mixed, state_sums] + list(token_sums),
        [
            smem(),
            pl.BlockSpec((1, BLOCK, 3 * lanes), lambda y: (y, b, 0)),
            block_spec(count_states, 3 * lanes),
            block_spec(count_states, 128),
            block_spec(count_states, lanes),
            block_spec(count_states, 2 * lanes),
        ]
        + [block_spec(BLOCK, 2 * lanes)] * count,
        [((2, count_states, 3 * lanes), BF), ((2, BLOCK, 2 * lanes), BF)],
        [block_spec(count_states, 3 * lanes), block_spec(BLOCK, 2 * lanes)],
        flops=10 * pairs * HEAD_DIM,
        exps=pairs,
        deps=deps,
    )


def body(
    tokens,
    counts,
    token_weights,
    token_output,
    state_weights,
    state_output,
    hidden_up,
    hidden_down,
    norm_gains,
    gate_bias,
    init_state,
    cotangent,
    state_cotangent,
):
    y, c = lax.axis_index("y"), lax.axis_index("c")
    width = tokens.shape[3]
    state_half = init_state.shape[0] // 2
    blocks = 4 * tokens.shape[2] // BLOCK
    valid_count = lax.dynamic_index_in_dim(counts[:, 0], y, 0, keepdims=False)
    if lax.axis_size("r") == 1:
        places, back = width_places(), width_places_back()
        before, after = (lambda array: array), (lambda array: array)
    else:
        places = back = list(range(PIECES))
        before, after = to_local, from_local
    info = jnp.stack([jnp.asarray(v, jnp.int32) for v in [c, valid_count, y] + places + back])

    def micro(array, index):
        return lax.dynamic_index_in_dim(array[:, 0], index, 0, keepdims=False)

    ORDER.last = []
    shard_rows = token_output.shape[0]
    head, ff = token_output.shape[1], hidden_up.shape[1]
    at_state, at_state_out, at_token_out = 0, 3 * head, ff
    flat = lambda array: array.reshape(shard_rows, -1)
    token = Gather(flat(token_weights))
    token_got = swap(micro(tokens, 1 - y), "y")
    small = jnp.concatenate(
        [
            lax.dynamic_slice_in_dim(init_state, c * state_half, state_half, 0),
            norm_gains,
            gate_bias[None],
            jnp.zeros((12, init_state.shape[1]), BF),
        ],
        axis=0,
    )
    if lax.axis_size("r") > 1:
        small = lax.all_gather(small, "r", axis=1, tiled=True)
    small_got = swap_z(small, 2)
    w_token = token.spread(by_x=True)
    mid = Gather(join_columns([flat(state_weights), state_output], ()))
    small = stack_rows(small, small_got)
    small = stack_rows(small, swap_z(small, 1))
    small_got = swap(small, "x")
    x_rows = own_rows(info, before(micro(tokens, y)), before(token_got))
    small = spread_rows(info, small, small_got)
    gains = [small[state_half + i : state_half + i + 1].astype(F32) for i in range(3)]
    gate_open = jax.nn.sigmoid(small[state_half + 3 : state_half + 4].astype(F32))
    state_now = small[:state_half].astype(F32)
    normed = pair(norm_rows(info, x_rows, gains[0], token.low))
    state_norm = pair(norm_rows(info, state_now, gains[1]))
    w_mid = mid.spread(token.low)
    up = Gather(join_columns([hidden_up, token_output], ()))

    token_proj = project(*normed, w_token, 0, 3 * head, 3 * head // 2, blocks=blocks)
    w_up = up.spread(mid.low)
    down = Gather(join_columns([hidden_down], ()))
    dy_got = swap(micro(cotangent, 1 - y), "y")
    grad_final = lax.dynamic_slice(
        state_cotangent, (y, 0, c * state_half, 0), (1, 1, state_half, width)
    )[0, 0]
    grad_final = local_rows(info, before(grad_final))
    grad_update = pair(back_update(info, grad_final, gate_open))
    kept = []
    mixed = []
    for b in range(blocks):
        proj_wait, state_wait, merge_wait, token_wait = (
            (up.ring, [], up.low + [down.got], up.high) if b == 0 else (up.far, [], down.ring, down.low)
        )
        state_proj = project(*state_norm, w_mid, at_state, 3 * head, 3 * head, deps=proj_wait)
        state_flat, state_logs = forward_states(b, blocks, info, token_proj, state_proj, deps=state_wait)
        both = merge([[state_flat]], w_mid, at_state_out, deps=merge_wait)
        mixed_b, logs = forward_tokens(b, blocks, info, token_proj, state_proj, deps=token_wait)
        mixed.append(mixed_b)
        if b < blocks - 1:
            state_next, next_norm, update = step_state(info, state_now, both, gate_open, gains[1])
        else:
            final_rows, update = last_state(info, state_now, both, gate_open)
            state_next, next_norm = None, None
        kept.append((state_now, state_norm, state_proj, logs, state_logs, state_flat, update))
        state_now = state_next
        state_norm = None if next_norm is None else pair(next_norm)
        if b == 0:
            dy_rows = own_rows(info, before(micro(cotangent, y)), before(dy_got))
            dy_pair = pair(dy_rows)
            grad_state_mixed = project(*grad_update, w_mid, at_state_out, head, head)
            w_down = down.spread()
    hidden, hidden_own = add_norm(
        info, x_rows, merge([[part] for part in mixed], w_up, at_token_out, blocks=blocks, deps=down.high), gains[2]
    )
    hidden_norm = pair(hidden_own)
    activated, slope = project(*hidden_norm, w_up, 0, ff, ff // 2, activate=True)

    quarters = outer([([dy_pair], [activated], 1)], ff // 2, share=2)
    grad_up = project(*dy_pair, w_down, 0, ff, ff // 2, gate=slope)
    both = merge([[grad_up]], w_up, 0)
    ff_grad = Reduce(outer([([hidden_norm], [grad_up], 1)], ff // 2, share=2, into=quarters))
    grad_hidden, branch, gain_hidden = back_hidden(info, hidden, both, gains[2], dy_rows)
    branch = pair(branch)

    grad_mixed = project(*branch, w_up, at_token_out, head, head, blocks=blocks)
    grad_state = grad_final
    gate_sums, gain_sums = [], []
    query_grads, pair_grads = [None] * blocks, [None] * blocks
    update_all, flat_all, norm_all, state_grads = [], [], [], []
    sums = [None] * blocks

    def tokens_back(b, deps=()):
        state_proj, logs = kept[b][2], kept[b][3]
        query_grads[b], *sums[b] = backward_tokens(b, blocks, info, token_proj, state_proj, logs, grad_mixed, deps)

    def states_back(b, later, deps=()):
        state_before, state_norm, state_proj, logs, state_logs, state_flat, update = kept[b]
        own_sums, state_sums, *before_sums = sums[b]
        state_grad, pair_grads[b] = backward_states(
            b, blocks, info, token_proj, state_proj, state_logs, grad_state_mixed, [own_sums] + later, state_sums, deps
        )
        update_all.append(grad_update)
        flat_all.append(state_flat)
        norm_all.append(state_norm)
        state_grads.append(state_grad)
        return merge([[state_grad]], w_mid, at_state), before_sums

    def state_step(b, both, grad_state):
        state_before, update = kept[b][0], kept[b][-1]
        grad_state, low, gain_sum, gate_sum = back_state(
            info, grad_state, state_before, update, both, gate_open, gains[1]
        )
        gain_sums.append(gain_sum)
        gate_sums.append(gate_sum)
        return grad_state, low

    last = blocks - 1
    tokens_back(last)
    both, later = states_back(last, [])
    ff_grad.second()
    for b in range(last - 1, -1, -1):
        tokens_back(b)
        grad_state, low = state_step(b + 1, both, grad_state)
        grad_update = pair(low)
        if b == 0:
            final_rows = after(final_rows)
            final_far = swap(final_rows, "y")
        grad_state_mixed = project(*grad_update, w_mid, at_state_out, head, head)
        if b == 0:
            early_grad = Reduce(
                outer(
                    [
                        ([branch], mixed, blocks),
                        ([normed], query_grads, blocks),
                        ([grad_update] + update_all, [kept[0][5]] + flat_all, 1),
                    ],
                    vmem=28,
                ),
                by_x=True,
            )
        both, later = states_back(b, later)

    late_grad = Reduce(outer([([normed], pair_grads, blocks), (norm_all, state_grads, 1)], vmem=28), by_x=True)
    token_both = merge([[query_grads[i], pair_grads[i]] for i in range(blocks)], w_token, 0, blocks=blocks)
    grad_state, low = state_step(0, both, grad_state)
    out_both = merge([[activated]], w_down, 0)
    early_grad.second()
    keep, send, gain_token = back_input(info, x_rows, token_both, gains[0], grad_hidden)
    input_keep, input_got = after(keep), swap(after(send), "y")
    near, far = pack_small(info, grad_state, [[gain_token], gain_sums, [gain_hidden], gate_sums])
    far = swap(far, "x")
    ff_grad.third()
    keep, send = add_out(info, hidden, out_both)
    output_got = swap(after(send), "y")
    output_keep = after(keep)
    late_grad.second()
    near, far = add_small(info, near, far)
    far = swap_z(far, 1)
    early_grad.third()
    ff_grad.fourth()
    near, far = add_small(info, near, far)
    far = swap_z(far, 2)
    final_state = place_state(info, final_rows, swap(final_rows, "c"), final_far, swap(final_far, "c"))[:, None]
    early_grad.fourth()
    near = add_pair(info, near, far)
    if lax.axis_size("r") > 1:
        near = lax.psum_scatter(near, "r", scatter_dimension=1, tiled=True)
    far = swap(near, "y")
    late_grad.third()
    near = add_pair(info, near, far)
    far = swap(near, "c")
    output = place_rows(info, output_keep, output_got)[:, None]
    init_grad, grad_gains, grad_gate = place_small(info, near, far, state_half)
    late_grad.fourth()
    input_grad = place_rows(info, input_keep, input_got)[:, None]
    both = ff_grad.total()
    grad_hidden_down, grad_hidden_up = both[:, :ff], both[:, ff:]
    early = early_grad.total()
    grad_token_output, grad_query, grad_state_output = [early[:, i * head : (i + 1) * head] for i in range(3)]
    late = late_grad.total()
    grad_token_weights = jnp.stack([grad_query, late[:, :head], late[:, head : 2 * head]], axis=1)
    grad_state_weights = late[:, 2 * head :].reshape(-1, 3, head)
    return (
        output,
        final_state,
        input_grad,
        grad_token_weights,
        grad_token_output,
        grad_state_weights,
        grad_state_output,
        grad_hidden_up,
        grad_hidden_down,
        grad_gains,
        grad_gate[0],
        init_grad,
    )


def solution(mesh):
    dp, heads = mesh.devices.shape
    fine = Mesh(mesh.devices.reshape(dp // (2 * RING), RING, 2, heads // 2, 2), ("r", "z", "x", "y", "c"))
    d, h = ("r", "z", "x"), ("y", "c")
    return jax.shard_map(
        body,
        mesh=fine,
        in_specs=(
            P(None, d, h, None),
            P(None, d),
            P(d, None, h),
            P(d, h),
            P(d, None, h),
            P(d, h),
            P(d, h),
            P(d, h),
            P(None, d),
            P(d),
            P(None, d),
            P(None, d, h, None),
            P(None, d, None, None),
        ),
        out_specs=(
            P(None, d, h, None),
            P(None, d, None, None),
            P(None, d, h, None),
            P(d, None, h),
            P(d, h),
            P(d, None, h),
            P(d, h),
            P(d, h),
            P(d, h),
            P(None, d),
            P(d),
            P(None, d),
        ),
        check_vma=False,
    )
```

```python
import functools

import jax
import jax.numpy as jnp
from jax import lax
from jax.experimental import pallas as pl
from jax.experimental.pallas import tpu as pltpu
from jax.sharding import Mesh
from jax.sharding import PartitionSpec as P

HEAD_DIM = 128
BLOCK = 512
EPSILON = 1e-06
MASKED = -1e30
COST = 0.01
LONG = 1e11
GELU = 0.7978845608028654
RING = 4
BF = jnp.bfloat16
F32 = jnp.float32


def swap(array, axis):
    return lax.ppermute(array, axis, [(0, 1), (1, 0)])


def swap_z(array, bit):
    return lax.ppermute(array, "z", [(i, i ^ bit) for i in range(RING)])


def matmul(left, right, contract):
    return lax.dot_general(
        left, right, (contract, ((), ())), preferred_element_type=jnp.float32
    )


def mm(left, right):
    return matmul(left, right, ((1,), (0,)))


def mm_nt(left, right):
    return matmul(left, right, ((1,), (1,)))


def mm_tn(left, right):
    return matmul(left, right, ((0,), (0,)))


RING_BITS = (0, 2, 1, 3)


def width_places():
    z, x = lax.axis_index("z"), lax.axis_index("x")
    return [jnp.bitwise_xor(z, RING_BITS[k]) * 2 + jnp.bitwise_xor(x, dx) for dx in range(2) for k in range(RING)]


def width_places_back():
    z, x = lax.axis_index("z"), lax.axis_index("x")
    places = []
    for z_to in range(RING):
        apart = jnp.bitwise_xor(z, z_to)
        k = lax.rem(apart, 2) * 2 + lax.div(apart, 2)
        places += [jnp.bitwise_xor(x, x_to) * RING + k for x_to in range(2)]
    return places


def take_pieces(array, places):
    groups = lax.axis_size("r")
    lead, width = array.shape[:-1], array.shape[-1]
    split = array.reshape(lead + (groups, len(places), width // (groups * len(places))))
    axis = len(lead) + 1
    return [lax.dynamic_index_in_dim(split, place, axis, keepdims=False) for place in places]


def to_local(array):
    pieces = take_pieces(array, width_places())
    lead = array.shape[:-1]
    return jnp.concatenate([p.reshape(lead + (-1,)) for p in pieces], axis=-1)


def from_local(array):
    groups = lax.axis_size("r")
    lead, width = array.shape[:-1], array.shape[-1]
    split = array.reshape(lead + (2 * RING, groups, width // (groups * 2 * RING)))
    axis = len(lead)
    pieces = [lax.dynamic_index_in_dim(split, place, axis, keepdims=False) for place in width_places_back()]
    return jnp.stack(pieces, axis=axis + 1).reshape(array.shape)


def gather_groups(array, axis):
    if lax.axis_size("r") == 1:
        return array
    return lax.all_gather(array, "r", axis=axis, tiled=True)


def scatter_groups(array, axis):
    if lax.axis_size("r") == 1:
        return array
    return lax.psum_scatter(array, "r", scatter_dimension=axis, tiled=True)


class Order:
    def __init__(self):
        self.last = []


ORDER = Order()


def call(kernel, grid, inputs, in_specs, outputs, out_specs, flops=0, exps=0, deps=(), vmem=16, long=False, **more):
    block_bytes = sum(a.size * a.dtype.itemsize for a in inputs)
    shapes = [jax.ShapeDtypeStruct(shape, dtype) for shape, dtype in outputs]
    out_bytes = sum(s.size * s.dtype.itemsize for s in shapes)
    given = len(inputs)
    deps = [array for array in list(deps) + ORDER.last if all(array is not other for other in inputs)]

    def run(*refs):
        kernel(*refs[:given], *refs[given + len(deps) :])

    out = pl.pallas_call(
        run,
        grid=grid,
        in_specs=list(in_specs) + [pl.BlockSpec(memory_space=pl.ANY)] * len(deps),
        out_specs=out_specs,
        out_shape=shapes,
        compiler_params=pltpu.CompilerParams(vmem_limit_bytes=vmem * 2**20),
        cost_estimate=pl.CostEstimate(
            flops=int(LONG) if long else int(flops * COST), bytes_accessed=int((block_bytes + out_bytes) * COST), transcendentals=int(exps * COST)
        ),
        **more,
    )(*inputs, *deps)
    ORDER.last = [min(out, key=lambda array: array.size)]
    return out


def whole(array):
    return pl.BlockSpec(array.shape, lambda *_: (0,) * array.ndim)


def whole_out(shape):
    return pl.BlockSpec(shape, lambda *_: (0,) * len(shape))


def stack_rows(first, second, deps=()):
    rows, width = first.shape

    def kernel(first_ref, second_ref, out_ref):
        out_ref[:rows] = first_ref[...]
        out_ref[rows:] = second_ref[...]

    return call(
        kernel,
        (1,),
        [first, second],
        [whole(first)] * 2,
        [((2 * rows, width), BF)],
        [whole_out((2 * rows, width))],
        deps=deps,
    )[0]


def join_columns(arrays, deps):
    rows = arrays[0].shape[0]
    width = sum(array.shape[1] for array in arrays)

    def kernel(*refs):
        place = 0
        for ref in refs[:-1]:
            refs[-1][:, place : place + ref.shape[1]] = ref[...]
            place += ref.shape[1]

    return call(
        kernel,
        (1,),
        arrays,
        [whole(array) for array in arrays],
        [((rows, width), BF)],
        [whole_out((rows, width))],
        deps=deps,
    )[0]


class Gather:
    def __init__(self, shard):
        self.shard = gather_groups(shard, 0)
        self.got = swap_z(self.shard, 2)

    def spread(self, deps=(), by_x=False):
        low = stack_rows(self.shard, self.got, deps)
        low_x, low_y = swap(low, "x"), swap(low, "y")
        high = swap_z(low, 1)
        high_y, high_x = swap(high, "y"), swap(high, "x")
        low_xy = swap(low_y, "x") if by_x else swap(low_x, "y")
        high_xy = swap(high_y, "x")
        self.pieces = [[[low, high], [low_x, high_x]], [[low_y, high_y], [low_xy, high_xy]]]
        self.ring, self.low, self.high, self.far = [high], [low_x, low_y], [high_x, high_y], [low_xy, high_xy]
        return self.pieces


def flat_pieces(pieces):
    return [pieces[y][x][half] for y in range(2) for x in range(2) for half in range(2)]


def spread_rows(info, near, far):
    size = near.shape[1]
    rows = near.shape[0] // RING

    def kernel(near_ref, far_ref, out_ref):
        for k in range(RING):
            out_ref[:, k * size : (k + 1) * size] = near_ref[k * rows : (k + 1) * rows]
            out_ref[:, (RING + k) * size : (RING + k + 1) * size] = far_ref[k * rows : (k + 1) * rows]

    return call(
        kernel,
        (1,),
        [near, far],
        [whole(near), whole(far)],
        [((rows, 2 * RING * size), near.dtype)],
        [whole_out((rows, 2 * RING * size))],
    )[0]


def row_order(own, other, blocks):
    per = own.shape[0] // blocks
    parts = []
    for b in range(blocks):
        parts += [own[b * per : (b + 1) * per], other[b * per : (b + 1) * per]]
    return jnp.concatenate(parts, axis=0)


def project(own, other, pieces, column, width, block, blocks=1, gate=None, activate=False, deps=(), long=False):
    rows = own.shape[0] * 2
    refs = flat_pieces(pieces)
    first = column // block

    def kernel(*args):
        own_ref, other_ref, weights = args[0], args[1], args[2:10]
        left = row_order(own_ref[...], other_ref[...], blocks)
        for y in range(2):
            weight = jnp.concatenate([ref[...] for ref in weights[4 * y : 4 * y + 4]], axis=0)
            total = mm(left, weight)
            if gate is not None:
                gate_ref, out_ref = args[10], args[11]
                low = total.astype(BF).astype(F32)
                out_ref[y] = (low * gate_ref[y].astype(F32)).astype(BF)
            elif activate:
                act_ref, slope_ref = args[10], args[11]
                square = total * total
                curve = jnp.tanh(total * (GELU * 0.044715 * square + GELU))
                share = 0.5 * curve + 0.5
                act = total * share
                act_ref[y] = act.astype(BF)
                slope = share + act * (1.0 - curve) * (GELU * 0.134145 * square + GELU)
                slope_ref[y] = slope.astype(BF)
            else:
                args[10][y] = total.astype(BF)

    spec = pl.BlockSpec((2, rows, block), lambda j: (0, 0, j))
    weight_spec = [pl.BlockSpec((ref.shape[0], block), lambda j: (0, first + j)) for ref in refs]
    extra = [] if gate is None else [gate]
    count = 2 if activate else 1
    out = call(
        kernel,
        (width // block,),
        [own, other] + refs + extra,
        [whole(own), whole(other)] + weight_spec + [spec] * len(extra),
        [((2, rows, width), BF)] * count,
        [spec] * count,
        flops=4 * rows * own.shape[1] * width,
        deps=deps, long=long,
    )
    return out if activate else out[0]


def merge(lefts, pieces, column, blocks=1, deps=(), long=False, halves=1):
    refs = flat_pieces(pieces)
    columns = sum(part.shape[2] for part in lefts[0])
    per = lefts[0][0].shape[1] // 2
    rows = per * len(lefts)
    width = 8 * refs[0].shape[0] // 2
    first = column // columns
    parts_count = len(lefts[0])
    flat = [part for left in lefts for part in left]

    def kernel(*args):
        left_refs, weights = args[: len(flat)], args[len(flat) : len(flat) + 8]
        own_ref, *other_refs = args[len(flat) + 8 :]
        size = rows // halves
        sides = [
            jnp.concatenate([ref[...] for ref in weights[4 * y : 4 * y + 4]], axis=0) for y in range(2)
        ]
        for core in (1, 0):
            total = None
            for y in range(2):
                left = []
                for b in range(len(lefts)):
                    here = left_refs[b * parts_count : (b + 1) * parts_count]
                    left.append(jnp.concatenate([ref[y, core * per : (core + 1) * per] for ref in here], axis=1))
                piece = mm_nt(jnp.concatenate(left, axis=0), sides[y])
                total = piece if total is None else total + piece
            if core:
                for i, ref in enumerate(other_refs):
                    ref[...] = total[i * size : (i + 1) * size].astype(BF)
            else:
                own_ref[...] = total

    weight_spec = [pl.BlockSpec((ref.shape[0], columns), lambda i: (0, first)) for ref in refs]
    return call(
        kernel,
        (1,),
        flat + refs,
        [whole(left) for left in flat] + weight_spec,
        [((rows, width), F32)] + [((rows // halves, width), BF)] * halves,
        [whole_out((rows, width))] + [whole_out((rows // halves, width))] * halves,
        flops=8 * rows * width * columns,
        deps=deps, long=long,
    )


QUARTERS = ((1, 1), (1, 0), (0, 1), (0, 0))


def outer(segments, block=None, vmem=16, deps=(), long=False, split=False):
    width = segments[0][0][0][0].shape[1]
    sizes = [rights[0].shape[2] for lefts, rights, blocks in segments]
    columns = sum(sizes)
    block = columns if block is None else block
    half = width // 2
    inputs, in_specs, flops = [], [], 0
    for lefts, rights, blocks in segments:
        flat = [array for pair_ in lefts for array in pair_]
        inputs += flat + list(rights)
        in_specs += [whole(array) for array in flat]
        wide = min(block, rights[0].shape[2])
        in_specs += [pl.BlockSpec((2, right.shape[1], wide), lambda j: (0, 0, j)) for right in rights]
        flops += 4 * width * rights[0].shape[2] * sum(right.shape[1] for right in rights)

    sizes_out = [half // 2, half, half, half, half // 2] if split else [half] * 4

    def kernel(*args):
        outs = args[len(inputs) :]
        place, column = 0, 0
        for lefts, rights, blocks in segments:
            left_refs = args[place : place + 2 * len(lefts)]
            right_refs = args[place + 2 * len(lefts) : place + 2 * len(lefts) + len(rights)]
            place += 2 * len(lefts) + len(rights)
            left = jnp.concatenate(
                [row_order(left_refs[2 * i][...], left_refs[2 * i + 1][...], blocks) for i in range(len(lefts))], axis=0
            )
            here = slice(column, column + right_refs[0].shape[2])
            column += right_refs[0].shape[2]
            for y in (1, 0):
                right = jnp.concatenate([ref[y] for ref in right_refs], axis=0)
                for x in (1, 0):
                    total = mm_tn(left[:, x * half : (x + 1) * half], right).astype(BF)
                    if split and x and y:
                        outs[0][:, here] = total[: half // 2]
                        outs[-1][:, here] = total[half // 2 :]
                    else:
                        outs[QUARTERS.index((x, y))][:, here] = total

    return call(
        kernel,
        (columns // block,),
        inputs,
        in_specs,
        [((rows, columns), BF) for rows in sizes_out],
        [pl.BlockSpec((rows, block), lambda j: (0, j)) for rows in sizes_out],
        flops=flops,
        vmem=vmem,
        deps=deps, long=long,
    )


def add_low(first, second, deps=(), long=False):
    rows, columns = first.shape
    half = rows // 2

    def kernel(first_ref, second_ref, out_ref):
        out_ref[...] = (first_ref[...].astype(F32) + second_ref[...].astype(F32)).astype(BF)

    spec = pl.BlockSpec((half, columns), lambda i: (i, 0))
    return call(kernel, (2,), [first, second], [spec, spec], [(first.shape, BF)], [spec], deps=deps, long=long)[0]


def add_split(arrays, deps=(), long=False, whole_sum=False):
    rows, columns = arrays[0].shape
    part = rows if whole_sum else rows // 2
    types = (F32,) if whole_sum else (F32, BF)

    def kernel(*refs):
        for half, out_ref in enumerate(refs[len(arrays) :]):
            piece = slice(half * part, (half + 1) * part)
            total = refs[0][piece].astype(F32)
            for ref in refs[1 : len(arrays)]:
                total = total + ref[piece].astype(F32)
            out_ref[...] = total.astype(out_ref.dtype)

    return call(
        kernel,
        (1,),
        arrays,
        [whole(array) for array in arrays],
        [((part, columns), dtype) for dtype in types],
        [whole_out((part, columns))] * len(types),
        deps=deps, long=long,
    )


def add_into(array, piece, half, deps=()):
    rows, columns = piece.shape

    def kernel(array_ref, piece_ref, out_ref):
        out_ref[...] = (array_ref[...].astype(F32) + piece_ref[...].astype(F32)).astype(BF)

    here, there = pl.BlockSpec((rows, columns), lambda i: (half, 0)), pl.BlockSpec((rows, columns), lambda i: (0, 0))
    return call(
        kernel,
        (1,),
        [array, piece],
        [here, there],
        [(array.shape, BF)],
        [here],
        input_output_aliases={0: 0},
        deps=deps,
    )[0]


class Reduce:
    def __init__(self, quarters, first_axis=None):
        self.first_axis = first_axis
        if first_axis is None:
            low11, self.out10, self.out01, self.out00, high11 = quarters
            self.first = [swap(low11, "y"), swap(high11, "x")]
        else:
            out11, self.out10, self.out01, self.out00 = quarters
            self.first = [swap(out11, first_axis)]

    def second(self, deps=(), long=False):
        if self.first_axis is None:
            self.out10 = add_into(self.out10, self.first[0], 0, deps)
            self.out01 = add_into(self.out01, self.first[1], 1, deps)
        elif self.first_axis == "x":
            self.out01 = add_low(self.out01, self.first[0], deps, long)
        else:
            self.out10 = add_low(self.out10, self.first[0], deps, long)
        self.next = [swap(self.out10, "x"), swap(self.out01, "y")]

    def third(self, deps=(), long=False):
        self.near, far = add_split([self.out00] + self.next, deps, long)
        self.got = swap_z(far, 1)

    def fourth(self, deps=(), long=False):
        self.near, far = add_split([self.near, self.got], deps, long)
        self.got = swap_z(far, 2)

    def finish(self, **how):
        self.total = scatter_groups(add_split([self.near, self.got], whole_sum=True, **how)[0], 0)


def pair(own):
    return own, swap(own, "c")


INFO = 3
PIECES = 2 * RING
SMALL = 16


def smem():
    return pl.BlockSpec(memory_space=pltpu.SMEM)


def lanes_at(info_ref, index, width):
    size = width // PIECES
    return pl.ds(pl.multiple_of(info_ref[index] * size, size), size)


def reorder_in(info_ref, source, target, rows=slice(None)):
    width = source.shape[-1]
    size = width // PIECES
    for k in range(PIECES):
        target[rows, k * size : (k + 1) * size] = source[:, lanes_at(info_ref, INFO + k, width)].astype(target.dtype)


def reorder_out(info_ref, source, target, rows=slice(None)):
    width = source.shape[-1]
    size = width // PIECES
    for k in range(PIECES):
        part = source[rows, lanes_at(info_ref, INFO + PIECES + k, width)]
        target[:, k * size : (k + 1) * size] = part.astype(target.dtype)


def swap_all(arrays):
    return [swap(array, "c") for array in arrays]


def both_cores(own_ref, low_ref, high_ref):
    return own_ref[...] + jnp.concatenate([low_ref[...], high_ref[...]], axis=0).astype(F32)


def inverse_rms(values):
    return lax.rsqrt(jnp.mean(values * values, axis=-1, keepdims=True) + EPSILON)


def rms_back(values, gain, grad):
    inverse = inverse_rms(values)
    scaled = values * inverse
    weighted = grad * gain
    back = inverse * (weighted - scaled * jnp.mean(scaled * weighted, axis=-1, keepdims=True))
    return back, jnp.sum(grad * scaled, axis=0, keepdims=True)


def rowwise(kernel, inputs, outputs, scratch=(), deps=(), long=False):
    return call(
        kernel,
        (1,),
        inputs,
        [smem()] + [whole(array) for array in inputs[1:]],
        outputs,
        [whole_out(shape) for shape, _ in outputs],
        scratch_shapes=[pltpu.VMEM(shape, dtype) for shape, dtype in scratch],
        deps=deps, long=long,
    )


def own_rows(info, keep, got):
    rows, width = keep.shape

    def kernel(info_ref, keep_ref, got_ref, out_ref):
        y = info_ref[2]
        reorder_in(info_ref, keep_ref, out_ref, pl.ds(pl.multiple_of(y * rows, rows), rows))
        reorder_in(info_ref, got_ref, out_ref, pl.ds(pl.multiple_of((1 - y) * rows, rows), rows))

    return rowwise(kernel, [info, keep, got], [((2 * rows, width), BF)])[0]


def local_rows(info, array):
    def kernel(info_ref, in_ref, out_ref):
        reorder_in(info_ref, in_ref, out_ref)

    return rowwise(kernel, [info, array], [(array.shape, array.dtype)])[0]


def norm_rows(info, values, gain, deps=()):
    def kernel(info_ref, in_ref, gain_ref, out_ref):
        rows = in_ref[...].astype(F32)
        out_ref[...] = (rows * inverse_rms(rows) * gain_ref[...]).astype(BF)

    return rowwise(kernel, [info, values, gain], [(values.shape, BF)], deps=deps)[0]


def add_norm(info, rows, both, gain):
    own, *others = both

    def kernel(info_ref, row_ref, own_ref, got_ref, gain_ref, hidden_ref, norm_ref):
        hidden = row_ref[...].astype(F32) + (own_ref[...] + got_ref[...].astype(F32))
        hidden_ref[...] = hidden
        norm_ref[...] = (hidden * inverse_rms(hidden) * gain_ref[...]).astype(BF)

    return rowwise(kernel, [info, rows, own, *swap_all(others), gain], [(rows.shape, F32), (rows.shape, BF)])


def add_out(info, hidden, both):
    own, *others = both
    rows, width = hidden.shape
    half = rows // 2

    def kernel(info_ref, hidden_ref, own_ref, low_ref, high_ref, keep_ref, send_ref, scratch):
        y = info_ref[2]
        scratch[...] = hidden_ref[...] + (both_cores(own_ref, low_ref, high_ref))
        reorder_out(info_ref, scratch, keep_ref, pl.ds(pl.multiple_of(y * half, half), half))
        reorder_out(info_ref, scratch, send_ref, pl.ds(pl.multiple_of((1 - y) * half, half), half))

    return rowwise(
        kernel,
        [info, hidden, own, *swap_all(others)],
        [((half, width), BF)] * 2,
        [((rows, width), F32)],
    )


def step_state(info, state, both, gate, gain):
    own, *others = both

    def kernel(info_ref, state_ref, own_ref, got_ref, gate_ref, gain_ref, next_ref, norm_ref, update_ref):
        update = own_ref[...] + got_ref[...].astype(F32)
        update_ref[...] = update
        after = gate_ref[...] * state_ref[...] + (1.0 - gate_ref[...]) * update
        next_ref[...] = after
        norm_ref[...] = (after * inverse_rms(after) * gain_ref[...]).astype(BF)

    return rowwise(
        kernel,
        [info, state, own, *swap_all(others), gate, gain],
        [(state.shape, F32), (state.shape, BF), (state.shape, F32)],
    )


def last_state(info, state, both, gate):
    own, *others = both

    def kernel(info_ref, state_ref, own_ref, got_ref, gate_ref, final_ref, update_ref, scratch):
        update = own_ref[...] + got_ref[...].astype(F32)
        update_ref[...] = update
        scratch[...] = gate_ref[...] * state_ref[...] + (1.0 - gate_ref[...]) * update
        reorder_out(info_ref, scratch, final_ref)

    return rowwise(
        kernel,
        [info, state, own, *swap_all(others), gate],
        [(state.shape, BF), (state.shape, F32)],
        [(state.shape, F32)],
    )


def back_hidden(info, hidden, both, gain, dy):
    own, *others = both

    def kernel(info_ref, hidden_ref, own_ref, low_ref, high_ref, gain_ref, dy_ref, grad_ref, branch_ref, gain_grad_ref):
        grad = both_cores(own_ref, low_ref, high_ref)
        back, gain_grad_ref[...] = rms_back(hidden_ref[...], gain_ref[...], grad)
        total = dy_ref[...].astype(F32) + back
        grad_ref[...] = total
        branch_ref[...] = total.astype(BF)

    return rowwise(
        kernel,
        [info, hidden, own, *swap_all(others), gain, dy],
        [(hidden.shape, F32), (hidden.shape, BF), ((1, hidden.shape[1]), F32)],
    )


def back_update(info, grad, gate):
    def kernel(info_ref, grad_ref, gate_ref, out_ref):
        out_ref[...] = ((1.0 - gate_ref[...]) * grad_ref[...].astype(F32)).astype(BF)

    return rowwise(kernel, [info, grad, gate], [(grad.shape, BF)])[0]


def back_state(info, grad, state, update, both, gate, gain):
    own, *others = both
    width = state.shape[1]

    def kernel(
        info_ref, grad_ref, state_ref, update_ref, own_ref, low_ref, high_ref, gate_ref, gain_ref, out_ref, next_ref, gain_grad_ref, gate_grad_ref
    ):
        gate_open = gate_ref[...]
        grad_now = grad_ref[...].astype(F32)
        values = state_ref[...]
        gate_grad_ref[...] = jnp.sum(grad_now * (values - update_ref[...]), axis=0, keepdims=True) * (
            gate_open * (1.0 - gate_open)
        )
        back, gain_grad_ref[...] = rms_back(values, gain_ref[...], both_cores(own_ref, low_ref, high_ref))
        total = gate_open * grad_now + back
        out_ref[...] = total
        next_ref[...] = ((1.0 - gate_open) * total).astype(BF)

    return rowwise(
        kernel,
        [info, grad, state, update, own, *swap_all(others), gate, gain],
        [(state.shape, F32), (state.shape, BF), ((1, width), F32), ((1, width), F32)],
    )


def back_input(info, values, both, gain, grad_hidden):
    own, *others = both
    rows, width = values.shape
    half = rows // 2

    def kernel(info_ref, value_ref, own_ref, low_ref, high_ref, gain_ref, grad_ref, keep_ref, send_ref, gain_grad_ref, scratch):
        y = info_ref[2]
        grad = both_cores(own_ref, low_ref, high_ref)
        back, gain_grad_ref[...] = rms_back(value_ref[...].astype(F32), gain_ref[...], grad)
        scratch[...] = grad_ref[...] + back
        reorder_out(info_ref, scratch, keep_ref, pl.ds(pl.multiple_of(y * half, half), half))
        reorder_out(info_ref, scratch, send_ref, pl.ds(pl.multiple_of((1 - y) * half, half), half))

    return rowwise(
        kernel,
        [info, values, own, *swap_all(others), gain, grad_hidden],
        [((half, width), F32), ((half, width), BF), ((1, width), F32)],
        [((rows, width), F32)],
    )


def pack_small(info, states, vectors):
    rows, width = states.shape
    half = width // 2
    counts = [len(group) for group in vectors]
    flat = [vector for group in vectors for vector in group]
    pad = SMALL - len(vectors)

    def kernel(info_ref, state_ref, *refs):
        near_ref, far_ref = refs[len(flat) :]
        parts, place = [], 0
        for count in counts:
            parts.append(sum(ref[...] for ref in refs[place : place + count]))
            place += count
        tail = jnp.concatenate(parts + [jnp.zeros((pad, width), F32)], axis=0)
        near_ref[:rows] = state_ref[:, :half]
        near_ref[rows:] = tail[:, :half]
        far_ref[:rows] = state_ref[:, half:].astype(BF)
        far_ref[rows:] = tail[:, half:].astype(BF)

    shape = (rows + SMALL, half)
    return rowwise(kernel, [info, states] + flat, [(shape, F32), (shape, BF)])


def add_small(info, near, got):
    rows, width = near.shape
    half = width // 2

    def kernel(info_ref, near_ref, got_ref, near_out, far_out):
        total = near_ref[...] + got_ref[...].astype(F32)
        near_out[...] = total[:, :half]
        far_out[...] = total[:, half:].astype(BF)

    return rowwise(kernel, [info, near, got], [((rows, half), F32), ((rows, half), BF)])


def add_pair(info, near, got):
    def kernel(info_ref, near_ref, got_ref, out_ref):
        out_ref[...] = near_ref[...] + got_ref[...].astype(F32)

    return rowwise(kernel, [info, near, got], [(near.shape, F32)])[0]


def place_small(info, near, far, states):
    size = near.shape[1]

    def kernel(info_ref, near_ref, far_ref, state_ref, gain_ref, gate_ref):
        c = info_ref[0]
        state_ref[pl.ds(pl.multiple_of(c * states, states), states)] = near_ref[:states]
        state_ref[pl.ds(pl.multiple_of((1 - c) * states, states), states)] = far_ref[:states]
        total = near_ref[states:] + far_ref[states:]
        gain_ref[...] = total[:3]
        gate_ref[...] = total[3:4]

    return rowwise(kernel, [info, near, far], [((2 * states, size), F32), ((3, size), F32), ((1, size), F32)])


def place_rows(info, keep, got):
    shape = (2,) + keep.shape

    def kernel(info_ref, keep_ref, got_ref, out_ref):
        y = info_ref[2]
        out_ref[y] = keep_ref[...]
        out_ref[1 - y] = got_ref[...].astype(keep.dtype)

    return rowwise(kernel, [info, keep, got], [(shape, keep.dtype)])[0]


def place_state(info, near, near_c, far, far_c):
    rows, width = near.shape

    def kernel(info_ref, near_ref, near_c_ref, far_ref, far_c_ref, out_ref):
        c, y = info_ref[0], info_ref[2]
        here = pl.ds(pl.multiple_of(c * rows, rows), rows)
        there = pl.ds(pl.multiple_of((1 - c) * rows, rows), rows)
        out_ref[y, here] = near_ref[...]
        out_ref[y, there] = near_c_ref[...]
        out_ref[1 - y, here] = far_ref[...]
        out_ref[1 - y, there] = far_c_ref[...]

    return rowwise(kernel, [info, near, near_c, far, far_c], [((2, 2 * rows, width), near.dtype)])[0]


SCALE = HEAD_DIM ** (-0.5)


def key_tiles(b, j):
    tiles = []
    if b > 0:
        tiles += [(b - 1, jj, "after" if jj == j else "all") for jj in range(j, 2)]
    tiles += [(b, jj, "until" if jj == j else "all") for jj in range(j + 1)]
    return tiles


def tile_mask(kind, size, limit):
    rows = lax.broadcasted_iota(jnp.int32, (size, size), 0)
    columns = lax.broadcasted_iota(jnp.int32, (size, size), 1)
    mask = None
    if kind == "after":
        mask = columns > rows
    if kind == "until":
        mask = columns <= rows
    if limit is not None:
        inside = columns < limit
        mask = inside if mask is None else mask & inside
    return mask


def masked_scores(queries, keys, masks):
    scores = mm_nt(queries, keys) * SCALE
    parts, place = [], 0
    for size, mask in masks:
        part = scores[:, place : place + size]
        parts.append(part if mask is None else jnp.where(mask, part, MASKED))
        place += size
    return jnp.concatenate(parts, axis=1)


def attention_plan(b, last, size, core, count, states):
    def start(block, j):
        return pl.multiple_of(block * 2 * size + jnp.bitwise_xor(core, j) * size, size)

    plan = []
    for j in range(2):
        tiles, masks = [], []
        for block, jj, kind in key_tiles(b, j):
            limit = count - jj * size if block == b and last else None
            tiles.append((block, jj))
            masks.append((size, tile_mask(kind, size, limit)))
        plan.append((tiles, masks + [(states, None)]))
    state_masks = [(states, None)]
    for jj in range(2):
        state_masks.append((size, tile_mask("all", size, count - jj * size if last else None)))
    return start, plan, state_masks


def block_spec(rows, width):
    return pl.BlockSpec((1, rows, width), lambda y: (y, 0, 0))


def head_slices(lanes, h):
    return [slice(p * lanes + h * HEAD_DIM, p * lanes + (h + 1) * HEAD_DIM) for p in range(3)]


def attend_rows(queries, keys, values, masks):
    scores = masked_scores(queries, keys, masks)
    top = jnp.max(scores, axis=1, keepdims=True)
    weights = jnp.exp(scores - top)
    total = jnp.sum(weights, axis=1, keepdims=True)
    mixed = mm(weights.astype(BF), values) / total
    return mixed.astype(BF), top + jnp.log(total)


def attend_rows_back(queries, keys, values, masks, log_total, grad):
    scores = masked_scores(queries, keys, masks)
    probs = jnp.exp(scores - log_total)
    grad_probs = mm_nt(grad, values)
    row_sum = jnp.sum(grad_probs * probs, axis=1, keepdims=True)
    low = (probs * (grad_probs - row_sum)).astype(BF)
    return mm(low, keys) * SCALE, mm_tn(low, queries) * SCALE, mm_tn(probs.astype(BF), grad)


def token_pairs(b, heads, states):
    return 2 * heads * BLOCK * (BLOCK * (1.25 if b else 0.75) + states)


def forward_tokens(b, blocks, info, tokens, states, deps=()):
    lanes = tokens.shape[2] // 3
    heads = lanes // HEAD_DIM
    size = BLOCK // 2
    count_states = states.shape[1]

    def kernel(info_ref, token_ref, state_ref, mixed_ref, log_ref):
        start, plan, state_masks = attention_plan(
            b, b == blocks - 1, size, info_ref[0], info_ref[1], count_states
        )
        for h in range(heads):
            query, key, value = head_slices(lanes, h)
            for j, (tiles, masks) in enumerate(plan):
                rows = [pl.ds(start(*place), size) for place in tiles]
                keys = jnp.concatenate([token_ref[0, at, key] for at in rows] + [state_ref[0, :, key]], axis=0)
                values = jnp.concatenate([token_ref[0, at, value] for at in rows] + [state_ref[0, :, value]], axis=0)
                here = pl.ds(start(0, j), size)
                mixed_ref[0, here, query], log_ref[0, here, h : h + 1] = attend_rows(
                    token_ref[0, pl.ds(start(b, j), size), query], keys, values, masks
                )

    pairs = int(token_pairs(b, heads, count_states))
    return call(
        kernel,
        (2,),
        [info, tokens, states],
        [smem(), block_spec((b + 1) * BLOCK, 3 * lanes), block_spec(count_states, 3 * lanes)],
        [((2, BLOCK, lanes), BF), ((2, BLOCK, 128), F32)],
        [block_spec(BLOCK, lanes), block_spec(BLOCK, 128)],
        flops=4 * pairs * HEAD_DIM,
        exps=pairs,
        deps=deps,
    )


def forward_states(b, blocks, info, tokens, states, deps=()):
    lanes = tokens.shape[2] // 3
    heads = lanes // HEAD_DIM
    size = BLOCK // 2
    count_states = states.shape[1]

    def kernel(info_ref, token_ref, state_ref, mixed_ref, log_ref):
        start, plan, state_masks = attention_plan(
            0, b == blocks - 1, size, info_ref[0], info_ref[1], count_states
        )
        for h in range(heads):
            query, key, value = head_slices(lanes, h)
            rows = [pl.ds(start(0, j), size) for j in range(2)]
            keys = jnp.concatenate([state_ref[0, :, key]] + [token_ref[0, at, key] for at in rows], axis=0)
            values = jnp.concatenate([state_ref[0, :, value]] + [token_ref[0, at, value] for at in rows], axis=0)
            for begin in range(0, count_states, size):
                here = slice(begin, begin + size)
                mixed_ref[0, here, query], log_ref[0, here, h : h + 1] = attend_rows(
                    state_ref[0, here, query], keys, values, state_masks
                )

    pairs = 2 * heads * count_states * (count_states + BLOCK)
    return call(
        kernel,
        (2,),
        [info, tokens, states],
        [smem(), pl.BlockSpec((1, BLOCK, 3 * lanes), lambda y: (y, b, 0)), block_spec(count_states, 3 * lanes)],
        [((2, count_states, lanes), BF), ((2, count_states, 128), F32)],
        [block_spec(count_states, lanes), block_spec(count_states, 128)],
        flops=4 * pairs * HEAD_DIM,
        exps=pairs,
        deps=deps,
    )


def add_part(sums, place, part):
    sums[place] = part if place not in sums else sums[place] + part


def backward_tokens(b, blocks, info, tokens, states, logs, grad_mixed, deps=(), long=False):
    lanes = tokens.shape[2] // 3
    heads = lanes // HEAD_DIM
    size = BLOCK // 2
    count_states = states.shape[1]

    def kernel(info_ref, token_ref, state_ref, log_ref, grad_ref, query_ref, own_ref, state_out_ref, *before_ref):
        start, plan, state_masks = attention_plan(
            b, b == blocks - 1, size, info_ref[0], info_ref[1], count_states
        )
        for h in range(heads):
            query, key, value = head_slices(lanes, h)
            sums = ({}, {})
            for j, (tiles, masks) in enumerate(plan):
                rows = [pl.ds(start(*place), size) for place in tiles]
                keys = jnp.concatenate([token_ref[0, at, key] for at in rows] + [state_ref[0, :, key]], axis=0)
                values = jnp.concatenate([token_ref[0, at, value] for at in rows] + [state_ref[0, :, value]], axis=0)
                here = pl.ds(start(0, j), size)
                dq, dk, dv = attend_rows_back(
                    token_ref[0, pl.ds(start(b, j), size), query],
                    keys,
                    values,
                    masks,
                    log_ref[0, here, h : h + 1],
                    grad_ref[0, here, query],
                )
                query_ref[0, here, query] = dq.astype(BF)
                for which, grads in enumerate((dk, dv)):
                    for i, place in enumerate(tiles):
                        add_part(sums[which], place, grads[i * size : (i + 1) * size])
                    add_part(sums[which], "state", grads[len(tiles) * size :])
            for which in range(2):
                columns = slice(which * lanes + h * HEAD_DIM, which * lanes + (h + 1) * HEAD_DIM)
                state_out_ref[0, :, columns] = sums[which]["state"]
                for j in range(2):
                    here = pl.ds(start(0, j), size)
                    own_ref[0, here, columns] = sums[which][(b, j)]
                    if b > 0:
                        before_ref[0][0, here, columns] = sums[which][(b - 1, j)]

    pairs = int(token_pairs(b, heads, count_states))
    outputs = [((2, BLOCK, lanes), BF), ((2, BLOCK, 2 * lanes), F32), ((2, count_states, 2 * lanes), F32)]
    out_specs = [block_spec(BLOCK, lanes), block_spec(BLOCK, 2 * lanes), block_spec(count_states, 2 * lanes)]
    if b > 0:
        outputs.append(((2, BLOCK, 2 * lanes), F32))
        out_specs.append(block_spec(BLOCK, 2 * lanes))
    return call(
        kernel,
        (2,),
        [info, tokens, states, logs, grad_mixed],
        [
            smem(),
            block_spec((b + 1) * BLOCK, 3 * lanes),
            block_spec(count_states, 3 * lanes),
            block_spec(BLOCK, 128),
            pl.BlockSpec((1, BLOCK, lanes), lambda y: (y, b, 0)),
        ],
        outputs,
        out_specs,
        flops=10 * pairs * HEAD_DIM,
        exps=pairs,
        deps=deps,
        long=long,
    )


def backward_states(b, blocks, info, tokens, states, logs, grad_mixed, token_sums, state_sums, deps=(), long=False):
    lanes = tokens.shape[2] // 3
    heads = lanes // HEAD_DIM
    size = BLOCK // 2
    count_states = states.shape[1]
    count = len(token_sums)

    def kernel(info_ref, token_ref, state_ref, log_ref, grad_ref, sum_ref, *rest):
        token_sum_refs, (state_out_ref, token_out_ref) = rest[:count], rest[count:]
        start, plan, state_masks = attention_plan(
            0, b == blocks - 1, size, info_ref[0], info_ref[1], count_states
        )
        for h in range(heads):
            query, key, value = head_slices(lanes, h)
            rows = [pl.ds(start(0, j), size) for j in range(2)]
            keys = jnp.concatenate([state_ref[0, :, key]] + [token_ref[0, at, key] for at in rows], axis=0)
            values = jnp.concatenate([state_ref[0, :, value]] + [token_ref[0, at, value] for at in rows], axis=0)
            sums = [None, None]
            for begin in range(0, count_states, size):
                here = slice(begin, begin + size)
                dq, dk, dv = attend_rows_back(
                    state_ref[0, here, query],
                    keys,
                    values,
                    state_masks,
                    log_ref[0, here, h : h + 1],
                    grad_ref[0, here, query],
                )
                state_out_ref[0, here, query] = dq.astype(BF)
                sums = [part if old is None else old + part for old, part in zip(sums, (dk, dv))]
            for which, to in ((0, key), (1, value)):
                columns = slice(which * lanes + h * HEAD_DIM, which * lanes + (h + 1) * HEAD_DIM)
                state_out_ref[0, :, to] = (sums[which][:count_states] + sum_ref[0, :, columns]).astype(BF)
                for j in range(2):
                    total = sums[which][count_states + j * size : count_states + (j + 1) * size]
                    for ref in token_sum_refs:
                        total = total + ref[0, rows[j], columns]
                    token_out_ref[0, rows[j], columns] = total.astype(BF)

    pairs = 2 * heads * count_states * (count_states + BLOCK)
    return call(
        kernel,
        (2,),
        [info, tokens, states, logs, grad_mixed, state_sums] + list(token_sums),
        [
            smem(),
            pl.BlockSpec((1, BLOCK, 3 * lanes), lambda y: (y, b, 0)),
            block_spec(count_states, 3 * lanes),
            block_spec(count_states, 128),
            block_spec(count_states, lanes),
            block_spec(count_states, 2 * lanes),
        ]
        + [block_spec(BLOCK, 2 * lanes)] * count,
        [((2, count_states, 3 * lanes), BF), ((2, BLOCK, 2 * lanes), BF)],
        [block_spec(count_states, 3 * lanes), block_spec(BLOCK, 2 * lanes)],
        flops=10 * pairs * HEAD_DIM,
        exps=pairs,
        deps=deps,
        long=long,
    )


def body(
    tokens,
    counts,
    token_weights,
    token_output,
    state_weights,
    state_output,
    hidden_up,
    hidden_down,
    norm_gains,
    gate_bias,
    init_state,
    cotangent,
    state_cotangent,
):
    y, c = lax.axis_index("y"), lax.axis_index("c")
    width = tokens.shape[3]
    state_half = init_state.shape[0] // 2
    blocks = 4 * tokens.shape[2] // BLOCK
    valid_count = lax.dynamic_index_in_dim(counts[:, 0], y, 0, keepdims=False)
    if lax.axis_size("r") == 1:
        places, back = width_places(), width_places_back()
        before, after = (lambda array: array), (lambda array: array)
    else:
        places = back = list(range(PIECES))
        before, after = to_local, from_local
    info = jnp.stack([jnp.asarray(v, jnp.int32) for v in [c, valid_count, y] + places + back])

    def micro(array, index):
        return lax.dynamic_index_in_dim(array[:, 0], index, 0, keepdims=False)

    ORDER.last = []
    shard_rows = token_output.shape[0]
    head, ff = token_output.shape[1], hidden_up.shape[1]
    at_state, at_state_out, at_token_out = 0, 3 * head, ff
    flat = lambda array: array.reshape(shard_rows, -1)
    token = Gather(flat(token_weights))
    token_got = swap(micro(tokens, 1 - y), "y")
    small = jnp.concatenate(
        [
            lax.dynamic_slice_in_dim(init_state, c * state_half, state_half, 0),
            norm_gains,
            gate_bias[None],
            jnp.zeros((12, init_state.shape[1]), BF),
        ],
        axis=0,
    )
    if lax.axis_size("r") > 1:
        small = lax.all_gather(small, "r", axis=1, tiled=True)
    small_got = swap_z(small, 2)
    w_token = token.spread(by_x=True)
    mid = Gather(join_columns([flat(state_weights), state_output], ()))
    small = stack_rows(small, small_got)
    small = stack_rows(small, swap_z(small, 1))
    small_got = swap(small, "x")
    x_rows = own_rows(info, before(micro(tokens, y)), before(token_got))
    small = spread_rows(info, small, small_got)
    gains = [small[state_half + i : state_half + i + 1].astype(F32) for i in range(3)]
    gate_open = jax.nn.sigmoid(small[state_half + 3 : state_half + 4].astype(F32))
    state_now = small[:state_half].astype(F32)
    normed = pair(norm_rows(info, x_rows, gains[0], token.low))
    state_norm = pair(norm_rows(info, state_now, gains[1]))
    w_mid = mid.spread(token.low)
    up = Gather(join_columns([hidden_up, token_output], ()))

    token_proj = project(*normed, w_token, 0, 3 * head, 3 * head // 2, blocks=blocks)
    w_up = up.spread(mid.low)
    down = Gather(join_columns([hidden_down], ()))
    dy_got = swap(micro(cotangent, 1 - y), "y")
    grad_final = lax.dynamic_slice(
        state_cotangent, (y, 0, c * state_half, 0), (1, 1, state_half, width)
    )[0, 0]
    grad_final = local_rows(info, before(grad_final))
    grad_update = pair(back_update(info, grad_final, gate_open))
    kept = []
    mixed = []
    for b in range(blocks):
        proj_wait, state_wait, merge_wait, token_wait = (
            (up.ring, [], up.low + [down.got], up.high) if b == 0 else (up.far, [], down.ring, down.low)
        )
        state_proj = project(*state_norm, w_mid, at_state, 3 * head, 3 * head, deps=proj_wait)
        state_flat, state_logs = forward_states(b, blocks, info, token_proj, state_proj, deps=state_wait)
        both = merge([[state_flat]], w_mid, at_state_out, deps=merge_wait)
        mixed_b, logs = forward_tokens(b, blocks, info, token_proj, state_proj, deps=token_wait)
        mixed.append(mixed_b)
        if b < blocks - 1:
            state_next, next_norm, update = step_state(info, state_now, both, gate_open, gains[1])
        else:
            final_rows, update = last_state(info, state_now, both, gate_open)
            state_next, next_norm = None, None
        kept.append((state_now, state_norm, state_proj, logs, state_logs, state_flat, update))
        state_now = state_next
        state_norm = None if next_norm is None else pair(next_norm)
        if b == 0:
            dy_rows = own_rows(info, before(micro(cotangent, y)), before(dy_got))
            dy_pair = pair(dy_rows)
            grad_state_mixed = project(*grad_update, w_mid, at_state_out, head, head)
            w_down = down.spread()
    hidden, hidden_own = add_norm(
        info, x_rows, merge([[part] for part in mixed], w_up, at_token_out, blocks=blocks, deps=down.high), gains[2]
    )
    hidden_norm = pair(hidden_own)
    activated, slope = project(*hidden_norm, w_up, 0, ff, ff // 2, activate=True)

    down_grad = Reduce(outer([([dy_pair], [activated], 1)], ff // 2, split=True))
    grad_up = project(*dy_pair, w_down, 0, ff, ff // 2, gate=slope, long=True)
    both = merge([[grad_up]], w_up, 0, halves=2)
    up_grad = Reduce(outer([([hidden_norm], [grad_up], 1)], ff // 2, split=True))
    down_grad.second()
    grad_hidden, branch, gain_hidden = back_hidden(info, hidden, both, gains[2], dy_rows)
    branch = pair(branch)

    grad_mixed = project(*branch, w_up, at_token_out, head, head, blocks=blocks)
    grad_state = grad_final
    gate_sums, gain_sums = [], []
    query_grads, pair_grads = [None] * blocks, [None] * blocks
    update_all, flat_all, norm_all, state_grads = [], [], [], []
    sums = [None] * blocks

    def tokens_back(b, **how):
        state_proj, logs = kept[b][2], kept[b][3]
        query_grads[b], *sums[b] = backward_tokens(b, blocks, info, token_proj, state_proj, logs, grad_mixed, **how)

    def states_back(b, later, **how):
        state_before, state_norm, state_proj, logs, state_logs, state_flat, update = kept[b]
        own_sums, state_sums, *before_sums = sums[b]
        state_grad, pair_grads[b] = backward_states(
            b, blocks, info, token_proj, state_proj, state_logs, grad_state_mixed, [own_sums] + later, state_sums, **how
        )
        update_all.append(grad_update)
        flat_all.append(state_flat)
        norm_all.append(state_norm)
        state_grads.append(state_grad)
        return merge([[state_grad]], w_mid, at_state, halves=2), before_sums

    def state_step(b, both, grad_state):
        state_before, update = kept[b][0], kept[b][-1]
        grad_state, low, gain_sum, gate_sum = back_state(
            info, grad_state, state_before, update, both, gate_open, gains[1]
        )
        gain_sums.append(gain_sum)
        gate_sums.append(gate_sum)
        return grad_state, low

    last = blocks - 1
    tokens_back(last)
    both, later = states_back(last, [])
    for b in range(last - 1, -1, -1):
        tokens_back(b)
        if b == last - 1:
            up_grad.second()
            down_grad.third()
        grad_state, low = state_step(b + 1, both, grad_state)
        grad_update = pair(low)
        grad_state_mixed = project(*grad_update, w_mid, at_state_out, head, head)
        if b == 0:
            early_grad = Reduce(
                outer(
                    [
                        ([branch], mixed, blocks),
                        ([normed], query_grads, blocks),
                        ([grad_update] + update_all, [kept[0][5]] + flat_all, 1),
                    ],
                    vmem=28,
                    split=True,
                )
            )
        both, later = states_back(b, later, long=b == 0)

    down_grad.fourth()
    token_both = merge([[query_grads[i], pair_grads[i]] for i in range(blocks)], w_token, 0, blocks=blocks, halves=2)
    late_grad = Reduce(outer([([normed], pair_grads, blocks), (norm_all, state_grads, 1)], vmem=28, split=True))
    up_grad.third()
    early_grad.second()
    down_grad.finish()
    grad_state, low = state_step(0, both, grad_state)
    keep, send, gain_token = back_input(info, x_rows, token_both, gains[0], grad_hidden)
    input_keep, input_got = after(keep), swap(after(send), "y")
    near, far = pack_small(info, grad_state, [[gain_token], gain_sums, [gain_hidden], gate_sums])
    far = swap(far, "x")
    up_grad.fourth()
    late_grad.second()
    out_both = merge([[activated]], w_down, 0, halves=2)
    up_grad.finish()
    early_grad.third()
    keep, send = add_out(info, hidden, out_both)
    output_got = swap(after(send), "y")
    output_keep = after(keep)
    final_rows = after(final_rows)
    final_far = swap(final_rows, "y")
    early_grad.fourth()
    late_grad.third()
    near, far = add_small(info, near, far)
    far = swap_z(far, 1)
    early_grad.finish()
    late_grad.fourth()
    near, far = add_small(info, near, far)
    far = swap_z(far, 2)
    near = add_pair(info, near, far)
    if lax.axis_size("r") > 1:
        near = lax.psum_scatter(near, "r", scatter_dimension=1, tiled=True)
    far = swap(near, "y")
    output = place_rows(info, output_keep, output_got)[:, None]
    near = add_pair(info, near, far)
    far = swap(near, "c")
    final_state = place_state(info, final_rows, swap(final_rows, "c"), final_far, swap(final_far, "c"))[:, None]
    init_grad, grad_gains, grad_gate = place_small(info, near, far, state_half)
    input_grad = place_rows(info, input_keep, input_got)[:, None]
    late_grad.finish()
    grad_hidden_down, grad_hidden_up = down_grad.total, up_grad.total
    grad_token_output, grad_query, grad_state_output = [
        early_grad.total[:, i * head : (i + 1) * head] for i in range(3)
    ]
    late = late_grad.total
    grad_token_weights = jnp.stack([grad_query, late[:, :head], late[:, head : 2 * head]], axis=1)
    grad_state_weights = late[:, 2 * head :].reshape(-1, 3, head)
    return (
        output,
        final_state,
        input_grad,
        grad_token_weights,
        grad_token_output,
        grad_state_weights,
        grad_state_output,
        grad_hidden_up,
        grad_hidden_down,
        grad_gains,
        grad_gate[0],
        init_grad,
    )


def solution(mesh):
    dp, heads = mesh.devices.shape
    fine = Mesh(mesh.devices.reshape(dp // (2 * RING), RING, 2, heads // 2, 2), ("r", "z", "x", "y", "c"))
    d, h = ("r", "z", "x"), ("y", "c")
    return jax.shard_map(
        body,
        mesh=fine,
        in_specs=(
            P(None, d, h, None),
            P(None, d),
            P(d, None, h),
            P(d, h),
            P(d, None, h),
            P(d, h),
            P(d, h),
            P(d, h),
            P(None, d),
            P(d),
            P(None, d),
            P(None, d, h, None),
            P(None, d, None, None),
        ),
        out_specs=(
            P(None, d, h, None),
            P(None, d, None, None),
            P(None, d, h, None),
            P(d, None, h),
            P(d, h),
            P(d, None, h),
            P(d, h),
            P(d, h),
            P(d, h),
            P(None, d),
            P(d),
            P(None, d),
        ),
        check_vma=False,
    )
```

```python
import functools

import jax
import jax.numpy as jnp
from jax import lax
from jax.experimental import pallas as pl
from jax.experimental.pallas import tpu as pltpu
from jax.sharding import Mesh
from jax.sharding import PartitionSpec as P

HEAD_DIM = 128
BLOCK = 512
EPSILON = 1e-06
MASKED = -1e30
COST = 0.01
LONG = 1e11
GELU = 0.7978845608028654
RING = 4
BF = jnp.bfloat16
F32 = jnp.float32


def swap(array, axis):
    return lax.ppermute(array, axis, [(0, 1), (1, 0)])


def swap_z(array, bit):
    return lax.ppermute(array, "z", [(i, i ^ bit) for i in range(RING)])


def matmul(left, right, contract):
    return lax.dot_general(
        left, right, (contract, ((), ())), preferred_element_type=jnp.float32
    )


def mm(left, right):
    return matmul(left, right, ((1,), (0,)))


def mm_nt(left, right):
    return matmul(left, right, ((1,), (1,)))


def mm_tn(left, right):
    return matmul(left, right, ((0,), (0,)))


RING_BITS = (0, 2, 1, 3)


def width_places():
    z, x = lax.axis_index("z"), lax.axis_index("x")
    return [jnp.bitwise_xor(z, RING_BITS[k]) * 2 + jnp.bitwise_xor(x, dx) for dx in range(2) for k in range(RING)]


def width_places_back():
    z, x = lax.axis_index("z"), lax.axis_index("x")
    places = []
    for z_to in range(RING):
        apart = jnp.bitwise_xor(z, z_to)
        k = lax.rem(apart, 2) * 2 + lax.div(apart, 2)
        places += [jnp.bitwise_xor(x, x_to) * RING + k for x_to in range(2)]
    return places


def take_pieces(array, places):
    groups = lax.axis_size("r")
    lead, width = array.shape[:-1], array.shape[-1]
    split = array.reshape(lead + (groups, len(places), width // (groups * len(places))))
    axis = len(lead) + 1
    return [lax.dynamic_index_in_dim(split, place, axis, keepdims=False) for place in places]


def to_local(array):
    pieces = take_pieces(array, width_places())
    lead = array.shape[:-1]
    return jnp.concatenate([p.reshape(lead + (-1,)) for p in pieces], axis=-1)


def from_local(array):
    groups = lax.axis_size("r")
    lead, width = array.shape[:-1], array.shape[-1]
    split = array.reshape(lead + (2 * RING, groups, width // (groups * 2 * RING)))
    axis = len(lead)
    pieces = [lax.dynamic_index_in_dim(split, place, axis, keepdims=False) for place in width_places_back()]
    return jnp.stack(pieces, axis=axis + 1).reshape(array.shape)


def gather_groups(array, axis):
    if lax.axis_size("r") == 1:
        return array
    return lax.all_gather(array, "r", axis=axis, tiled=True)


def scatter_groups(array, axis):
    if lax.axis_size("r") == 1:
        return array
    return lax.psum_scatter(array, "r", scatter_dimension=axis, tiled=True)


class Order:
    def __init__(self):
        self.last = []


ORDER = Order()


def call(kernel, grid, inputs, in_specs, outputs, out_specs, flops=0, exps=0, deps=(), vmem=16, long=False, **more):
    block_bytes = sum(a.size * a.dtype.itemsize for a in inputs)
    shapes = [jax.ShapeDtypeStruct(shape, dtype) for shape, dtype in outputs]
    out_bytes = sum(s.size * s.dtype.itemsize for s in shapes)
    given = len(inputs)
    deps = [array for array in list(deps) + ORDER.last if all(array is not other for other in inputs)]

    def run(*refs):
        kernel(*refs[:given], *refs[given + len(deps) :])

    out = pl.pallas_call(
        run,
        grid=grid,
        in_specs=list(in_specs) + [pl.BlockSpec(memory_space=pl.ANY)] * len(deps),
        out_specs=out_specs,
        out_shape=shapes,
        compiler_params=pltpu.CompilerParams(vmem_limit_bytes=vmem * 2**20),
        cost_estimate=pl.CostEstimate(
            flops=int(LONG) if long else int(flops * COST), bytes_accessed=int((block_bytes + out_bytes) * COST), transcendentals=int(exps * COST)
        ),
        **more,
    )(*inputs, *deps)
    ORDER.last = [min(out, key=lambda array: array.size)]
    return out


def whole(array):
    return pl.BlockSpec(array.shape, lambda *_: (0,) * array.ndim)


def whole_out(shape):
    return pl.BlockSpec(shape, lambda *_: (0,) * len(shape))


def stack_rows(first, second, deps=()):
    rows, width = first.shape

    def kernel(first_ref, second_ref, out_ref):
        out_ref[:rows] = first_ref[...]
        out_ref[rows:] = second_ref[...]

    return call(
        kernel,
        (1,),
        [first, second],
        [whole(first)] * 2,
        [((2 * rows, width), BF)],
        [whole_out((2 * rows, width))],
        deps=deps,
    )[0]


def join_columns(arrays, deps):
    rows = arrays[0].shape[0]
    width = sum(array.shape[1] for array in arrays)

    def kernel(*refs):
        place = 0
        for ref in refs[:-1]:
            refs[-1][:, place : place + ref.shape[1]] = ref[...]
            place += ref.shape[1]

    return call(
        kernel,
        (1,),
        arrays,
        [whole(array) for array in arrays],
        [((rows, width), BF)],
        [whole_out((rows, width))],
        deps=deps,
    )[0]


class Gather:
    def __init__(self, shard):
        self.shard = gather_groups(shard, 0)
        self.got = swap_z(self.shard, 2)

    def spread(self, deps=(), by_x=False):
        low = stack_rows(self.shard, self.got, deps)
        low_x, low_y = swap(low, "x"), swap(low, "y")
        high = swap_z(low, 1)
        high_y, high_x = swap(high, "y"), swap(high, "x")
        low_xy = swap(low_y, "x") if by_x else swap(low_x, "y")
        high_xy = swap(high_y, "x")
        self.pieces = [[[low, high], [low_x, high_x]], [[low_y, high_y], [low_xy, high_xy]]]
        self.ring, self.low, self.high, self.far = [high], [low_x, low_y], [high_x, high_y], [low_xy, high_xy]
        return self.pieces


def flat_pieces(pieces):
    return [pieces[y][x][half] for y in range(2) for x in range(2) for half in range(2)]


def spread_rows(info, near, far):
    size = near.shape[1]
    rows = near.shape[0] // RING

    def kernel(near_ref, far_ref, out_ref):
        for k in range(RING):
            out_ref[:, k * size : (k + 1) * size] = near_ref[k * rows : (k + 1) * rows]
            out_ref[:, (RING + k) * size : (RING + k + 1) * size] = far_ref[k * rows : (k + 1) * rows]

    return call(
        kernel,
        (1,),
        [near, far],
        [whole(near), whole(far)],
        [((rows, 2 * RING * size), near.dtype)],
        [whole_out((rows, 2 * RING * size))],
    )[0]


def row_order(own, other, blocks):
    per = own.shape[0] // blocks
    parts = []
    for b in range(blocks):
        parts += [own[b * per : (b + 1) * per], other[b * per : (b + 1) * per]]
    return jnp.concatenate(parts, axis=0)


def project(own, other, pieces, column, width, block, blocks=1, gate=None, activate=False, deps=(), long=False):
    rows = own.shape[0] * 2
    refs = flat_pieces(pieces)
    first = column // block

    def kernel(*args):
        own_ref, other_ref, weights = args[0], args[1], args[2:10]
        left = row_order(own_ref[...], other_ref[...], blocks)
        for y in range(2):
            weight = jnp.concatenate([ref[...] for ref in weights[4 * y : 4 * y + 4]], axis=0)
            total = mm(left, weight)
            if gate is not None:
                gate_ref, out_ref = args[10], args[11]
                low = total.astype(BF).astype(F32)
                out_ref[y] = (low * gate_ref[y].astype(F32)).astype(BF)
            elif activate:
                act_ref, slope_ref = args[10], args[11]
                square = total * total
                curve = jnp.tanh(total * (GELU * 0.044715 * square + GELU))
                share = 0.5 * curve + 0.5
                act = total * share
                act_ref[y] = act.astype(BF)
                slope = share + act * (1.0 - curve) * (GELU * 0.134145 * square + GELU)
                slope_ref[y] = slope.astype(BF)
            else:
                args[10][y] = total.astype(BF)

    spec = pl.BlockSpec((2, rows, block), lambda j: (0, 0, j))
    weight_spec = [pl.BlockSpec((ref.shape[0], block), lambda j: (0, first + j)) for ref in refs]
    extra = [] if gate is None else [gate]
    count = 2 if activate else 1
    out = call(
        kernel,
        (width // block,),
        [own, other] + refs + extra,
        [whole(own), whole(other)] + weight_spec + [spec] * len(extra),
        [((2, rows, width), BF)] * count,
        [spec] * count,
        flops=4 * rows * own.shape[1] * width,
        deps=deps, long=long,
    )
    return out if activate else out[0]


def merge(lefts, pieces, column, blocks=1, deps=(), long=False, halves=1):
    refs = flat_pieces(pieces)
    columns = sum(part.shape[2] for part in lefts[0])
    per = lefts[0][0].shape[1] // 2
    rows = per * len(lefts)
    width = 8 * refs[0].shape[0] // 2
    first = column // columns
    parts_count = len(lefts[0])
    flat = [part for left in lefts for part in left]

    def kernel(*args):
        left_refs, weights = args[: len(flat)], args[len(flat) : len(flat) + 8]
        own_ref, *other_refs = args[len(flat) + 8 :]
        size = rows // halves
        sides = [
            jnp.concatenate([ref[...] for ref in weights[4 * y : 4 * y + 4]], axis=0) for y in range(2)
        ]
        for core in (1, 0):
            total = None
            for y in range(2):
                left = []
                for b in range(len(lefts)):
                    here = left_refs[b * parts_count : (b + 1) * parts_count]
                    left.append(jnp.concatenate([ref[y, core * per : (core + 1) * per] for ref in here], axis=1))
                piece = mm_nt(jnp.concatenate(left, axis=0), sides[y])
                total = piece if total is None else total + piece
            if core:
                for i, ref in enumerate(other_refs):
                    ref[...] = total[i * size : (i + 1) * size].astype(BF)
            else:
                own_ref[...] = total

    weight_spec = [pl.BlockSpec((ref.shape[0], columns), lambda i: (0, first)) for ref in refs]
    return call(
        kernel,
        (1,),
        flat + refs,
        [whole(left) for left in flat] + weight_spec,
        [((rows, width), F32)] + [((rows // halves, width), BF)] * halves,
        [whole_out((rows, width))] + [whole_out((rows // halves, width))] * halves,
        flops=8 * rows * width * columns,
        deps=deps, long=long,
    )


QUARTERS = ((1, 1), (1, 0), (0, 1), (0, 0))


def outer(segments, block=None, vmem=16, deps=(), long=False, split=False):
    width = segments[0][0][0][0].shape[1]
    sizes = [rights[0].shape[2] for lefts, rights, blocks in segments]
    columns = sum(sizes)
    block = columns if block is None else block
    half = width // 2
    inputs, in_specs, flops = [], [], 0
    for lefts, rights, blocks in segments:
        flat = [array for pair_ in lefts for array in pair_]
        inputs += flat + list(rights)
        in_specs += [whole(array) for array in flat]
        wide = min(block, rights[0].shape[2])
        in_specs += [pl.BlockSpec((2, right.shape[1], wide), lambda j: (0, 0, j)) for right in rights]
        flops += 4 * width * rights[0].shape[2] * sum(right.shape[1] for right in rights)

    sizes_out = [half // 2, half, half, half, half // 2] if split else [half] * 4

    def kernel(*args):
        outs = args[len(inputs) :]
        place, column = 0, 0
        for lefts, rights, blocks in segments:
            left_refs = args[place : place + 2 * len(lefts)]
            right_refs = args[place + 2 * len(lefts) : place + 2 * len(lefts) + len(rights)]
            place += 2 * len(lefts) + len(rights)
            left = jnp.concatenate(
                [row_order(left_refs[2 * i][...], left_refs[2 * i + 1][...], blocks) for i in range(len(lefts))], axis=0
            )
            here = slice(column, column + right_refs[0].shape[2])
            column += right_refs[0].shape[2]
            for y in (1, 0):
                right = jnp.concatenate([ref[y] for ref in right_refs], axis=0)
                for x in (1, 0):
                    total = mm_tn(left[:, x * half : (x + 1) * half], right).astype(BF)
                    if split and x and y:
                        outs[0][:, here] = total[: half // 2]
                        outs[-1][:, here] = total[half // 2 :]
                    else:
                        outs[QUARTERS.index((x, y))][:, here] = total

    return call(
        kernel,
        (columns // block,),
        inputs,
        in_specs,
        [((rows, columns), BF) for rows in sizes_out],
        [pl.BlockSpec((rows, block), lambda j: (0, j)) for rows in sizes_out],
        flops=flops,
        vmem=vmem,
        deps=deps, long=long,
    )


def add_low(first, second, deps=(), long=False):
    rows, columns = first.shape
    half = rows // 2

    def kernel(first_ref, second_ref, out_ref):
        out_ref[...] = (first_ref[...].astype(F32) + second_ref[...].astype(F32)).astype(BF)

    spec = pl.BlockSpec((half, columns), lambda i: (i, 0))
    return call(kernel, (2,), [first, second], [spec, spec], [(first.shape, BF)], [spec], deps=deps, long=long)[0]


def add_split(arrays, deps=(), long=False, whole_sum=False):
    rows, columns = arrays[0].shape
    part = rows if whole_sum else rows // 2
    types = (F32,) if whole_sum else (F32, BF)

    def kernel(*refs):
        for half, out_ref in enumerate(refs[len(arrays) :]):
            piece = slice(half * part, (half + 1) * part)
            total = refs[0][piece].astype(F32)
            for ref in refs[1 : len(arrays)]:
                total = total + ref[piece].astype(F32)
            out_ref[...] = total.astype(out_ref.dtype)

    return call(
        kernel,
        (1,),
        arrays,
        [whole(array) for array in arrays],
        [((part, columns), dtype) for dtype in types],
        [whole_out((part, columns))] * len(types),
        deps=deps, long=long,
    )


def add_into(array, piece, half, deps=()):
    rows, columns = piece.shape

    def kernel(array_ref, piece_ref, out_ref):
        out_ref[...] = (array_ref[...].astype(F32) + piece_ref[...].astype(F32)).astype(BF)

    here, there = pl.BlockSpec((rows, columns), lambda i: (half, 0)), pl.BlockSpec((rows, columns), lambda i: (0, 0))
    return call(
        kernel,
        (1,),
        [array, piece],
        [here, there],
        [(array.shape, BF)],
        [here],
        input_output_aliases={0: 0},
        deps=deps,
    )[0]


class Reduce:
    def __init__(self, quarters, first_axis=None):
        self.first_axis = first_axis
        if first_axis is None:
            low11, self.out10, self.out01, self.out00, high11 = quarters
            self.first = [swap(low11, "y"), swap(high11, "x")]
        else:
            out11, self.out10, self.out01, self.out00 = quarters
            self.first = [swap(out11, first_axis)]

    def second(self, deps=(), long=False):
        if self.first_axis is None:
            self.out10 = add_into(self.out10, self.first[0], 0, deps)
            self.out01 = add_into(self.out01, self.first[1], 1, deps)
        elif self.first_axis == "x":
            self.out01 = add_low(self.out01, self.first[0], deps, long)
        else:
            self.out10 = add_low(self.out10, self.first[0], deps, long)
        self.next = [swap(self.out10, "x"), swap(self.out01, "y")]

    def third(self, deps=(), long=False):
        self.near, far = add_split([self.out00] + self.next, deps, long)
        self.got = swap_z(far, 1)

    def fourth(self, deps=(), long=False):
        self.near, far = add_split([self.near, self.got], deps, long)
        self.got = swap_z(far, 2)

    def finish(self, **how):
        self.total = scatter_groups(add_split([self.near, self.got], whole_sum=True, **how)[0], 0)


def pair(own):
    return own, swap(own, "c")


INFO = 3
PIECES = 2 * RING
SMALL = 16


def smem():
    return pl.BlockSpec(memory_space=pltpu.SMEM)


def lanes_at(info_ref, index, width):
    size = width // PIECES
    return pl.ds(pl.multiple_of(info_ref[index] * size, size), size)


def reorder_in(info_ref, source, target, rows=slice(None)):
    width = source.shape[-1]
    size = width // PIECES
    for k in range(PIECES):
        target[rows, k * size : (k + 1) * size] = source[:, lanes_at(info_ref, INFO + k, width)].astype(target.dtype)


def reorder_out(info_ref, source, target, rows=slice(None)):
    width = source.shape[-1]
    size = width // PIECES
    for k in range(PIECES):
        part = source[rows, lanes_at(info_ref, INFO + PIECES + k, width)]
        target[:, k * size : (k + 1) * size] = part.astype(target.dtype)


def swap_all(arrays):
    return [swap(array, "c") for array in arrays]


def both_cores(own_ref, *got_refs):
    return own_ref[...] + jnp.concatenate([ref[...] for ref in got_refs], axis=0).astype(F32)


def inverse_rms(values):
    return lax.rsqrt(jnp.mean(values * values, axis=-1, keepdims=True) + EPSILON)


def rms_back(values, gain, grad):
    inverse = inverse_rms(values)
    scaled = values * inverse
    weighted = grad * gain
    back = inverse * (weighted - scaled * jnp.mean(scaled * weighted, axis=-1, keepdims=True))
    return back, jnp.sum(grad * scaled, axis=0, keepdims=True)


def rowwise(kernel, inputs, outputs, scratch=(), deps=(), long=False):
    return call(
        kernel,
        (1,),
        inputs,
        [smem()] + [whole(array) for array in inputs[1:]],
        outputs,
        [whole_out(shape) for shape, _ in outputs],
        scratch_shapes=[pltpu.VMEM(shape, dtype) for shape, dtype in scratch],
        deps=deps, long=long,
    )


def own_rows(info, keep, got):
    rows, width = keep.shape

    def kernel(info_ref, keep_ref, got_ref, out_ref):
        y = info_ref[2]
        reorder_in(info_ref, keep_ref, out_ref, pl.ds(pl.multiple_of(y * rows, rows), rows))
        reorder_in(info_ref, got_ref, out_ref, pl.ds(pl.multiple_of((1 - y) * rows, rows), rows))

    return rowwise(kernel, [info, keep, got], [((2 * rows, width), BF)])[0]


def local_rows(info, array):
    def kernel(info_ref, in_ref, out_ref):
        reorder_in(info_ref, in_ref, out_ref)

    return rowwise(kernel, [info, array], [(array.shape, array.dtype)])[0]


def norm_rows(info, values, gain, deps=()):
    def kernel(info_ref, in_ref, gain_ref, out_ref):
        rows = in_ref[...].astype(F32)
        out_ref[...] = (rows * inverse_rms(rows) * gain_ref[...]).astype(BF)

    return rowwise(kernel, [info, values, gain], [(values.shape, BF)], deps=deps)[0]


def add_norm(info, rows, both, gain):
    own, *others = both

    def kernel(info_ref, row_ref, own_ref, got_ref, gain_ref, hidden_ref, norm_ref):
        hidden = row_ref[...].astype(F32) + (own_ref[...] + got_ref[...].astype(F32))
        hidden_ref[...] = hidden
        norm_ref[...] = (hidden * inverse_rms(hidden) * gain_ref[...]).astype(BF)

    return rowwise(kernel, [info, rows, own, *swap_all(others), gain], [(rows.shape, F32), (rows.shape, BF)])


def add_out(info, hidden, both):
    own, *others = both
    rows, width = hidden.shape
    half = rows // 2

    def kernel(info_ref, hidden_ref, own_ref, low_ref, high_ref, keep_ref, send_ref, scratch):
        y = info_ref[2]
        scratch[...] = hidden_ref[...] + (both_cores(own_ref, low_ref, high_ref))
        reorder_out(info_ref, scratch, keep_ref, pl.ds(pl.multiple_of(y * half, half), half))
        reorder_out(info_ref, scratch, send_ref, pl.ds(pl.multiple_of((1 - y) * half, half), half))

    return rowwise(
        kernel,
        [info, hidden, own, *swap_all(others)],
        [((half, width), BF)] * 2,
        [((rows, width), F32)],
    )


def step_state(info, state, both, gate, gain):
    own, *others = both

    def kernel(info_ref, state_ref, own_ref, got_ref, gate_ref, gain_ref, next_ref, norm_ref, update_ref):
        update = own_ref[...] + got_ref[...].astype(F32)
        update_ref[...] = update
        after = gate_ref[...] * state_ref[...] + (1.0 - gate_ref[...]) * update
        next_ref[...] = after
        norm_ref[...] = (after * inverse_rms(after) * gain_ref[...]).astype(BF)

    return rowwise(
        kernel,
        [info, state, own, *swap_all(others), gate, gain],
        [(state.shape, F32), (state.shape, BF), (state.shape, F32)],
    )


def last_state(info, state, both, gate):
    own, *others = both

    def kernel(info_ref, state_ref, own_ref, got_ref, gate_ref, final_ref, update_ref, scratch):
        update = own_ref[...] + got_ref[...].astype(F32)
        update_ref[...] = update
        scratch[...] = gate_ref[...] * state_ref[...] + (1.0 - gate_ref[...]) * update
        reorder_out(info_ref, scratch, final_ref)

    return rowwise(
        kernel,
        [info, state, own, *swap_all(others), gate],
        [(state.shape, BF), (state.shape, F32)],
        [(state.shape, F32)],
    )


def back_hidden(info, hidden, both, gain, dy):
    own, *others = both

    def kernel(info_ref, hidden_ref, own_ref, low_ref, high_ref, gain_ref, dy_ref, grad_ref, branch_ref, gain_grad_ref):
        grad = both_cores(own_ref, low_ref, high_ref)
        back, gain_grad_ref[...] = rms_back(hidden_ref[...], gain_ref[...], grad)
        total = dy_ref[...].astype(F32) + back
        grad_ref[...] = total
        branch_ref[...] = total.astype(BF)

    return rowwise(
        kernel,
        [info, hidden, own, *swap_all(others), gain, dy],
        [(hidden.shape, F32), (hidden.shape, BF), ((1, hidden.shape[1]), F32)],
    )


def back_update(info, grad, gate):
    def kernel(info_ref, grad_ref, gate_ref, out_ref):
        out_ref[...] = ((1.0 - gate_ref[...]) * grad_ref[...].astype(F32)).astype(BF)

    return rowwise(kernel, [info, grad, gate], [(grad.shape, BF)])[0]


def back_state(info, grad, state, update, both, gate, gain):
    own, *others = both
    width = state.shape[1]

    def kernel(
        info_ref, grad_ref, state_ref, update_ref, own_ref, *refs
    ):
        got_refs = refs[: len(others)]
        gate_ref, gain_ref, out_ref, next_ref, gain_grad_ref, gate_grad_ref = refs[len(others) :]
        gate_open = gate_ref[...]
        grad_now = grad_ref[...].astype(F32)
        values = state_ref[...]
        gate_grad_ref[...] = jnp.sum(grad_now * (values - update_ref[...]), axis=0, keepdims=True) * (
            gate_open * (1.0 - gate_open)
        )
        back, gain_grad_ref[...] = rms_back(values, gain_ref[...], both_cores(own_ref, *got_refs))
        total = gate_open * grad_now + back
        out_ref[...] = total
        next_ref[...] = ((1.0 - gate_open) * total).astype(BF)

    return rowwise(
        kernel,
        [info, grad, state, update, own, *swap_all(others), gate, gain],
        [(state.shape, F32), (state.shape, BF), ((1, width), F32), ((1, width), F32)],
    )


def back_input(info, values, both, gain, grad_hidden):
    own, *others = both
    rows, width = values.shape
    half = rows // 2

    def kernel(info_ref, value_ref, own_ref, low_ref, high_ref, gain_ref, grad_ref, keep_ref, send_ref, gain_grad_ref, scratch):
        y = info_ref[2]
        grad = both_cores(own_ref, low_ref, high_ref)
        back, gain_grad_ref[...] = rms_back(value_ref[...].astype(F32), gain_ref[...], grad)
        scratch[...] = grad_ref[...] + back
        reorder_out(info_ref, scratch, keep_ref, pl.ds(pl.multiple_of(y * half, half), half))
        reorder_out(info_ref, scratch, send_ref, pl.ds(pl.multiple_of((1 - y) * half, half), half))

    return rowwise(
        kernel,
        [info, values, own, *swap_all(others), gain, grad_hidden],
        [((half, width), F32), ((half, width), BF), ((1, width), F32)],
        [((rows, width), F32)],
    )


def pack_small(info, states, vectors):
    rows, width = states.shape
    half = width // 2
    counts = [len(group) for group in vectors]
    flat = [vector for group in vectors for vector in group]
    pad = SMALL - len(vectors)

    def kernel(info_ref, state_ref, *refs):
        near_ref, far_ref = refs[len(flat) :]
        parts, place = [], 0
        for count in counts:
            parts.append(sum(ref[...] for ref in refs[place : place + count]))
            place += count
        tail = jnp.concatenate(parts + [jnp.zeros((pad, width), F32)], axis=0)
        quarter = half // 2
        for source, here in ((state_ref[...], slice(0, rows)), (tail, slice(rows, rows + SMALL))):
            for x in range(2):
                to = slice(x * quarter, (x + 1) * quarter)
                near_ref[here, to] = source[:, 2 * x * quarter : (2 * x + 1) * quarter]
                far_ref[here, to] = source[:, (2 * x + 1) * quarter : (2 * x + 2) * quarter].astype(BF)

    shape = (rows + SMALL, half)
    return rowwise(kernel, [info, states] + flat, [(shape, F32), (shape, BF)])


def add_small(info, near, got, groups=1):
    rows, width = near.shape
    half = width // 2

    def kernel(info_ref, near_ref, got_ref, near_out, far_out):
        total = near_ref[...] + got_ref[...].astype(F32)
        size = half // groups
        for g in range(groups):
            to = slice(g * size, (g + 1) * size)
            near_out[:, to] = total[:, 2 * g * size : (2 * g + 1) * size]
            far_out[:, to] = total[:, (2 * g + 1) * size : (2 * g + 2) * size].astype(BF)

    return rowwise(kernel, [info, near, got], [((rows, half), F32), ((rows, half), BF)])


def add_pair(info, near, got):
    def kernel(info_ref, near_ref, got_ref, out_ref):
        out_ref[...] = near_ref[...] + got_ref[...].astype(F32)

    return rowwise(kernel, [info, near, got], [(near.shape, F32)])[0]


def place_small(info, near, far, states):
    size = near.shape[1]

    def kernel(info_ref, near_ref, far_ref, state_ref, gain_ref, gate_ref):
        c = info_ref[0]
        state_ref[pl.ds(pl.multiple_of(c * states, states), states)] = near_ref[:states]
        state_ref[pl.ds(pl.multiple_of((1 - c) * states, states), states)] = far_ref[:states]
        total = near_ref[states:] + far_ref[states:]
        gain_ref[...] = total[:3]
        gate_ref[...] = total[3:4]

    return rowwise(kernel, [info, near, far], [((2 * states, size), F32), ((3, size), F32), ((1, size), F32)])


def place_rows(info, keep, got):
    shape = (2,) + keep.shape

    def kernel(info_ref, keep_ref, got_ref, out_ref):
        y = info_ref[2]
        out_ref[y] = keep_ref[...]
        out_ref[1 - y] = got_ref[...].astype(keep.dtype)

    return rowwise(kernel, [info, keep, got], [(shape, keep.dtype)])[0]


def place_state(info, near, near_c, far, far_c):
    rows, width = near.shape

    def kernel(info_ref, near_ref, near_c_ref, far_ref, far_c_ref, out_ref):
        c, y = info_ref[0], info_ref[2]
        here = pl.ds(pl.multiple_of(c * rows, rows), rows)
        there = pl.ds(pl.multiple_of((1 - c) * rows, rows), rows)
        out_ref[y, here] = near_ref[...]
        out_ref[y, there] = near_c_ref[...]
        out_ref[1 - y, here] = far_ref[...]
        out_ref[1 - y, there] = far_c_ref[...]

    return rowwise(kernel, [info, near, near_c, far, far_c], [((2, 2 * rows, width), near.dtype)])[0]


SCALE = HEAD_DIM ** (-0.5)


def key_tiles(b, j):
    tiles = []
    if b > 0:
        tiles += [(b - 1, jj, "after" if jj == j else "all") for jj in range(j, 2)]
    tiles += [(b, jj, "until" if jj == j else "all") for jj in range(j + 1)]
    return tiles


def tile_mask(kind, size, limit):
    rows = lax.broadcasted_iota(jnp.int32, (size, size), 0)
    columns = lax.broadcasted_iota(jnp.int32, (size, size), 1)
    mask = None
    if kind == "after":
        mask = columns > rows
    if kind == "until":
        mask = columns <= rows
    if limit is not None:
        inside = columns < limit
        mask = inside if mask is None else mask & inside
    return mask


def masked_scores(queries, keys, masks):
    scores = mm_nt(queries, keys) * SCALE
    parts, place = [], 0
    for size, mask in masks:
        part = scores[:, place : place + size]
        parts.append(part if mask is None else jnp.where(mask, part, MASKED))
        place += size
    return jnp.concatenate(parts, axis=1)


def attention_plan(b, last, size, core, count, states):
    def start(block, j):
        return pl.multiple_of(block * 2 * size + jnp.bitwise_xor(core, j) * size, size)

    plan = []
    for j in range(2):
        tiles, masks = [], []
        for block, jj, kind in key_tiles(b, j):
            limit = count - jj * size if block == b and last else None
            tiles.append((block, jj))
            masks.append((size, tile_mask(kind, size, limit)))
        plan.append((tiles, masks + [(states, None)]))
    state_masks = [(states, None)]
    for jj in range(2):
        state_masks.append((size, tile_mask("all", size, count - jj * size if last else None)))
    return start, plan, state_masks


def block_spec(rows, width):
    return pl.BlockSpec((1, rows, width), lambda y: (y, 0, 0))


def head_slices(lanes, h):
    return [slice(p * lanes + h * HEAD_DIM, p * lanes + (h + 1) * HEAD_DIM) for p in range(3)]


def attend_rows(queries, keys, values, masks):
    scores = masked_scores(queries, keys, masks)
    top = jnp.max(scores, axis=1, keepdims=True)
    weights = jnp.exp(scores - top)
    total = jnp.sum(weights, axis=1, keepdims=True)
    mixed = mm(weights.astype(BF), values) / total
    return mixed.astype(BF), top + jnp.log(total)


def attend_rows_back(queries, keys, values, masks, log_total, grad):
    scores = masked_scores(queries, keys, masks)
    probs = jnp.exp(scores - log_total)
    grad_probs = mm_nt(grad, values)
    row_sum = jnp.sum(grad_probs * probs, axis=1, keepdims=True)
    low = (probs * (grad_probs - row_sum)).astype(BF)
    return mm(low, keys) * SCALE, mm_tn(low, queries) * SCALE, mm_tn(probs.astype(BF), grad)


def token_pairs(b, heads, states):
    return 2 * heads * BLOCK * (BLOCK * (1.25 if b else 0.75) + states)


def forward_tokens(b, blocks, info, tokens, states, deps=()):
    lanes = tokens.shape[2] // 3
    heads = lanes // HEAD_DIM
    size = BLOCK // 2
    count_states = states.shape[1]

    def kernel(info_ref, token_ref, state_ref, mixed_ref, log_ref):
        start, plan, state_masks = attention_plan(
            b, b == blocks - 1, size, info_ref[0], info_ref[1], count_states
        )
        for h in range(heads):
            query, key, value = head_slices(lanes, h)
            for j, (tiles, masks) in enumerate(plan):
                rows = [pl.ds(start(*place), size) for place in tiles]
                keys = jnp.concatenate([token_ref[0, at, key] for at in rows] + [state_ref[0, :, key]], axis=0)
                values = jnp.concatenate([token_ref[0, at, value] for at in rows] + [state_ref[0, :, value]], axis=0)
                here = pl.ds(start(0, j), size)
                mixed_ref[0, here, query], log_ref[0, here, h : h + 1] = attend_rows(
                    token_ref[0, pl.ds(start(b, j), size), query], keys, values, masks
                )

    pairs = int(token_pairs(b, heads, count_states))
    return call(
        kernel,
        (2,),
        [info, tokens, states],
        [smem(), block_spec((b + 1) * BLOCK, 3 * lanes), block_spec(count_states, 3 * lanes)],
        [((2, BLOCK, lanes), BF), ((2, BLOCK, 128), F32)],
        [block_spec(BLOCK, lanes), block_spec(BLOCK, 128)],
        flops=4 * pairs * HEAD_DIM,
        exps=pairs,
        deps=deps,
    )


def forward_states(b, blocks, info, tokens, states, deps=()):
    lanes = tokens.shape[2] // 3
    heads = lanes // HEAD_DIM
    size = BLOCK // 2
    count_states = states.shape[1]

    def kernel(info_ref, token_ref, state_ref, mixed_ref, log_ref):
        start, plan, state_masks = attention_plan(
            0, b == blocks - 1, size, info_ref[0], info_ref[1], count_states
        )
        for h in range(heads):
            query, key, value = head_slices(lanes, h)
            rows = [pl.ds(start(0, j), size) for j in range(2)]
            keys = jnp.concatenate([state_ref[0, :, key]] + [token_ref[0, at, key] for at in rows], axis=0)
            values = jnp.concatenate([state_ref[0, :, value]] + [token_ref[0, at, value] for at in rows], axis=0)
            for begin in range(0, count_states, size):
                here = slice(begin, begin + size)
                mixed_ref[0, here, query], log_ref[0, here, h : h + 1] = attend_rows(
                    state_ref[0, here, query], keys, values, state_masks
                )

    pairs = 2 * heads * count_states * (count_states + BLOCK)
    return call(
        kernel,
        (2,),
        [info, tokens, states],
        [smem(), pl.BlockSpec((1, BLOCK, 3 * lanes), lambda y: (y, b, 0)), block_spec(count_states, 3 * lanes)],
        [((2, count_states, lanes), BF), ((2, count_states, 128), F32)],
        [block_spec(count_states, lanes), block_spec(count_states, 128)],
        flops=4 * pairs * HEAD_DIM,
        exps=pairs,
        deps=deps,
    )


def add_part(sums, place, part):
    sums[place] = part if place not in sums else sums[place] + part


def backward_tokens(b, blocks, info, tokens, states, logs, grad_mixed, deps=(), long=False):
    lanes = tokens.shape[2] // 3
    heads = lanes // HEAD_DIM
    size = BLOCK // 2
    count_states = states.shape[1]

    def kernel(info_ref, token_ref, state_ref, log_ref, grad_ref, query_ref, own_ref, state_out_ref, *before_ref):
        start, plan, state_masks = attention_plan(
            b, b == blocks - 1, size, info_ref[0], info_ref[1], count_states
        )
        for h in range(heads):
            query, key, value = head_slices(lanes, h)
            sums = ({}, {})
            for j, (tiles, masks) in enumerate(plan):
                rows = [pl.ds(start(*place), size) for place in tiles]
                keys = jnp.concatenate([token_ref[0, at, key] for at in rows] + [state_ref[0, :, key]], axis=0)
                values = jnp.concatenate([token_ref[0, at, value] for at in rows] + [state_ref[0, :, value]], axis=0)
                here = pl.ds(start(0, j), size)
                dq, dk, dv = attend_rows_back(
                    token_ref[0, pl.ds(start(b, j), size), query],
                    keys,
                    values,
                    masks,
                    log_ref[0, here, h : h + 1],
                    grad_ref[0, here, query],
                )
                query_ref[0, here, query] = dq.astype(BF)
                for which, grads in enumerate((dk, dv)):
                    for i, place in enumerate(tiles):
                        add_part(sums[which], place, grads[i * size : (i + 1) * size])
                    add_part(sums[which], "state", grads[len(tiles) * size :])
            for which in range(2):
                columns = slice(which * lanes + h * HEAD_DIM, which * lanes + (h + 1) * HEAD_DIM)
                state_out_ref[0, :, columns] = sums[which]["state"]
                for j in range(2):
                    here = pl.ds(start(0, j), size)
                    own_ref[0, here, columns] = sums[which][(b, j)]
                    if b > 0:
                        before_ref[0][0, here, columns] = sums[which][(b - 1, j)]

    pairs = int(token_pairs(b, heads, count_states))
    outputs = [((2, BLOCK, lanes), BF), ((2, BLOCK, 2 * lanes), F32), ((2, count_states, 2 * lanes), F32)]
    out_specs = [block_spec(BLOCK, lanes), block_spec(BLOCK, 2 * lanes), block_spec(count_states, 2 * lanes)]
    if b > 0:
        outputs.append(((2, BLOCK, 2 * lanes), F32))
        out_specs.append(block_spec(BLOCK, 2 * lanes))
    return call(
        kernel,
        (2,),
        [info, tokens, states, logs, grad_mixed],
        [
            smem(),
            block_spec((b + 1) * BLOCK, 3 * lanes),
            block_spec(count_states, 3 * lanes),
            block_spec(BLOCK, 128),
            pl.BlockSpec((1, BLOCK, lanes), lambda y: (y, b, 0)),
        ],
        outputs,
        out_specs,
        flops=10 * pairs * HEAD_DIM,
        exps=pairs,
        deps=deps,
        long=long,
    )


def backward_states(b, blocks, info, tokens, states, logs, grad_mixed, token_sums, state_sums, deps=(), long=False):
    lanes = tokens.shape[2] // 3
    heads = lanes // HEAD_DIM
    size = BLOCK // 2
    count_states = states.shape[1]
    count = len(token_sums)

    def kernel(info_ref, token_ref, state_ref, log_ref, grad_ref, sum_ref, *rest):
        token_sum_refs, (state_out_ref, token_out_ref) = rest[:count], rest[count:]
        start, plan, state_masks = attention_plan(
            0, b == blocks - 1, size, info_ref[0], info_ref[1], count_states
        )
        for h in range(heads):
            query, key, value = head_slices(lanes, h)
            rows = [pl.ds(start(0, j), size) for j in range(2)]
            keys = jnp.concatenate([state_ref[0, :, key]] + [token_ref[0, at, key] for at in rows], axis=0)
            values = jnp.concatenate([state_ref[0, :, value]] + [token_ref[0, at, value] for at in rows], axis=0)
            sums = [None, None]
            for begin in range(0, count_states, size):
                here = slice(begin, begin + size)
                dq, dk, dv = attend_rows_back(
                    state_ref[0, here, query],
                    keys,
                    values,
                    state_masks,
                    log_ref[0, here, h : h + 1],
                    grad_ref[0, here, query],
                )
                state_out_ref[0, here, query] = dq.astype(BF)
                sums = [part if old is None else old + part for old, part in zip(sums, (dk, dv))]
            for which, to in ((0, key), (1, value)):
                columns = slice(which * lanes + h * HEAD_DIM, which * lanes + (h + 1) * HEAD_DIM)
                state_out_ref[0, :, to] = (sums[which][:count_states] + sum_ref[0, :, columns]).astype(BF)
                for j in range(2):
                    total = sums[which][count_states + j * size : count_states + (j + 1) * size]
                    for ref in token_sum_refs:
                        total = total + ref[0, rows[j], columns]
                    token_out_ref[0, rows[j], columns] = total.astype(BF)

    pairs = 2 * heads * count_states * (count_states + BLOCK)
    return call(
        kernel,
        (2,),
        [info, tokens, states, logs, grad_mixed, state_sums] + list(token_sums),
        [
            smem(),
            pl.BlockSpec((1, BLOCK, 3 * lanes), lambda y: (y, b, 0)),
            block_spec(count_states, 3 * lanes),
            block_spec(count_states, 128),
            block_spec(count_states, lanes),
            block_spec(count_states, 2 * lanes),
        ]
        + [block_spec(BLOCK, 2 * lanes)] * count,
        [((2, count_states, 3 * lanes), BF), ((2, BLOCK, 2 * lanes), BF)],
        [block_spec(count_states, 3 * lanes), block_spec(BLOCK, 2 * lanes)],
        flops=10 * pairs * HEAD_DIM,
        exps=pairs,
        deps=deps,
        long=long,
    )


def body(
    tokens,
    counts,
    token_weights,
    token_output,
    state_weights,
    state_output,
    hidden_up,
    hidden_down,
    norm_gains,
    gate_bias,
    init_state,
    cotangent,
    state_cotangent,
):
    y, c = lax.axis_index("y"), lax.axis_index("c")
    width = tokens.shape[3]
    state_half = init_state.shape[0] // 2
    blocks = 4 * tokens.shape[2] // BLOCK
    valid_count = lax.dynamic_index_in_dim(counts[:, 0], y, 0, keepdims=False)
    if lax.axis_size("r") == 1:
        places, back = width_places(), width_places_back()
        before, after = (lambda array: array), (lambda array: array)
    else:
        places = back = list(range(PIECES))
        before, after = to_local, from_local
    info = jnp.stack([jnp.asarray(v, jnp.int32) for v in [c, valid_count, y] + places + back])

    def micro(array, index):
        return lax.dynamic_index_in_dim(array[:, 0], index, 0, keepdims=False)

    ORDER.last = []
    shard_rows = token_output.shape[0]
    head, ff = token_output.shape[1], hidden_up.shape[1]
    at_state, at_state_out, at_token_out = 0, 3 * head, ff
    flat = lambda array: array.reshape(shard_rows, -1)
    token = Gather(flat(token_weights))
    token_got = swap(micro(tokens, 1 - y), "y")
    small = jnp.concatenate(
        [
            lax.dynamic_slice_in_dim(init_state, c * state_half, state_half, 0),
            norm_gains,
            gate_bias[None],
            jnp.zeros((12, init_state.shape[1]), BF),
        ],
        axis=0,
    )
    if lax.axis_size("r") > 1:
        small = lax.all_gather(small, "r", axis=1, tiled=True)
    small_got = swap_z(small, 2)
    w_token = token.spread(by_x=True)
    mid = Gather(join_columns([flat(state_weights), state_output], ()))
    small = stack_rows(small, small_got)
    small = stack_rows(small, swap_z(small, 1))
    small_got = swap(small, "x")
    x_rows = own_rows(info, before(micro(tokens, y)), before(token_got))
    small = spread_rows(info, small, small_got)
    gains = [small[state_half + i : state_half + i + 1].astype(F32) for i in range(3)]
    gate_open = jax.nn.sigmoid(small[state_half + 3 : state_half + 4].astype(F32))
    state_now = small[:state_half].astype(F32)
    normed = pair(norm_rows(info, x_rows, gains[0], token.low))
    state_norm = pair(norm_rows(info, state_now, gains[1]))
    w_mid = mid.spread(token.low)
    up = Gather(join_columns([hidden_up, token_output], ()))

    token_proj = project(*normed, w_token, 0, 3 * head, 3 * head // 2, blocks=blocks)
    w_up = up.spread(mid.low)
    down = Gather(join_columns([hidden_down], ()))
    dy_got = swap(micro(cotangent, 1 - y), "y")
    grad_final = lax.dynamic_slice(
        state_cotangent, (y, 0, c * state_half, 0), (1, 1, state_half, width)
    )[0, 0]
    grad_final = local_rows(info, before(grad_final))
    grad_update = pair(back_update(info, grad_final, gate_open))
    kept = []
    mixed = []
    for b in range(blocks):
        proj_wait, state_wait, merge_wait, token_wait = (
            (up.ring, [], up.low + [down.got], up.high) if b == 0 else (up.far, [], down.ring, down.low)
        )
        state_proj = project(*state_norm, w_mid, at_state, 3 * head, 3 * head, deps=proj_wait)
        state_flat, state_logs = forward_states(b, blocks, info, token_proj, state_proj, deps=state_wait)
        both = merge([[state_flat]], w_mid, at_state_out, deps=merge_wait)
        mixed_b, logs = forward_tokens(b, blocks, info, token_proj, state_proj, deps=token_wait)
        mixed.append(mixed_b)
        if b < blocks - 1:
            state_next, next_norm, update = step_state(info, state_now, both, gate_open, gains[1])
        else:
            final_rows, update = last_state(info, state_now, both, gate_open)
            state_next, next_norm = None, None
        kept.append((state_now, state_norm, state_proj, logs, state_logs, state_flat, update))
        state_now = state_next
        state_norm = None if next_norm is None else pair(next_norm)
        if b == 0:
            dy_rows = own_rows(info, before(micro(cotangent, y)), before(dy_got))
            dy_pair = pair(dy_rows)
            grad_state_mixed = project(*grad_update, w_mid, at_state_out, head, head)
            w_down = down.spread()
    hidden, hidden_own = add_norm(
        info, x_rows, merge([[part] for part in mixed], w_up, at_token_out, blocks=blocks, deps=down.high), gains[2]
    )
    hidden_norm = pair(hidden_own)
    activated, slope = project(*hidden_norm, w_up, 0, ff, ff // 2, activate=True)

    down_grad = Reduce(outer([([dy_pair], [activated], 1)], ff // 2, split=True))
    grad_up = project(*dy_pair, w_down, 0, ff, ff // 2, gate=slope, long=True)
    both = merge([[grad_up]], w_up, 0, halves=2)
    up_grad = Reduce(outer([([hidden_norm], [grad_up], 1)], ff // 2, split=True))
    down_grad.second()
    grad_hidden, branch, gain_hidden = back_hidden(info, hidden, both, gains[2], dy_rows)
    branch = pair(branch)

    grad_mixed = project(*branch, w_up, at_token_out, head, head, blocks=blocks)
    grad_state = grad_final
    gate_sums, gain_sums = [], []
    query_grads, pair_grads = [None] * blocks, [None] * blocks
    update_all, flat_all, norm_all, state_grads = [], [], [], []
    sums = [None] * blocks

    def tokens_back(b, **how):
        state_proj, logs = kept[b][2], kept[b][3]
        query_grads[b], *sums[b] = backward_tokens(b, blocks, info, token_proj, state_proj, logs, grad_mixed, **how)

    def states_back(b, later, **how):
        state_before, state_norm, state_proj, logs, state_logs, state_flat, update = kept[b]
        own_sums, state_sums, *before_sums = sums[b]
        state_grad, pair_grads[b] = backward_states(
            b, blocks, info, token_proj, state_proj, state_logs, grad_state_mixed, [own_sums] + later, state_sums, **how
        )
        update_all.append(grad_update)
        flat_all.append(state_flat)
        norm_all.append(state_norm)
        state_grads.append(state_grad)
        return merge([[state_grad]], w_mid, at_state, halves=1 if b else 2), before_sums

    def state_step(b, both, grad_state):
        state_before, update = kept[b][0], kept[b][-1]
        grad_state, low, gain_sum, gate_sum = back_state(
            info, grad_state, state_before, update, both, gate_open, gains[1]
        )
        gain_sums.append(gain_sum)
        gate_sums.append(gate_sum)
        return grad_state, low

    last = blocks - 1
    tokens_back(last)
    both, later = states_back(last, [])
    for b in range(last - 1, -1, -1):
        tokens_back(b)
        if b == last - 1:
            up_grad.second()
            down_grad.third()
        grad_state, low = state_step(b + 1, both, grad_state)
        grad_update = pair(low)
        grad_state_mixed = project(*grad_update, w_mid, at_state_out, head, head)
        if b == 0:
            early_grad = Reduce(
                outer(
                    [
                        ([branch], mixed, blocks),
                        ([normed], query_grads, blocks),
                        ([grad_update] + update_all, [kept[0][5]] + flat_all, 1),
                    ],
                    vmem=28,
                    split=True,
                )
            )
        both, later = states_back(b, later, long=b == 0)

    down_grad.fourth()
    early_grad.second()
    token_both = merge(
        [[query_grads[i], pair_grads[i]] for i in range(blocks)], w_token, 0, blocks=blocks, halves=2
    )
    grad_state, low = state_step(0, both, grad_state)
    late_grad = Reduce(outer([([normed], pair_grads, blocks), (norm_all, state_grads, 1)], vmem=28, split=True))
    keep, send, gain_token = back_input(info, x_rows, token_both, gains[0], grad_hidden)
    input_keep, input_got = after(keep), swap(after(send), "y")
    near, far = pack_small(info, grad_state, [[gain_token], gain_sums, [gain_hidden], gate_sums])
    far = swap_z(far, 1)
    up_grad.third()
    down_grad.finish()
    late_grad.second(early_grad.next)
    out_both = merge([[activated]], w_down, 0, halves=2)
    early_grad.third()
    up_grad.fourth()
    near, far = add_small(info, near, far, 2)
    far = swap_z(far, 2)
    keep, send = add_out(info, hidden, out_both)
    output_got = swap(after(send), "y")
    output_keep = after(keep)
    final_rows = after(final_rows)
    final_far = swap(final_rows, "y")
    early_grad.fourth()
    up_grad.finish()
    near, far = add_small(info, near, far)
    far = swap(far, "x")
    late_grad.third()
    near = add_pair(info, near, far)
    if lax.axis_size("r") > 1:
        near = lax.psum_scatter(near, "r", scatter_dimension=1, tiled=True)
    far = swap(near, "y")
    early_grad.finish()
    near = add_pair(info, near, far)
    far = swap(near, "c")
    late_grad.fourth()
    init_grad, grad_gains, grad_gate = place_small(info, near, far, state_half)
    output = place_rows(info, output_keep, output_got)[:, None]
    final_state = place_state(info, final_rows, swap(final_rows, "c"), final_far, swap(final_far, "c"))[:, None]
    input_grad = place_rows(info, input_keep, input_got)[:, None]
    late_grad.finish()
    grad_hidden_down, grad_hidden_up = down_grad.total, up_grad.total
    grad_token_output, grad_query, grad_state_output = [
        early_grad.total[:, i * head : (i + 1) * head] for i in range(3)
    ]
    late = late_grad.total
    grad_token_weights = jnp.stack([grad_query, late[:, :head], late[:, head : 2 * head]], axis=1)
    grad_state_weights = late[:, 2 * head :].reshape(-1, 3, head)
    return (
        output,
        final_state,
        input_grad,
        grad_token_weights,
        grad_token_output,
        grad_state_weights,
        grad_state_output,
        grad_hidden_up,
        grad_hidden_down,
        grad_gains,
        grad_gate[0],
        init_grad,
    )


def solution(mesh):
    dp, heads = mesh.devices.shape
    fine = Mesh(mesh.devices.reshape(dp // (2 * RING), RING, 2, heads // 2, 2), ("r", "z", "x", "y", "c"))
    d, h = ("r", "z", "x"), ("y", "c")
    return jax.shard_map(
        body,
        mesh=fine,
        in_specs=(
            P(None, d, h, None),
            P(None, d),
            P(d, None, h),
            P(d, h),
            P(d, None, h),
            P(d, h),
            P(d, h),
            P(d, h),
            P(None, d),
            P(d),
            P(None, d),
            P(None, d, h, None),
            P(None, d, None, None),
        ),
        out_specs=(
            P(None, d, h, None),
            P(None, d, None, None),
            P(None, d, h, None),
            P(d, None, h),
            P(d, h),
            P(d, None, h),
            P(d, h),
            P(d, h),
            P(d, h),
            P(None, d),
            P(d),
            P(None, d),
        ),
        check_vma=False,
    )
```

```python
import functools

import jax
import jax.numpy as jnp
from jax import lax
from jax.experimental import pallas as pl
from jax.experimental.pallas import tpu as pltpu
from jax.sharding import Mesh
from jax.sharding import PartitionSpec as P

HEAD_DIM = 128
BLOCK = 512
EPSILON = 1e-06
MASKED = -1e30
COST = 0.01
LONG = 1e11
GELU = 0.7978845608028654
RING = 4
BF = jnp.bfloat16
F32 = jnp.float32


def swap(array, axis):
    return lax.ppermute(array, axis, [(0, 1), (1, 0)])


def swap_z(array, bit):
    return lax.ppermute(array, "z", [(i, i ^ bit) for i in range(RING)])


def matmul(left, right, contract):
    return lax.dot_general(
        left, right, (contract, ((), ())), preferred_element_type=jnp.float32
    )


def mm(left, right):
    return matmul(left, right, ((1,), (0,)))


def mm_nt(left, right):
    return matmul(left, right, ((1,), (1,)))


def mm_tn(left, right):
    return matmul(left, right, ((0,), (0,)))


RING_BITS = (0, 2, 1, 3)


def width_places():
    z, x = lax.axis_index("z"), lax.axis_index("x")
    return [jnp.bitwise_xor(z, RING_BITS[k]) * 2 + jnp.bitwise_xor(x, dx) for dx in range(2) for k in range(RING)]


def width_places_back():
    z, x = lax.axis_index("z"), lax.axis_index("x")
    places = []
    for z_to in range(RING):
        apart = jnp.bitwise_xor(z, z_to)
        k = lax.rem(apart, 2) * 2 + lax.div(apart, 2)
        places += [jnp.bitwise_xor(x, x_to) * RING + k for x_to in range(2)]
    return places


def take_pieces(array, places):
    groups = lax.axis_size("r")
    lead, width = array.shape[:-1], array.shape[-1]
    split = array.reshape(lead + (groups, len(places), width // (groups * len(places))))
    axis = len(lead) + 1
    return [lax.dynamic_index_in_dim(split, place, axis, keepdims=False) for place in places]


def to_local(array):
    pieces = take_pieces(array, width_places())
    lead = array.shape[:-1]
    return jnp.concatenate([p.reshape(lead + (-1,)) for p in pieces], axis=-1)


def from_local(array):
    groups = lax.axis_size("r")
    lead, width = array.shape[:-1], array.shape[-1]
    split = array.reshape(lead + (2 * RING, groups, width // (groups * 2 * RING)))
    axis = len(lead)
    pieces = [lax.dynamic_index_in_dim(split, place, axis, keepdims=False) for place in width_places_back()]
    return jnp.stack(pieces, axis=axis + 1).reshape(array.shape)


def gather_groups(array, axis):
    if lax.axis_size("r") == 1:
        return array
    return lax.all_gather(array, "r", axis=axis, tiled=True)


def scatter_groups(array, axis):
    if lax.axis_size("r") == 1:
        return array
    return lax.psum_scatter(array, "r", scatter_dimension=axis, tiled=True)


class Order:
    def __init__(self):
        self.last = []


ORDER = Order()


def call(kernel, grid, inputs, in_specs, outputs, out_specs, flops=0, exps=0, deps=(), vmem=16, long=False, **more):
    block_bytes = sum(a.size * a.dtype.itemsize for a in inputs)
    shapes = [jax.ShapeDtypeStruct(shape, dtype) for shape, dtype in outputs]
    out_bytes = sum(s.size * s.dtype.itemsize for s in shapes)
    given = len(inputs)
    deps = [array for array in list(deps) + ORDER.last if all(array is not other for other in inputs)]

    def run(*refs):
        kernel(*refs[:given], *refs[given + len(deps) :])

    out = pl.pallas_call(
        run,
        grid=grid,
        in_specs=list(in_specs) + [pl.BlockSpec(memory_space=pl.ANY)] * len(deps),
        out_specs=out_specs,
        out_shape=shapes,
        compiler_params=pltpu.CompilerParams(vmem_limit_bytes=vmem * 2**20),
        cost_estimate=pl.CostEstimate(
            flops=int(LONG) if long else int(flops * COST), bytes_accessed=int((block_bytes + out_bytes) * COST), transcendentals=int(exps * COST)
        ),
        **more,
    )(*inputs, *deps)
    ORDER.last = [min(out, key=lambda array: array.size)]
    return out


def whole(array):
    return pl.BlockSpec(array.shape, lambda *_: (0,) * array.ndim)


def whole_out(shape):
    return pl.BlockSpec(shape, lambda *_: (0,) * len(shape))


def stack_rows(first, second, deps=()):
    rows, width = first.shape

    def kernel(first_ref, second_ref, out_ref):
        out_ref[:rows] = first_ref[...]
        out_ref[rows:] = second_ref[...]

    return call(
        kernel,
        (1,),
        [first, second],
        [whole(first)] * 2,
        [((2 * rows, width), BF)],
        [whole_out((2 * rows, width))],
        deps=deps,
    )[0]


def join_columns(arrays, deps):
    rows = arrays[0].shape[0]
    width = sum(array.shape[1] for array in arrays)

    def kernel(*refs):
        place = 0
        for ref in refs[:-1]:
            refs[-1][:, place : place + ref.shape[1]] = ref[...]
            place += ref.shape[1]

    return call(
        kernel,
        (1,),
        arrays,
        [whole(array) for array in arrays],
        [((rows, width), BF)],
        [whole_out((rows, width))],
        deps=deps,
    )[0]


class Gather:
    def __init__(self, shard):
        self.shard = gather_groups(shard, 0)
        self.got = swap_z(self.shard, 2)

    def spread(self, deps=(), by_x=False):
        low = stack_rows(self.shard, self.got, deps)
        low_x, low_y = swap(low, "x"), swap(low, "y")
        high = swap_z(low, 1)
        high_y, high_x = swap(high, "y"), swap(high, "x")
        low_xy = swap(low_y, "x") if by_x else swap(low_x, "y")
        high_xy = swap(high_y, "x")
        self.pieces = [[[low, high], [low_x, high_x]], [[low_y, high_y], [low_xy, high_xy]]]
        self.ring, self.low, self.high, self.far = [high], [low_x, low_y], [high_x, high_y], [low_xy, high_xy]
        return self.pieces


def flat_pieces(pieces):
    return [pieces[y][x][half] for y in range(2) for x in range(2) for half in range(2)]


def spread_rows(info, near, far):
    size = near.shape[1]
    rows = near.shape[0] // RING

    def kernel(near_ref, far_ref, out_ref):
        for k in range(RING):
            out_ref[:, k * size : (k + 1) * size] = near_ref[k * rows : (k + 1) * rows]
            out_ref[:, (RING + k) * size : (RING + k + 1) * size] = far_ref[k * rows : (k + 1) * rows]

    return call(
        kernel,
        (1,),
        [near, far],
        [whole(near), whole(far)],
        [((rows, 2 * RING * size), near.dtype)],
        [whole_out((rows, 2 * RING * size))],
    )[0]


def row_order(own, other, blocks):
    per = own.shape[0] // blocks
    parts = []
    for b in range(blocks):
        parts += [own[b * per : (b + 1) * per], other[b * per : (b + 1) * per]]
    return jnp.concatenate(parts, axis=0)


def project(own, other, pieces, column, width, block, blocks=1, gate=None, activate=False, deps=(), long=False):
    rows = own.shape[0] * 2
    refs = flat_pieces(pieces)
    first = column // block

    def kernel(*args):
        own_ref, other_ref, weights = args[0], args[1], args[2:10]
        left = row_order(own_ref[...], other_ref[...], blocks)
        for y in range(2):
            weight = jnp.concatenate([ref[...] for ref in weights[4 * y : 4 * y + 4]], axis=0)
            total = mm(left, weight)
            if gate is not None:
                gate_ref, out_ref = args[10], args[11]
                low = total.astype(BF).astype(F32)
                out_ref[y] = (low * gate_ref[y].astype(F32)).astype(BF)
            elif activate:
                act_ref, slope_ref = args[10], args[11]
                square = total * total
                curve = jnp.tanh(total * (GELU * 0.044715 * square + GELU))
                share = 0.5 * curve + 0.5
                act = total * share
                act_ref[y] = act.astype(BF)
                slope = share + act * (1.0 - curve) * (GELU * 0.134145 * square + GELU)
                slope_ref[y] = slope.astype(BF)
            else:
                args[10][y] = total.astype(BF)

    spec = pl.BlockSpec((2, rows, block), lambda j: (0, 0, j))
    weight_spec = [pl.BlockSpec((ref.shape[0], block), lambda j: (0, first + j)) for ref in refs]
    extra = [] if gate is None else [gate]
    count = 2 if activate else 1
    out = call(
        kernel,
        (width // block,),
        [own, other] + refs + extra,
        [whole(own), whole(other)] + weight_spec + [spec] * len(extra),
        [((2, rows, width), BF)] * count,
        [spec] * count,
        flops=4 * rows * own.shape[1] * width,
        deps=deps, long=long,
    )
    return out if activate else out[0]


def merge(lefts, pieces, column, blocks=1, deps=(), long=False, halves=1):
    refs = flat_pieces(pieces)
    columns = sum(part.shape[2] for part in lefts[0])
    per = lefts[0][0].shape[1] // 2
    rows = per * len(lefts)
    width = 8 * refs[0].shape[0] // 2
    first = column // columns
    parts_count = len(lefts[0])
    flat = [part for left in lefts for part in left]

    def kernel(*args):
        left_refs, weights = args[: len(flat)], args[len(flat) : len(flat) + 8]
        own_ref, *other_refs = args[len(flat) + 8 :]
        size = rows // halves
        sides = [
            jnp.concatenate([ref[...] for ref in weights[4 * y : 4 * y + 4]], axis=0) for y in range(2)
        ]
        for core in (1, 0):
            total = None
            for y in range(2):
                left = []
                for b in range(len(lefts)):
                    here = left_refs[b * parts_count : (b + 1) * parts_count]
                    left.append(jnp.concatenate([ref[y, core * per : (core + 1) * per] for ref in here], axis=1))
                piece = mm_nt(jnp.concatenate(left, axis=0), sides[y])
                total = piece if total is None else total + piece
            if core:
                for i, ref in enumerate(other_refs):
                    ref[...] = total[i * size : (i + 1) * size].astype(BF)
            else:
                own_ref[...] = total

    weight_spec = [pl.BlockSpec((ref.shape[0], columns), lambda i: (0, first)) for ref in refs]
    return call(
        kernel,
        (1,),
        flat + refs,
        [whole(left) for left in flat] + weight_spec,
        [((rows, width), F32)] + [((rows // halves, width), BF)] * halves,
        [whole_out((rows, width))] + [whole_out((rows // halves, width))] * halves,
        flops=8 * rows * width * columns,
        deps=deps, long=long,
    )


QUARTERS = ((1, 1), (1, 0), (0, 1), (0, 0))


def outer(segments, block=None, vmem=16, deps=(), long=False, split=False):
    width = segments[0][0][0][0].shape[1]
    sizes = [rights[0].shape[2] for lefts, rights, blocks in segments]
    columns = sum(sizes)
    block = columns if block is None else block
    half = width // 2
    inputs, in_specs, flops = [], [], 0
    for lefts, rights, blocks in segments:
        flat = [array for pair_ in lefts for array in pair_]
        inputs += flat + list(rights)
        in_specs += [whole(array) for array in flat]
        wide = min(block, rights[0].shape[2])
        in_specs += [pl.BlockSpec((2, right.shape[1], wide), lambda j: (0, 0, j)) for right in rights]
        flops += 4 * width * rights[0].shape[2] * sum(right.shape[1] for right in rights)

    sizes_out = [half // 2, half, half, half, half // 2] if split else [half] * 4

    def kernel(*args):
        outs = args[len(inputs) :]
        place, column = 0, 0
        for lefts, rights, blocks in segments:
            left_refs = args[place : place + 2 * len(lefts)]
            right_refs = args[place + 2 * len(lefts) : place + 2 * len(lefts) + len(rights)]
            place += 2 * len(lefts) + len(rights)
            left = jnp.concatenate(
                [row_order(left_refs[2 * i][...], left_refs[2 * i + 1][...], blocks) for i in range(len(lefts))], axis=0
            )
            here = slice(column, column + right_refs[0].shape[2])
            column += right_refs[0].shape[2]
            for y in (1, 0):
                right = jnp.concatenate([ref[y] for ref in right_refs], axis=0)
                for x in (1, 0):
                    total = mm_tn(left[:, x * half : (x + 1) * half], right).astype(BF)
                    if split and x and y:
                        outs[0][:, here] = total[: half // 2]
                        outs[-1][:, here] = total[half // 2 :]
                    else:
                        outs[QUARTERS.index((x, y))][:, here] = total

    return call(
        kernel,
        (columns // block,),
        inputs,
        in_specs,
        [((rows, columns), BF) for rows in sizes_out],
        [pl.BlockSpec((rows, block), lambda j: (0, j)) for rows in sizes_out],
        flops=flops,
        vmem=vmem,
        deps=deps, long=long,
    )


def add_low(first, second, deps=(), long=False):
    rows, columns = first.shape
    half = rows // 2

    def kernel(first_ref, second_ref, out_ref):
        out_ref[...] = (first_ref[...].astype(F32) + second_ref[...].astype(F32)).astype(BF)

    spec = pl.BlockSpec((half, columns), lambda i: (i, 0))
    return call(kernel, (2,), [first, second], [spec, spec], [(first.shape, BF)], [spec], deps=deps, long=long)[0]


def add_split(arrays, deps=(), long=False, whole_sum=False):
    rows, columns = arrays[0].shape
    part = rows if whole_sum else rows // 2
    types = (F32,) if whole_sum else (F32, BF)

    def kernel(*refs):
        for half, out_ref in enumerate(refs[len(arrays) :]):
            piece = slice(half * part, (half + 1) * part)
            total = refs[0][piece].astype(F32)
            for ref in refs[1 : len(arrays)]:
                total = total + ref[piece].astype(F32)
            out_ref[...] = total.astype(out_ref.dtype)

    return call(
        kernel,
        (1,),
        arrays,
        [whole(array) for array in arrays],
        [((part, columns), dtype) for dtype in types],
        [whole_out((part, columns))] * len(types),
        deps=deps, long=long,
    )


def add_into(array, piece, half, deps=()):
    rows, columns = piece.shape

    def kernel(array_ref, piece_ref, out_ref):
        out_ref[...] = (array_ref[...].astype(F32) + piece_ref[...].astype(F32)).astype(BF)

    here, there = pl.BlockSpec((rows, columns), lambda i: (half, 0)), pl.BlockSpec((rows, columns), lambda i: (0, 0))
    return call(
        kernel,
        (1,),
        [array, piece],
        [here, there],
        [(array.shape, BF)],
        [here],
        input_output_aliases={0: 0},
        deps=deps,
    )[0]


class Reduce:
    def __init__(self, quarters, first_axis=None):
        self.first_axis = first_axis
        if first_axis is None:
            low11, self.out10, self.out01, self.out00, high11 = quarters
            self.first = [swap(low11, "y"), swap(high11, "x")]
        else:
            out11, self.out10, self.out01, self.out00 = quarters
            self.first = [swap(out11, first_axis)]

    def second(self, deps=(), long=False):
        if self.first_axis is None:
            self.out10 = add_into(self.out10, self.first[0], 0, deps)
            self.out01 = add_into(self.out01, self.first[1], 1, deps)
        elif self.first_axis == "x":
            self.out01 = add_low(self.out01, self.first[0], deps, long)
        else:
            self.out10 = add_low(self.out10, self.first[0], deps, long)
        self.next = [swap(self.out10, "x"), swap(self.out01, "y")]

    def third(self, deps=(), long=False):
        self.near, far = add_split([self.out00] + self.next, deps, long)
        self.got = swap_z(far, 1)

    def fourth(self, deps=(), long=False):
        self.near, far = add_split([self.near, self.got], deps, long)
        self.got = swap_z(far, 2)

    def finish(self, **how):
        self.total = scatter_groups(add_split([self.near, self.got], whole_sum=True, **how)[0], 0)


def pair(own):
    return own, swap(own, "c")


INFO = 3
PIECES = 2 * RING
SMALL = 16


def smem():
    return pl.BlockSpec(memory_space=pltpu.SMEM)


def lanes_at(info_ref, index, width):
    size = width // PIECES
    return pl.ds(pl.multiple_of(info_ref[index] * size, size), size)


def reorder_in(info_ref, source, target, rows=slice(None)):
    width = source.shape[-1]
    size = width // PIECES
    for k in range(PIECES):
        target[rows, k * size : (k + 1) * size] = source[:, lanes_at(info_ref, INFO + k, width)].astype(target.dtype)


def reorder_out(info_ref, source, target, rows=slice(None)):
    width = source.shape[-1]
    size = width // PIECES
    for k in range(PIECES):
        part = source[rows, lanes_at(info_ref, INFO + PIECES + k, width)]
        target[:, k * size : (k + 1) * size] = part.astype(target.dtype)


def swap_all(arrays):
    return [swap(array, "c") for array in arrays]


def both_cores(own_ref, *got_refs):
    return own_ref[...] + jnp.concatenate([ref[...] for ref in got_refs], axis=0).astype(F32)


def inverse_rms(values):
    return lax.rsqrt(jnp.mean(values * values, axis=-1, keepdims=True) + EPSILON)


def rms_back(values, gain, grad):
    inverse = inverse_rms(values)
    scaled = values * inverse
    weighted = grad * gain
    back = inverse * (weighted - scaled * jnp.mean(scaled * weighted, axis=-1, keepdims=True))
    return back, jnp.sum(grad * scaled, axis=0, keepdims=True)


def rowwise(kernel, inputs, outputs, scratch=(), deps=(), long=False):
    return call(
        kernel,
        (1,),
        inputs,
        [smem()] + [whole(array) for array in inputs[1:]],
        outputs,
        [whole_out(shape) for shape, _ in outputs],
        scratch_shapes=[pltpu.VMEM(shape, dtype) for shape, dtype in scratch],
        deps=deps, long=long,
    )


def own_rows(info, keep, got):
    rows, width = keep.shape

    def kernel(info_ref, keep_ref, got_ref, out_ref):
        y = info_ref[2]
        reorder_in(info_ref, keep_ref, out_ref, pl.ds(pl.multiple_of(y * rows, rows), rows))
        reorder_in(info_ref, got_ref, out_ref, pl.ds(pl.multiple_of((1 - y) * rows, rows), rows))

    return rowwise(kernel, [info, keep, got], [((2 * rows, width), BF)])[0]


def local_rows(info, array):
    def kernel(info_ref, in_ref, out_ref):
        reorder_in(info_ref, in_ref, out_ref)

    return rowwise(kernel, [info, array], [(array.shape, array.dtype)])[0]


def norm_rows(info, values, gain, deps=()):
    def kernel(info_ref, in_ref, gain_ref, out_ref):
        rows = in_ref[...].astype(F32)
        out_ref[...] = (rows * inverse_rms(rows) * gain_ref[...]).astype(BF)

    return rowwise(kernel, [info, values, gain], [(values.shape, BF)], deps=deps)[0]


def add_norm(info, rows, both, gain, deps=()):
    own, *others = both

    def kernel(info_ref, row_ref, own_ref, got_ref, gain_ref, hidden_ref, norm_ref):
        hidden = row_ref[...].astype(F32) + (own_ref[...] + got_ref[...].astype(F32))
        hidden_ref[...] = hidden
        norm_ref[...] = (hidden * inverse_rms(hidden) * gain_ref[...]).astype(BF)

    return rowwise(kernel, [info, rows, own, *swap_all(others), gain], [(rows.shape, F32), (rows.shape, BF)], deps=deps)


def add_out(info, hidden, both):
    own, *others = both
    rows, width = hidden.shape
    half = rows // 2

    def kernel(info_ref, hidden_ref, own_ref, low_ref, high_ref, keep_ref, send_ref, scratch):
        y = info_ref[2]
        scratch[...] = hidden_ref[...] + (both_cores(own_ref, low_ref, high_ref))
        reorder_out(info_ref, scratch, keep_ref, pl.ds(pl.multiple_of(y * half, half), half))
        reorder_out(info_ref, scratch, send_ref, pl.ds(pl.multiple_of((1 - y) * half, half), half))

    return rowwise(
        kernel,
        [info, hidden, own, *swap_all(others)],
        [((half, width), BF)] * 2,
        [((rows, width), F32)],
    )


def step_state(info, state, both, gate, gain):
    own, *others = both

    def kernel(info_ref, state_ref, own_ref, got_ref, gate_ref, gain_ref, next_ref, norm_ref, update_ref):
        update = own_ref[...] + got_ref[...].astype(F32)
        update_ref[...] = update
        after = gate_ref[...] * state_ref[...] + (1.0 - gate_ref[...]) * update
        next_ref[...] = after
        norm_ref[...] = (after * inverse_rms(after) * gain_ref[...]).astype(BF)

    return rowwise(
        kernel,
        [info, state, own, *swap_all(others), gate, gain],
        [(state.shape, F32), (state.shape, BF), (state.shape, F32)],
    )


def last_state(info, state, both, gate):
    own, *others = both

    def kernel(info_ref, state_ref, own_ref, got_ref, gate_ref, final_ref, update_ref, scratch):
        update = own_ref[...] + got_ref[...].astype(F32)
        update_ref[...] = update
        scratch[...] = gate_ref[...] * state_ref[...] + (1.0 - gate_ref[...]) * update
        reorder_out(info_ref, scratch, final_ref)

    return rowwise(
        kernel,
        [info, state, own, *swap_all(others), gate],
        [(state.shape, BF), (state.shape, F32)],
        [(state.shape, F32)],
    )


def back_hidden(info, hidden, both, gain, dy):
    own, *others = both

    def kernel(info_ref, hidden_ref, own_ref, low_ref, high_ref, gain_ref, dy_ref, grad_ref, branch_ref, gain_grad_ref):
        grad = both_cores(own_ref, low_ref, high_ref)
        back, gain_grad_ref[...] = rms_back(hidden_ref[...], gain_ref[...], grad)
        total = dy_ref[...].astype(F32) + back
        grad_ref[...] = total
        branch_ref[...] = total.astype(BF)

    return rowwise(
        kernel,
        [info, hidden, own, *swap_all(others), gain, dy],
        [(hidden.shape, F32), (hidden.shape, BF), ((1, hidden.shape[1]), F32)],
    )


def back_update(info, grad, gate):
    def kernel(info_ref, grad_ref, gate_ref, out_ref):
        out_ref[...] = ((1.0 - gate_ref[...]) * grad_ref[...].astype(F32)).astype(BF)

    return rowwise(kernel, [info, grad, gate], [(grad.shape, BF)])[0]


def back_state(info, grad, state, update, both, gate, gain):
    own, *others = both
    width = state.shape[1]

    def kernel(
        info_ref, grad_ref, state_ref, update_ref, own_ref, *refs
    ):
        got_refs = refs[: len(others)]
        gate_ref, gain_ref, out_ref, next_ref, gain_grad_ref, gate_grad_ref = refs[len(others) :]
        gate_open = gate_ref[...]
        grad_now = grad_ref[...].astype(F32)
        values = state_ref[...]
        gate_grad_ref[...] = jnp.sum(grad_now * (values - update_ref[...]), axis=0, keepdims=True) * (
            gate_open * (1.0 - gate_open)
        )
        back, gain_grad_ref[...] = rms_back(values, gain_ref[...], both_cores(own_ref, *got_refs))
        total = gate_open * grad_now + back
        out_ref[...] = total
        next_ref[...] = ((1.0 - gate_open) * total).astype(BF)

    return rowwise(
        kernel,
        [info, grad, state, update, own, *swap_all(others), gate, gain],
        [(state.shape, F32), (state.shape, BF), ((1, width), F32), ((1, width), F32)],
    )


def back_input(info, values, both, gain, grad_hidden):
    own, *others = both
    rows, width = values.shape
    half = rows // 2

    def kernel(info_ref, value_ref, own_ref, low_ref, high_ref, gain_ref, grad_ref, keep_ref, send_ref, gain_grad_ref, scratch):
        y = info_ref[2]
        grad = both_cores(own_ref, low_ref, high_ref)
        back, gain_grad_ref[...] = rms_back(value_ref[...].astype(F32), gain_ref[...], grad)
        scratch[...] = grad_ref[...] + back
        reorder_out(info_ref, scratch, keep_ref, pl.ds(pl.multiple_of(y * half, half), half))
        reorder_out(info_ref, scratch, send_ref, pl.ds(pl.multiple_of((1 - y) * half, half), half))

    return rowwise(
        kernel,
        [info, values, own, *swap_all(others), gain, grad_hidden],
        [((half, width), F32), ((half, width), BF), ((1, width), F32)],
        [((rows, width), F32)],
    )


def pack_small(info, states, vectors):
    rows, width = states.shape
    half = width // 2
    counts = [len(group) for group in vectors]
    flat = [vector for group in vectors for vector in group]
    pad = SMALL - len(vectors)

    def kernel(info_ref, state_ref, *refs):
        near_ref, far_ref = refs[len(flat) :]
        parts, place = [], 0
        for count in counts:
            parts.append(sum(ref[...] for ref in refs[place : place + count]))
            place += count
        tail = jnp.concatenate(parts + [jnp.zeros((pad, width), F32)], axis=0)
        quarter = half // 2
        for source, here in ((state_ref[...], slice(0, rows)), (tail, slice(rows, rows + SMALL))):
            for x in range(2):
                to = slice(x * quarter, (x + 1) * quarter)
                near_ref[here, to] = source[:, 2 * x * quarter : (2 * x + 1) * quarter]
                far_ref[here, to] = source[:, (2 * x + 1) * quarter : (2 * x + 2) * quarter].astype(BF)

    shape = (rows + SMALL, half)
    return rowwise(kernel, [info, states] + flat, [(shape, F32), (shape, BF)])


def add_small(info, near, got, groups=1):
    rows, width = near.shape
    half = width // 2

    def kernel(info_ref, near_ref, got_ref, near_out, far_out):
        total = near_ref[...] + got_ref[...].astype(F32)
        size = half // groups
        for g in range(groups):
            to = slice(g * size, (g + 1) * size)
            near_out[:, to] = total[:, 2 * g * size : (2 * g + 1) * size]
            far_out[:, to] = total[:, (2 * g + 1) * size : (2 * g + 2) * size].astype(BF)

    return rowwise(kernel, [info, near, got], [((rows, half), F32), ((rows, half), BF)])


def add_pair(info, near, got):
    def kernel(info_ref, near_ref, got_ref, out_ref):
        out_ref[...] = near_ref[...] + got_ref[...].astype(F32)

    return rowwise(kernel, [info, near, got], [(near.shape, F32)])[0]


def place_small(info, near, far, states):
    size = near.shape[1]

    def kernel(info_ref, near_ref, far_ref, state_ref, gain_ref, gate_ref):
        c = info_ref[0]
        state_ref[pl.ds(pl.multiple_of(c * states, states), states)] = near_ref[:states]
        state_ref[pl.ds(pl.multiple_of((1 - c) * states, states), states)] = far_ref[:states]
        total = near_ref[states:] + far_ref[states:]
        gain_ref[...] = total[:3]
        gate_ref[...] = total[3:4]

    return rowwise(kernel, [info, near, far], [((2 * states, size), F32), ((3, size), F32), ((1, size), F32)])


def place_rows(info, keep, got):
    shape = (2,) + keep.shape

    def kernel(info_ref, keep_ref, got_ref, out_ref):
        y = info_ref[2]
        out_ref[y] = keep_ref[...]
        out_ref[1 - y] = got_ref[...].astype(keep.dtype)

    return rowwise(kernel, [info, keep, got], [(shape, keep.dtype)])[0]


def place_state(info, near, near_c, far, far_c):
    rows, width = near.shape

    def kernel(info_ref, near_ref, near_c_ref, far_ref, far_c_ref, out_ref):
        c, y = info_ref[0], info_ref[2]
        here = pl.ds(pl.multiple_of(c * rows, rows), rows)
        there = pl.ds(pl.multiple_of((1 - c) * rows, rows), rows)
        out_ref[y, here] = near_ref[...]
        out_ref[y, there] = near_c_ref[...]
        out_ref[1 - y, here] = far_ref[...]
        out_ref[1 - y, there] = far_c_ref[...]

    return rowwise(kernel, [info, near, near_c, far, far_c], [((2, 2 * rows, width), near.dtype)])[0]


SCALE = HEAD_DIM ** (-0.5)


def key_tiles(b, j):
    tiles = []
    if b > 0:
        tiles += [(b - 1, jj, "after" if jj == j else "all") for jj in range(j, 2)]
    tiles += [(b, jj, "until" if jj == j else "all") for jj in range(j + 1)]
    return tiles


def tile_mask(kind, size, limit):
    rows = lax.broadcasted_iota(jnp.int32, (size, size), 0)
    columns = lax.broadcasted_iota(jnp.int32, (size, size), 1)
    mask = None
    if kind == "after":
        mask = columns > rows
    if kind == "until":
        mask = columns <= rows
    if limit is not None:
        inside = columns < limit
        mask = inside if mask is None else mask & inside
    return mask


def masked_scores(queries, keys, masks):
    scores = mm_nt(queries, keys) * SCALE
    parts, place = [], 0
    for size, mask in masks:
        part = scores[:, place : place + size]
        parts.append(part if mask is None else jnp.where(mask, part, MASKED))
        place += size
    return jnp.concatenate(parts, axis=1)


def attention_plan(b, last, size, core, count, states):
    def start(block, j):
        return pl.multiple_of(block * 2 * size + jnp.bitwise_xor(core, j) * size, size)

    plan = []
    for j in range(2):
        tiles, masks = [], []
        for block, jj, kind in key_tiles(b, j):
            limit = count - jj * size if block == b and last else None
            tiles.append((block, jj))
            masks.append((size, tile_mask(kind, size, limit)))
        plan.append((tiles, masks + [(states, None)]))
    state_masks = [(states, None)]
    for jj in range(2):
        state_masks.append((size, tile_mask("all", size, count - jj * size if last else None)))
    return start, plan, state_masks


def block_spec(rows, width):
    return pl.BlockSpec((1, rows, width), lambda y: (y, 0, 0))


def head_slices(lanes, h):
    return [slice(p * lanes + h * HEAD_DIM, p * lanes + (h + 1) * HEAD_DIM) for p in range(3)]


def attend_rows(queries, keys, values, masks):
    scores = masked_scores(queries, keys, masks)
    top = jnp.max(scores, axis=1, keepdims=True)
    weights = jnp.exp(scores - top)
    total = jnp.sum(weights, axis=1, keepdims=True)
    mixed = mm(weights.astype(BF), values) / total
    return mixed.astype(BF), top + jnp.log(total)


def attend_rows_back(queries, keys, values, masks, log_total, grad):
    scores = masked_scores(queries, keys, masks)
    probs = jnp.exp(scores - log_total)
    grad_probs = mm_nt(grad, values)
    row_sum = jnp.sum(grad_probs * probs, axis=1, keepdims=True)
    low = (probs * (grad_probs - row_sum)).astype(BF)
    return mm(low, keys) * SCALE, mm_tn(low, queries) * SCALE, mm_tn(probs.astype(BF), grad)


def token_pairs(b, heads, states):
    return 2 * heads * BLOCK * (BLOCK * (1.25 if b else 0.75) + states)


def forward_tokens(b, blocks, info, tokens, states, deps=()):
    lanes = tokens.shape[2] // 3
    heads = lanes // HEAD_DIM
    size = BLOCK // 2
    count_states = states.shape[1]

    def kernel(info_ref, token_ref, state_ref, mixed_ref, log_ref):
        start, plan, state_masks = attention_plan(
            b, b == blocks - 1, size, info_ref[0], info_ref[1], count_states
        )
        for h in range(heads):
            query, key, value = head_slices(lanes, h)
            for j, (tiles, masks) in enumerate(plan):
                rows = [pl.ds(start(*place), size) for place in tiles]
                keys = jnp.concatenate([token_ref[0, at, key] for at in rows] + [state_ref[0, :, key]], axis=0)
                values = jnp.concatenate([token_ref[0, at, value] for at in rows] + [state_ref[0, :, value]], axis=0)
                here = pl.ds(start(0, j), size)
                mixed_ref[0, here, query], log_ref[0, here, h : h + 1] = attend_rows(
                    token_ref[0, pl.ds(start(b, j), size), query], keys, values, masks
                )

    pairs = int(token_pairs(b, heads, count_states))
    return call(
        kernel,
        (2,),
        [info, tokens, states],
        [smem(), block_spec((b + 1) * BLOCK, 3 * lanes), block_spec(count_states, 3 * lanes)],
        [((2, BLOCK, lanes), BF), ((2, BLOCK, 128), F32)],
        [block_spec(BLOCK, lanes), block_spec(BLOCK, 128)],
        flops=4 * pairs * HEAD_DIM,
        exps=pairs,
        deps=deps,
    )


def forward_states(b, blocks, info, tokens, states, deps=()):
    lanes = tokens.shape[2] // 3
    heads = lanes // HEAD_DIM
    size = BLOCK // 2
    count_states = states.shape[1]

    def kernel(info_ref, token_ref, state_ref, mixed_ref, log_ref):
        start, plan, state_masks = attention_plan(
            0, b == blocks - 1, size, info_ref[0], info_ref[1], count_states
        )
        for h in range(heads):
            query, key, value = head_slices(lanes, h)
            rows = [pl.ds(start(0, j), size) for j in range(2)]
            keys = jnp.concatenate([state_ref[0, :, key]] + [token_ref[0, at, key] for at in rows], axis=0)
            values = jnp.concatenate([state_ref[0, :, value]] + [token_ref[0, at, value] for at in rows], axis=0)
            for begin in range(0, count_states, size):
                here = slice(begin, begin + size)
                mixed_ref[0, here, query], log_ref[0, here, h : h + 1] = attend_rows(
                    state_ref[0, here, query], keys, values, state_masks
                )

    pairs = 2 * heads * count_states * (count_states + BLOCK)
    return call(
        kernel,
        (2,),
        [info, tokens, states],
        [smem(), pl.BlockSpec((1, BLOCK, 3 * lanes), lambda y: (y, b, 0)), block_spec(count_states, 3 * lanes)],
        [((2, count_states, lanes), BF), ((2, count_states, 128), F32)],
        [block_spec(count_states, lanes), block_spec(count_states, 128)],
        flops=4 * pairs * HEAD_DIM,
        exps=pairs,
        deps=deps,
    )


def add_part(sums, place, part):
    sums[place] = part if place not in sums else sums[place] + part


def backward_tokens(b, blocks, info, tokens, states, logs, grad_mixed, deps=(), long=False):
    lanes = tokens.shape[2] // 3
    heads = lanes // HEAD_DIM
    size = BLOCK // 2
    count_states = states.shape[1]

    def kernel(info_ref, token_ref, state_ref, log_ref, grad_ref, query_ref, own_ref, state_out_ref, *before_ref):
        start, plan, state_masks = attention_plan(
            b, b == blocks - 1, size, info_ref[0], info_ref[1], count_states
        )
        for h in range(heads):
            query, key, value = head_slices(lanes, h)
            sums = ({}, {})
            for j, (tiles, masks) in enumerate(plan):
                rows = [pl.ds(start(*place), size) for place in tiles]
                keys = jnp.concatenate([token_ref[0, at, key] for at in rows] + [state_ref[0, :, key]], axis=0)
                values = jnp.concatenate([token_ref[0, at, value] for at in rows] + [state_ref[0, :, value]], axis=0)
                here = pl.ds(start(0, j), size)
                dq, dk, dv = attend_rows_back(
                    token_ref[0, pl.ds(start(b, j), size), query],
                    keys,
                    values,
                    masks,
                    log_ref[0, here, h : h + 1],
                    grad_ref[0, here, query],
                )
                query_ref[0, here, query] = dq.astype(BF)
                for which, grads in enumerate((dk, dv)):
                    for i, place in enumerate(tiles):
                        add_part(sums[which], place, grads[i * size : (i + 1) * size])
                    add_part(sums[which], "state", grads[len(tiles) * size :])
            for which in range(2):
                columns = slice(which * lanes + h * HEAD_DIM, which * lanes + (h + 1) * HEAD_DIM)
                state_out_ref[0, :, columns] = sums[which]["state"].astype(BF)
                for j in range(2):
                    here = pl.ds(start(0, j), size)
                    own_ref[0, here, columns] = sums[which][(b, j)].astype(BF)
                    if b > 0:
                        before_ref[0][0, here, columns] = sums[which][(b - 1, j)].astype(BF)

    pairs = int(token_pairs(b, heads, count_states))
    outputs = [((2, BLOCK, lanes), BF), ((2, BLOCK, 2 * lanes), BF), ((2, count_states, 2 * lanes), BF)]
    out_specs = [block_spec(BLOCK, lanes), block_spec(BLOCK, 2 * lanes), block_spec(count_states, 2 * lanes)]
    if b > 0:
        outputs.append(((2, BLOCK, 2 * lanes), BF))
        out_specs.append(block_spec(BLOCK, 2 * lanes))
    return call(
        kernel,
        (2,),
        [info, tokens, states, logs, grad_mixed],
        [
            smem(),
            block_spec((b + 1) * BLOCK, 3 * lanes),
            block_spec(count_states, 3 * lanes),
            block_spec(BLOCK, 128),
            pl.BlockSpec((1, BLOCK, lanes), lambda y: (y, b, 0)),
        ],
        outputs,
        out_specs,
        flops=10 * pairs * HEAD_DIM,
        exps=pairs,
        deps=deps,
        long=long,
    )


def backward_states(b, blocks, info, tokens, states, logs, grad_mixed, token_sums, state_sums, deps=(), long=False):
    lanes = tokens.shape[2] // 3
    heads = lanes // HEAD_DIM
    size = BLOCK // 2
    count_states = states.shape[1]
    count = len(token_sums)

    def kernel(info_ref, token_ref, state_ref, log_ref, grad_ref, sum_ref, *rest):
        token_sum_refs, (state_out_ref, token_out_ref) = rest[:count], rest[count:]
        start, plan, state_masks = attention_plan(
            0, b == blocks - 1, size, info_ref[0], info_ref[1], count_states
        )
        for h in range(heads):
            query, key, value = head_slices(lanes, h)
            rows = [pl.ds(start(0, j), size) for j in range(2)]
            keys = jnp.concatenate([state_ref[0, :, key]] + [token_ref[0, at, key] for at in rows], axis=0)
            values = jnp.concatenate([state_ref[0, :, value]] + [token_ref[0, at, value] for at in rows], axis=0)
            sums = [None, None]
            for begin in range(0, count_states, size):
                here = slice(begin, begin + size)
                dq, dk, dv = attend_rows_back(
                    state_ref[0, here, query],
                    keys,
                    values,
                    state_masks,
                    log_ref[0, here, h : h + 1],
                    grad_ref[0, here, query],
                )
                state_out_ref[0, here, query] = dq.astype(BF)
                sums = [part if old is None else old + part for old, part in zip(sums, (dk, dv))]
            for which, to in ((0, key), (1, value)):
                columns = slice(which * lanes + h * HEAD_DIM, which * lanes + (h + 1) * HEAD_DIM)
                state_out_ref[0, :, to] = (sums[which][:count_states] + sum_ref[0, :, columns].astype(F32)).astype(BF)
                for j in range(2):
                    total = sums[which][count_states + j * size : count_states + (j + 1) * size]
                    for ref in token_sum_refs:
                        total = total + ref[0, rows[j], columns].astype(F32)
                    token_out_ref[0, rows[j], columns] = total.astype(BF)

    pairs = 2 * heads * count_states * (count_states + BLOCK)
    return call(
        kernel,
        (2,),
        [info, tokens, states, logs, grad_mixed, state_sums] + list(token_sums),
        [
            smem(),
            pl.BlockSpec((1, BLOCK, 3 * lanes), lambda y: (y, b, 0)),
            block_spec(count_states, 3 * lanes),
            block_spec(count_states, 128),
            block_spec(count_states, lanes),
            block_spec(count_states, 2 * lanes),
        ]
        + [block_spec(BLOCK, 2 * lanes)] * count,
        [((2, count_states, 3 * lanes), BF), ((2, BLOCK, 2 * lanes), BF)],
        [block_spec(count_states, 3 * lanes), block_spec(BLOCK, 2 * lanes)],
        flops=10 * pairs * HEAD_DIM,
        exps=pairs,
        deps=deps,
        long=long,
    )


def body(
    tokens,
    counts,
    token_weights,
    token_output,
    state_weights,
    state_output,
    hidden_up,
    hidden_down,
    norm_gains,
    gate_bias,
    init_state,
    cotangent,
    state_cotangent,
):
    y, c = lax.axis_index("y"), lax.axis_index("c")
    width = tokens.shape[3]
    state_half = init_state.shape[0] // 2
    blocks = 4 * tokens.shape[2] // BLOCK
    valid_count = lax.dynamic_index_in_dim(counts[:, 0], y, 0, keepdims=False)
    if lax.axis_size("r") == 1:
        places, back = width_places(), width_places_back()
        before, after = (lambda array: array), (lambda array: array)
    else:
        places = back = list(range(PIECES))
        before, after = to_local, from_local
    info = jnp.stack([jnp.asarray(v, jnp.int32) for v in [c, valid_count, y] + places + back])

    def micro(array, index):
        return lax.dynamic_index_in_dim(array[:, 0], index, 0, keepdims=False)

    ORDER.last = []
    shard_rows = token_output.shape[0]
    head, ff = token_output.shape[1], hidden_up.shape[1]
    at_state, at_state_out, at_token_out = 0, 3 * head, ff
    flat = lambda array: array.reshape(shard_rows, -1)
    token = Gather(flat(token_weights))
    token_got = swap(micro(tokens, 1 - y), "y")
    small = jnp.concatenate(
        [
            lax.dynamic_slice_in_dim(init_state, c * state_half, state_half, 0),
            norm_gains,
            gate_bias[None],
            jnp.zeros((12, init_state.shape[1]), BF),
        ],
        axis=0,
    )
    if lax.axis_size("r") > 1:
        small = lax.all_gather(small, "r", axis=1, tiled=True)
    small_got = swap_z(small, 2)
    w_token = token.spread(by_x=True)
    mid = Gather(join_columns([flat(state_weights), state_output], ()))
    small = stack_rows(small, small_got)
    small = stack_rows(small, swap_z(small, 1))
    small_got = swap(small, "x")
    x_rows = own_rows(info, before(micro(tokens, y)), before(token_got))
    small = spread_rows(info, small, small_got)
    gains = [small[state_half + i : state_half + i + 1].astype(F32) for i in range(3)]
    gate_open = jax.nn.sigmoid(small[state_half + 3 : state_half + 4].astype(F32))
    state_now = small[:state_half].astype(F32)
    normed = pair(norm_rows(info, x_rows, gains[0], token.low))
    state_norm = pair(norm_rows(info, state_now, gains[1]))
    w_mid = mid.spread(token.low)
    up = Gather(join_columns([hidden_up, token_output], ()))

    token_proj = project(*normed, w_token, 0, 3 * head, 3 * head // 2, blocks=blocks)
    w_up = up.spread(mid.low)
    down = Gather(join_columns([hidden_down], ()))
    dy_got = swap(micro(cotangent, 1 - y), "y")
    grad_final = lax.dynamic_slice(
        state_cotangent, (y, 0, c * state_half, 0), (1, 1, state_half, width)
    )[0, 0]
    grad_final = local_rows(info, before(grad_final))
    grad_update = pair(back_update(info, grad_final, gate_open))
    kept = []
    mixed = []
    for b in range(blocks):
        proj_wait, state_wait, merge_wait, token_wait = (
            (up.ring, [], up.low + [down.got], up.high) if b == 0 else ([], up.far, down.ring, down.low)
        )
        state_proj = project(*state_norm, w_mid, at_state, 3 * head, 3 * head, deps=proj_wait)
        state_flat, state_logs = forward_states(b, blocks, info, token_proj, state_proj, deps=state_wait)
        both = merge([[state_flat]], w_mid, at_state_out, deps=merge_wait)
        mixed_b, logs = forward_tokens(b, blocks, info, token_proj, state_proj, deps=token_wait)
        mixed.append(mixed_b)
        if b < blocks - 1:
            state_next, next_norm, update = step_state(info, state_now, both, gate_open, gains[1])
        else:
            final_rows, update = last_state(info, state_now, both, gate_open)
            state_next, next_norm = None, None
        kept.append((state_now, state_norm, state_proj, logs, state_logs, state_flat, update))
        state_now = state_next
        state_norm = None if next_norm is None else pair(next_norm)
        if b == 0:
            dy_rows = own_rows(info, before(micro(cotangent, y)), before(dy_got))
            dy_pair = pair(dy_rows)
            grad_state_mixed = project(*grad_update, w_mid, at_state_out, head, head)
            w_down = down.spread()
    hidden, hidden_own = add_norm(
        info, x_rows, merge([[part] for part in mixed], w_up, at_token_out, blocks=blocks, deps=down.high), gains[2]
    )
    hidden_norm = pair(hidden_own)
    activated, slope = project(*hidden_norm, w_up, 0, ff, ff // 2, activate=True)

    down_grad = Reduce(outer([([dy_pair], [activated], 1)], ff // 2, split=True, long=True))
    grad_up = project(*dy_pair, w_down, 0, ff, ff // 2, gate=slope, long=True)
    both = merge([[grad_up]], w_up, 0, halves=2)
    up_grad = Reduce(outer([([hidden_norm], [grad_up], 1)], ff // 2, split=True))
    down_grad.second()
    grad_hidden, branch, gain_hidden = back_hidden(info, hidden, both, gains[2], dy_rows)
    branch = pair(branch)

    grad_mixed = project(*branch, w_up, at_token_out, head, head, blocks=blocks)
    grad_state = grad_final
    gate_sums, gain_sums = [], []
    query_grads, pair_grads = [None] * blocks, [None] * blocks
    update_all, flat_all, norm_all, state_grads = [], [], [], []
    sums = [None] * blocks

    def tokens_back(b, **how):
        state_proj, logs = kept[b][2], kept[b][3]
        query_grads[b], *sums[b] = backward_tokens(b, blocks, info, token_proj, state_proj, logs, grad_mixed, **how)

    def states_back(b, later, **how):
        state_before, state_norm, state_proj, logs, state_logs, state_flat, update = kept[b]
        own_sums, state_sums, *before_sums = sums[b]
        state_grad, pair_grads[b] = backward_states(
            b, blocks, info, token_proj, state_proj, state_logs, grad_state_mixed, [own_sums] + later, state_sums, **how
        )
        update_all.append(grad_update)
        flat_all.append(state_flat)
        norm_all.append(state_norm)
        state_grads.append(state_grad)
        return merge([[state_grad]], w_mid, at_state, halves=1 if b else 2), before_sums

    def state_step(b, both, grad_state):
        state_before, update = kept[b][0], kept[b][-1]
        grad_state, low, gain_sum, gate_sum = back_state(
            info, grad_state, state_before, update, both, gate_open, gains[1]
        )
        gain_sums.append(gain_sum)
        gate_sums.append(gate_sum)
        return grad_state, low

    last = blocks - 1
    tokens_back(last, long=True)
    both, later = states_back(last, [])
    for b in range(last - 1, -1, -1):
        tokens_back(b)
        if b == last - 1:
            up_grad.second()
            down_grad.third()
        grad_state, low = state_step(b + 1, both, grad_state)
        grad_update = pair(low)
        grad_state_mixed = project(*grad_update, w_mid, at_state_out, head, head)
        if b == 0:
            early_grad = Reduce(
                outer(
                    [
                        ([branch], mixed, blocks),
                        ([normed], query_grads, blocks),
                        ([grad_update] + update_all, [kept[0][5]] + flat_all, 1),
                    ],
                    vmem=28,
                    split=True,
                )
            )
        both, later = states_back(b, later, long=b == 0)

    down_grad.fourth()
    early_grad.second()
    token_both = merge(
        [[query_grads[i], pair_grads[i]] for i in range(blocks)], w_token, 0, blocks=blocks, halves=2
    )
    grad_state, low = state_step(0, both, grad_state)
    late_grad = Reduce(outer([([normed], pair_grads, blocks), (norm_all, state_grads, 1)], vmem=28, split=True))
    keep, send, gain_token = back_input(info, x_rows, token_both, gains[0], grad_hidden)
    input_keep, input_got = after(keep), swap(after(send), "y")
    near, far = pack_small(info, grad_state, [[gain_token], gain_sums, [gain_hidden], gate_sums])
    far = swap_z(far, 1)
    up_grad.third()
    down_grad.finish()
    late_grad.second(early_grad.next)
    early_grad.third()
    out_both = merge([[activated]], w_down, 0, halves=2)
    up_grad.fourth()
    near, far = add_small(info, near, far, 2)
    far = swap_z(far, 2)
    keep, send = add_out(info, hidden, out_both)
    output_got = swap(after(send), "y")
    output_keep = after(keep)
    final_rows = after(final_rows)
    final_far = swap(final_rows, "y")
    early_grad.fourth()
    up_grad.finish()
    near, far = add_small(info, near, far)
    far = swap(far, "x")
    late_grad.third()
    near = add_pair(info, near, far)
    if lax.axis_size("r") > 1:
        near = lax.psum_scatter(near, "r", scatter_dimension=1, tiled=True)
    far = swap(near, "y")
    early_grad.finish()
    near = add_pair(info, near, far)
    far = swap(near, "c")
    late_grad.fourth()
    init_grad, grad_gains, grad_gate = place_small(info, near, far, state_half)
    output = place_rows(info, output_keep, output_got)[:, None]
    final_state = place_state(info, final_rows, swap(final_rows, "c"), final_far, swap(final_far, "c"))[:, None]
    input_grad = place_rows(info, input_keep, input_got)[:, None]
    late_grad.finish()
    grad_hidden_down, grad_hidden_up = down_grad.total, up_grad.total
    grad_token_output, grad_query, grad_state_output = [
        early_grad.total[:, i * head : (i + 1) * head] for i in range(3)
    ]
    late = late_grad.total
    grad_token_weights = jnp.stack([grad_query, late[:, :head], late[:, head : 2 * head]], axis=1)
    grad_state_weights = late[:, 2 * head :].reshape(-1, 3, head)
    return (
        output,
        final_state,
        input_grad,
        grad_token_weights,
        grad_token_output,
        grad_state_weights,
        grad_state_output,
        grad_hidden_up,
        grad_hidden_down,
        grad_gains,
        grad_gate[0],
        init_grad,
    )


def solution(mesh):
    dp, heads = mesh.devices.shape
    fine = Mesh(mesh.devices.reshape(dp // (2 * RING), RING, 2, heads // 2, 2), ("r", "z", "x", "y", "c"))
    d, h = ("r", "z", "x"), ("y", "c")
    return jax.shard_map(
        body,
        mesh=fine,
        in_specs=(
            P(None, d, h, None),
            P(None, d),
            P(d, None, h),
            P(d, h),
            P(d, None, h),
            P(d, h),
            P(d, h),
            P(d, h),
            P(None, d),
            P(d),
            P(None, d),
            P(None, d, h, None),
            P(None, d, None, None),
        ),
        out_specs=(
            P(None, d, h, None),
            P(None, d, None, None),
            P(None, d, h, None),
            P(d, None, h),
            P(d, h),
            P(d, None, h),
            P(d, h),
            P(d, h),
            P(d, h),
            P(None, d),
            P(d),
            P(None, d),
        ),
        check_vma=False,
    )
```

```python
import functools

import jax
import jax.numpy as jnp
from jax import lax
from jax.experimental import pallas as pl
from jax.experimental.pallas import tpu as pltpu
from jax.sharding import Mesh
from jax.sharding import PartitionSpec as P

HEAD_DIM = 128
BLOCK = 512
EPSILON = 1e-06
MASKED = -1e30
COST = 0.01
LONG = 1e11
GELU = 0.7978845608028654
RING = 4
BF = jnp.bfloat16
F32 = jnp.float32


def swap(array, axis):
    return lax.ppermute(array, axis, [(0, 1), (1, 0)])


def swap_z(array, bit):
    return lax.ppermute(array, "z", [(i, i ^ bit) for i in range(RING)])


def matmul(left, right, contract):
    return lax.dot_general(
        left, right, (contract, ((), ())), preferred_element_type=jnp.float32
    )


def mm(left, right):
    return matmul(left, right, ((1,), (0,)))


def mm_nt(left, right):
    return matmul(left, right, ((1,), (1,)))


def mm_tn(left, right):
    return matmul(left, right, ((0,), (0,)))


RING_BITS = (0, 2, 1, 3)


def width_places():
    z, x = lax.axis_index("z"), lax.axis_index("x")
    return [jnp.bitwise_xor(z, RING_BITS[k]) * 2 + jnp.bitwise_xor(x, dx) for dx in range(2) for k in range(RING)]


def width_places_back():
    z, x = lax.axis_index("z"), lax.axis_index("x")
    places = []
    for z_to in range(RING):
        apart = jnp.bitwise_xor(z, z_to)
        k = lax.rem(apart, 2) * 2 + lax.div(apart, 2)
        places += [jnp.bitwise_xor(x, x_to) * RING + k for x_to in range(2)]
    return places


def take_pieces(array, places):
    groups = lax.axis_size("r")
    lead, width = array.shape[:-1], array.shape[-1]
    split = array.reshape(lead + (groups, len(places), width // (groups * len(places))))
    axis = len(lead) + 1
    return [lax.dynamic_index_in_dim(split, place, axis, keepdims=False) for place in places]


def to_local(array):
    pieces = take_pieces(array, width_places())
    lead = array.shape[:-1]
    return jnp.concatenate([p.reshape(lead + (-1,)) for p in pieces], axis=-1)


def from_local(array):
    groups = lax.axis_size("r")
    lead, width = array.shape[:-1], array.shape[-1]
    split = array.reshape(lead + (2 * RING, groups, width // (groups * 2 * RING)))
    axis = len(lead)
    pieces = [lax.dynamic_index_in_dim(split, place, axis, keepdims=False) for place in width_places_back()]
    return jnp.stack(pieces, axis=axis + 1).reshape(array.shape)


def gather_groups(array, axis):
    if lax.axis_size("r") == 1:
        return array
    return lax.all_gather(array, "r", axis=axis, tiled=True)


def scatter_groups(array, axis):
    if lax.axis_size("r") == 1:
        return array
    return lax.psum_scatter(array, "r", scatter_dimension=axis, tiled=True)


class Order:
    def __init__(self):
        self.last = []


ORDER = Order()


def call(kernel, grid, inputs, in_specs, outputs, out_specs, flops=0, exps=0, deps=(), vmem=16, long=False, **more):
    block_bytes = sum(a.size * a.dtype.itemsize for a in inputs)
    shapes = [jax.ShapeDtypeStruct(shape, dtype) for shape, dtype in outputs]
    out_bytes = sum(s.size * s.dtype.itemsize for s in shapes)
    given = len(inputs)
    deps = [array for array in list(deps) + ORDER.last if all(array is not other for other in inputs)]

    def run(*refs):
        kernel(*refs[:given], *refs[given + len(deps) :])

    out = pl.pallas_call(
        run,
        grid=grid,
        in_specs=list(in_specs) + [pl.BlockSpec(memory_space=pl.ANY)] * len(deps),
        out_specs=out_specs,
        out_shape=shapes,
        compiler_params=pltpu.CompilerParams(vmem_limit_bytes=vmem * 2**20),
        cost_estimate=pl.CostEstimate(
            flops=int(LONG) if long else int(flops * COST), bytes_accessed=int((block_bytes + out_bytes) * COST), transcendentals=int(exps * COST)
        ),
        **more,
    )(*inputs, *deps)
    ORDER.last = [min(out, key=lambda array: array.size)]
    return out


def whole(array):
    return pl.BlockSpec(array.shape, lambda *_: (0,) * array.ndim)


def whole_out(shape):
    return pl.BlockSpec(shape, lambda *_: (0,) * len(shape))


def stack_rows(first, second, deps=()):
    rows, width = first.shape

    def kernel(first_ref, second_ref, out_ref):
        out_ref[:rows] = first_ref[...]
        out_ref[rows:] = second_ref[...]

    return call(
        kernel,
        (1,),
        [first, second],
        [whole(first)] * 2,
        [((2 * rows, width), BF)],
        [whole_out((2 * rows, width))],
        deps=deps,
    )[0]


def join_columns(arrays, deps):
    rows = arrays[0].shape[0]
    width = sum(array.shape[1] for array in arrays)

    def kernel(*refs):
        place = 0
        for ref in refs[:-1]:
            refs[-1][:, place : place + ref.shape[1]] = ref[...]
            place += ref.shape[1]

    return call(
        kernel,
        (1,),
        arrays,
        [whole(array) for array in arrays],
        [((rows, width), BF)],
        [whole_out((rows, width))],
        deps=deps,
    )[0]


class Gather:
    def __init__(self, shard):
        self.shard = gather_groups(shard, 0)
        self.got = swap_z(self.shard, 2)

    def spread(self, deps=(), by_x=False):
        low = stack_rows(self.shard, self.got, deps)
        low_x, low_y = swap(low, "x"), swap(low, "y")
        high = swap_z(low, 1)
        high_y, high_x = swap(high, "y"), swap(high, "x")
        low_xy = swap(low_y, "x") if by_x else swap(low_x, "y")
        high_xy = swap(high_y, "x")
        self.pieces = [[[low, high], [low_x, high_x]], [[low_y, high_y], [low_xy, high_xy]]]
        self.ring, self.low, self.high, self.far = [high], [low_x, low_y], [high_x, high_y], [low_xy, high_xy]
        return self.pieces


def flat_pieces(pieces):
    return [pieces[y][x][half] for y in range(2) for x in range(2) for half in range(2)]


def spread_rows(info, near, far):
    size = near.shape[1]
    rows = near.shape[0] // RING

    def kernel(near_ref, far_ref, out_ref):
        for k in range(RING):
            out_ref[:, k * size : (k + 1) * size] = near_ref[k * rows : (k + 1) * rows]
            out_ref[:, (RING + k) * size : (RING + k + 1) * size] = far_ref[k * rows : (k + 1) * rows]

    return call(
        kernel,
        (1,),
        [near, far],
        [whole(near), whole(far)],
        [((rows, 2 * RING * size), near.dtype)],
        [whole_out((rows, 2 * RING * size))],
    )[0]


def row_order(own, other, blocks):
    per = own.shape[0] // blocks
    parts = []
    for b in range(blocks):
        parts += [own[b * per : (b + 1) * per], other[b * per : (b + 1) * per]]
    return jnp.concatenate(parts, axis=0)


def project(own, other, pieces, column, width, block, blocks=1, gate=None, activate=False, deps=(), long=False):
    rows = own.shape[0] * 2
    refs = flat_pieces(pieces)
    first = column // block

    def kernel(*args):
        own_ref, other_ref, weights = args[0], args[1], args[2:10]
        left = row_order(own_ref[...], other_ref[...], blocks)
        for y in range(2):
            weight = jnp.concatenate([ref[...] for ref in weights[4 * y : 4 * y + 4]], axis=0)
            total = mm(left, weight)
            if gate is not None:
                gate_ref, out_ref = args[10], args[11]
                low = total.astype(BF).astype(F32)
                out_ref[y] = (low * gate_ref[y].astype(F32)).astype(BF)
            elif activate:
                act_ref, slope_ref = args[10], args[11]
                square = total * total
                curve = jnp.tanh(total * (GELU * 0.044715 * square + GELU))
                share = 0.5 * curve + 0.5
                act = total * share
                act_ref[y] = act.astype(BF)
                slope = share + act * (1.0 - curve) * (GELU * 0.134145 * square + GELU)
                slope_ref[y] = slope.astype(BF)
            else:
                args[10][y] = total.astype(BF)

    spec = pl.BlockSpec((2, rows, block), lambda j: (0, 0, j))
    weight_spec = [pl.BlockSpec((ref.shape[0], block), lambda j: (0, first + j)) for ref in refs]
    extra = [] if gate is None else [gate]
    count = 2 if activate else 1
    out = call(
        kernel,
        (width // block,),
        [own, other] + refs + extra,
        [whole(own), whole(other)] + weight_spec + [spec] * len(extra),
        [((2, rows, width), BF)] * count,
        [spec] * count,
        flops=4 * rows * own.shape[1] * width,
        deps=deps, long=long,
    )
    return out if activate else out[0]


def merge(lefts, pieces, column, blocks=1, deps=(), long=False, halves=1):
    refs = flat_pieces(pieces)
    columns = sum(part.shape[2] for part in lefts[0])
    per = lefts[0][0].shape[1] // 2
    rows = per * len(lefts)
    width = 8 * refs[0].shape[0] // 2
    first = column // columns
    parts_count = len(lefts[0])
    flat = [part for left in lefts for part in left]

    def kernel(*args):
        left_refs, weights = args[: len(flat)], args[len(flat) : len(flat) + 8]
        own_ref, *other_refs = args[len(flat) + 8 :]
        size = rows // halves
        sides = [
            jnp.concatenate([ref[...] for ref in weights[4 * y : 4 * y + 4]], axis=0) for y in range(2)
        ]
        for core in (1, 0):
            total = None
            for y in range(2):
                left = []
                for b in range(len(lefts)):
                    here = left_refs[b * parts_count : (b + 1) * parts_count]
                    left.append(jnp.concatenate([ref[y, core * per : (core + 1) * per] for ref in here], axis=1))
                piece = mm_nt(jnp.concatenate(left, axis=0), sides[y])
                total = piece if total is None else total + piece
            if core:
                for i, ref in enumerate(other_refs):
                    ref[...] = total[i * size : (i + 1) * size].astype(BF)
            else:
                own_ref[...] = total

    weight_spec = [pl.BlockSpec((ref.shape[0], columns), lambda i: (0, first)) for ref in refs]
    return call(
        kernel,
        (1,),
        flat + refs,
        [whole(left) for left in flat] + weight_spec,
        [((rows, width), F32)] + [((rows // halves, width), BF)] * halves,
        [whole_out((rows, width))] + [whole_out((rows // halves, width))] * halves,
        flops=8 * rows * width * columns,
        deps=deps, long=long,
    )


QUARTERS = ((1, 1), (1, 0), (0, 1), (0, 0))


def outer(segments, block=None, vmem=16, deps=(), long=False, split=False):
    width = segments[0][0][0][0].shape[1]
    sizes = [rights[0].shape[2] for lefts, rights, blocks in segments]
    columns = sum(sizes)
    block = columns if block is None else block
    half = width // 2
    inputs, in_specs, flops = [], [], 0
    for lefts, rights, blocks in segments:
        flat = [array for pair_ in lefts for array in pair_]
        inputs += flat + list(rights)
        in_specs += [whole(array) for array in flat]
        wide = min(block, rights[0].shape[2])
        in_specs += [pl.BlockSpec((2, right.shape[1], wide), lambda j: (0, 0, j)) for right in rights]
        flops += 4 * width * rights[0].shape[2] * sum(right.shape[1] for right in rights)

    sizes_out = [half // 2, half, half, half, half // 2] if split else [half] * 4

    def kernel(*args):
        outs = args[len(inputs) :]
        place, column = 0, 0
        for lefts, rights, blocks in segments:
            left_refs = args[place : place + 2 * len(lefts)]
            right_refs = args[place + 2 * len(lefts) : place + 2 * len(lefts) + len(rights)]
            place += 2 * len(lefts) + len(rights)
            left = jnp.concatenate(
                [row_order(left_refs[2 * i][...], left_refs[2 * i + 1][...], blocks) for i in range(len(lefts))], axis=0
            )
            here = slice(column, column + right_refs[0].shape[2])
            column += right_refs[0].shape[2]
            for y in (1, 0):
                right = jnp.concatenate([ref[y] for ref in right_refs], axis=0)
                for x in (1, 0):
                    total = mm_tn(left[:, x * half : (x + 1) * half], right).astype(BF)
                    if split and x and y:
                        outs[0][:, here] = total[: half // 2]
                        outs[-1][:, here] = total[half // 2 :]
                    else:
                        outs[QUARTERS.index((x, y))][:, here] = total

    return call(
        kernel,
        (columns // block,),
        inputs,
        in_specs,
        [((rows, columns), BF) for rows in sizes_out],
        [pl.BlockSpec((rows, block), lambda j: (0, j)) for rows in sizes_out],
        flops=flops,
        vmem=vmem,
        deps=deps, long=long,
    )


def add_low(first, second, deps=(), long=False):
    rows, columns = first.shape
    half = rows // 2

    def kernel(first_ref, second_ref, out_ref):
        out_ref[...] = (first_ref[...].astype(F32) + second_ref[...].astype(F32)).astype(BF)

    spec = pl.BlockSpec((half, columns), lambda i: (i, 0))
    return call(kernel, (2,), [first, second], [spec, spec], [(first.shape, BF)], [spec], deps=deps, long=long)[0]


def add_split(arrays, deps=(), long=False, whole_sum=False):
    rows, columns = arrays[0].shape
    part = rows if whole_sum else rows // 2
    types = (F32,) if whole_sum else (F32, BF)

    def kernel(*refs):
        for half, out_ref in enumerate(refs[len(arrays) :]):
            piece = slice(half * part, (half + 1) * part)
            total = refs[0][piece].astype(F32)
            for ref in refs[1 : len(arrays)]:
                total = total + ref[piece].astype(F32)
            out_ref[...] = total.astype(out_ref.dtype)

    return call(
        kernel,
        (1,),
        arrays,
        [whole(array) for array in arrays],
        [((part, columns), dtype) for dtype in types],
        [whole_out((part, columns))] * len(types),
        deps=deps, long=long,
    )


def add_into(array, piece, half, deps=()):
    rows, columns = piece.shape

    def kernel(array_ref, piece_ref, out_ref):
        out_ref[...] = (array_ref[...].astype(F32) + piece_ref[...].astype(F32)).astype(BF)

    here, there = pl.BlockSpec((rows, columns), lambda i: (half, 0)), pl.BlockSpec((rows, columns), lambda i: (0, 0))
    return call(
        kernel,
        (1,),
        [array, piece],
        [here, there],
        [(array.shape, BF)],
        [here],
        input_output_aliases={0: 0},
        deps=deps,
    )[0]


class Reduce:
    def __init__(self, quarters, first_axis=None):
        self.first_axis = first_axis
        if first_axis is None:
            low11, self.out10, self.out01, self.out00, high11 = quarters
            self.first = [swap(low11, "y"), swap(high11, "x")]
        else:
            out11, self.out10, self.out01, self.out00 = quarters
            self.first = [swap(out11, first_axis)]

    def second(self, deps=(), long=False):
        if self.first_axis is None:
            self.out10 = add_into(self.out10, self.first[0], 0, deps)
            self.out01 = add_into(self.out01, self.first[1], 1, deps)
        elif self.first_axis == "x":
            self.out01 = add_low(self.out01, self.first[0], deps, long)
        else:
            self.out10 = add_low(self.out10, self.first[0], deps, long)
        self.next = [swap(self.out10, "x"), swap(self.out01, "y")]

    def third(self, deps=(), long=False):
        self.near, far = add_split([self.out00] + self.next, deps, long)
        self.got = swap_z(far, 1)

    def fourth(self, deps=(), long=False):
        self.near, far = add_split([self.near, self.got], deps, long)
        self.got = swap_z(far, 2)

    def finish(self, **how):
        self.total = scatter_groups(add_split([self.near, self.got], whole_sum=True, **how)[0], 0)


def pair(own):
    return own, swap(own, "c")


INFO = 3
PIECES = 2 * RING
SMALL = 16


def smem():
    return pl.BlockSpec(memory_space=pltpu.SMEM)


def lanes_at(info_ref, index, width):
    size = width // PIECES
    return pl.ds(pl.multiple_of(info_ref[index] * size, size), size)


def reorder_in(info_ref, source, target, rows=slice(None)):
    width = source.shape[-1]
    size = width // PIECES
    for k in range(PIECES):
        target[rows, k * size : (k + 1) * size] = source[:, lanes_at(info_ref, INFO + k, width)].astype(target.dtype)


def reorder_out(info_ref, source, target, rows=slice(None)):
    width = source.shape[-1]
    size = width // PIECES
    for k in range(PIECES):
        part = source[rows, lanes_at(info_ref, INFO + PIECES + k, width)]
        target[:, k * size : (k + 1) * size] = part.astype(target.dtype)


def swap_all(arrays):
    return [swap(array, "c") for array in arrays]


def both_cores(own_ref, *got_refs):
    return own_ref[...] + jnp.concatenate([ref[...] for ref in got_refs], axis=0).astype(F32)


def inverse_rms(values):
    return lax.rsqrt(jnp.mean(values * values, axis=-1, keepdims=True) + EPSILON)


def rms_back(values, gain, grad):
    inverse = inverse_rms(values)
    scaled = values * inverse
    weighted = grad * gain
    back = inverse * (weighted - scaled * jnp.mean(scaled * weighted, axis=-1, keepdims=True))
    return back, jnp.sum(grad * scaled, axis=0, keepdims=True)


def rowwise(kernel, inputs, outputs, scratch=(), deps=(), long=False):
    return call(
        kernel,
        (1,),
        inputs,
        [smem()] + [whole(array) for array in inputs[1:]],
        outputs,
        [whole_out(shape) for shape, _ in outputs],
        scratch_shapes=[pltpu.VMEM(shape, dtype) for shape, dtype in scratch],
        deps=deps, long=long,
    )


def own_rows(info, keep, got):
    rows, width = keep.shape

    def kernel(info_ref, keep_ref, got_ref, out_ref):
        y = info_ref[2]
        reorder_in(info_ref, keep_ref, out_ref, pl.ds(pl.multiple_of(y * rows, rows), rows))
        reorder_in(info_ref, got_ref, out_ref, pl.ds(pl.multiple_of((1 - y) * rows, rows), rows))

    return rowwise(kernel, [info, keep, got], [((2 * rows, width), BF)])[0]


def local_rows(info, array):
    def kernel(info_ref, in_ref, out_ref):
        reorder_in(info_ref, in_ref, out_ref)

    return rowwise(kernel, [info, array], [(array.shape, array.dtype)])[0]


def norm_rows(info, values, gain, deps=()):
    def kernel(info_ref, in_ref, gain_ref, out_ref):
        rows = in_ref[...].astype(F32)
        out_ref[...] = (rows * inverse_rms(rows) * gain_ref[...]).astype(BF)

    return rowwise(kernel, [info, values, gain], [(values.shape, BF)], deps=deps)[0]


def add_norm(info, rows, both, gain, deps=()):
    own, *others = both

    def kernel(info_ref, row_ref, own_ref, got_ref, gain_ref, hidden_ref, norm_ref):
        hidden = row_ref[...].astype(F32) + (own_ref[...] + got_ref[...].astype(F32))
        hidden_ref[...] = hidden
        norm_ref[...] = (hidden * inverse_rms(hidden) * gain_ref[...]).astype(BF)

    return rowwise(kernel, [info, rows, own, *swap_all(others), gain], [(rows.shape, F32), (rows.shape, BF)], deps=deps)


def add_out(info, hidden, both):
    own, *others = both
    rows, width = hidden.shape
    half = rows // 2

    def kernel(info_ref, hidden_ref, own_ref, low_ref, high_ref, keep_ref, send_ref, scratch):
        y = info_ref[2]
        scratch[...] = hidden_ref[...] + (both_cores(own_ref, low_ref, high_ref))
        reorder_out(info_ref, scratch, keep_ref, pl.ds(pl.multiple_of(y * half, half), half))
        reorder_out(info_ref, scratch, send_ref, pl.ds(pl.multiple_of((1 - y) * half, half), half))

    return rowwise(
        kernel,
        [info, hidden, own, *swap_all(others)],
        [((half, width), BF)] * 2,
        [((rows, width), F32)],
    )


def step_state(info, state, both, gate, gain):
    own, *others = both

    def kernel(info_ref, state_ref, own_ref, got_ref, gate_ref, gain_ref, next_ref, norm_ref, update_ref):
        update = own_ref[...] + got_ref[...].astype(F32)
        update_ref[...] = update
        after = gate_ref[...] * state_ref[...] + (1.0 - gate_ref[...]) * update
        next_ref[...] = after
        norm_ref[...] = (after * inverse_rms(after) * gain_ref[...]).astype(BF)

    return rowwise(
        kernel,
        [info, state, own, *swap_all(others), gate, gain],
        [(state.shape, F32), (state.shape, BF), (state.shape, F32)],
    )


def last_state(info, state, both, gate):
    own, *others = both

    def kernel(info_ref, state_ref, own_ref, got_ref, gate_ref, final_ref, update_ref, scratch):
        update = own_ref[...] + got_ref[...].astype(F32)
        update_ref[...] = update
        scratch[...] = gate_ref[...] * state_ref[...] + (1.0 - gate_ref[...]) * update
        reorder_out(info_ref, scratch, final_ref)

    return rowwise(
        kernel,
        [info, state, own, *swap_all(others), gate],
        [(state.shape, BF), (state.shape, F32)],
        [(state.shape, F32)],
    )


def back_hidden(info, hidden, both, gain, dy):
    own, *others = both

    def kernel(info_ref, hidden_ref, own_ref, low_ref, high_ref, gain_ref, dy_ref, grad_ref, branch_ref, gain_grad_ref):
        grad = both_cores(own_ref, low_ref, high_ref)
        back, gain_grad_ref[...] = rms_back(hidden_ref[...], gain_ref[...], grad)
        total = dy_ref[...].astype(F32) + back
        grad_ref[...] = total
        branch_ref[...] = total.astype(BF)

    return rowwise(
        kernel,
        [info, hidden, own, *swap_all(others), gain, dy],
        [(hidden.shape, F32), (hidden.shape, BF), ((1, hidden.shape[1]), F32)],
    )


def back_update(info, grad, gate):
    def kernel(info_ref, grad_ref, gate_ref, out_ref):
        out_ref[...] = ((1.0 - gate_ref[...]) * grad_ref[...].astype(F32)).astype(BF)

    return rowwise(kernel, [info, grad, gate], [(grad.shape, BF)])[0]


def back_state(info, grad, state, update, both, gate, gain, long=False):
    own, *others = both
    width = state.shape[1]

    def kernel(
        info_ref, grad_ref, state_ref, update_ref, own_ref, *refs
    ):
        got_refs = refs[: len(others)]
        gate_ref, gain_ref, out_ref, next_ref, gain_grad_ref, gate_grad_ref = refs[len(others) :]
        gate_open = gate_ref[...]
        grad_now = grad_ref[...].astype(F32)
        values = state_ref[...]
        gate_grad_ref[...] = jnp.sum(grad_now * (values - update_ref[...]), axis=0, keepdims=True) * (
            gate_open * (1.0 - gate_open)
        )
        back, gain_grad_ref[...] = rms_back(values, gain_ref[...], both_cores(own_ref, *got_refs))
        total = gate_open * grad_now + back
        out_ref[...] = total
        next_ref[...] = ((1.0 - gate_open) * total).astype(BF)

    return rowwise(
        kernel,
        [info, grad, state, update, own, *swap_all(others), gate, gain],
        [(state.shape, F32), (state.shape, BF), ((1, width), F32), ((1, width), F32)],
        long=long,
    )


def back_input(info, values, both, gain, grad_hidden):
    own, *others = both
    rows, width = values.shape
    half = rows // 2

    def kernel(info_ref, value_ref, own_ref, low_ref, high_ref, gain_ref, grad_ref, keep_ref, send_ref, gain_grad_ref, scratch):
        y = info_ref[2]
        grad = both_cores(own_ref, low_ref, high_ref)
        back, gain_grad_ref[...] = rms_back(value_ref[...].astype(F32), gain_ref[...], grad)
        scratch[...] = grad_ref[...] + back
        reorder_out(info_ref, scratch, keep_ref, pl.ds(pl.multiple_of(y * half, half), half))
        reorder_out(info_ref, scratch, send_ref, pl.ds(pl.multiple_of((1 - y) * half, half), half))

    return rowwise(
        kernel,
        [info, values, own, *swap_all(others), gain, grad_hidden],
        [((half, width), F32), ((half, width), BF), ((1, width), F32)],
        [((rows, width), F32)],
    )


def pack_small(info, states, vectors):
    rows, width = states.shape
    half = width // 2
    counts = [len(group) for group in vectors]
    flat = [vector for group in vectors for vector in group]
    pad = SMALL - len(vectors)

    def kernel(info_ref, state_ref, *refs):
        near_ref, far_ref = refs[len(flat) :]
        parts, place = [], 0
        for count in counts:
            parts.append(sum(ref[...] for ref in refs[place : place + count]))
            place += count
        tail = jnp.concatenate(parts + [jnp.zeros((pad, width), F32)], axis=0)
        quarter = half // 2
        for source, here in ((state_ref[...], slice(0, rows)), (tail, slice(rows, rows + SMALL))):
            for x in range(2):
                to = slice(x * quarter, (x + 1) * quarter)
                near_ref[here, to] = source[:, 2 * x * quarter : (2 * x + 1) * quarter]
                far_ref[here, to] = source[:, (2 * x + 1) * quarter : (2 * x + 2) * quarter].astype(BF)

    shape = (rows + SMALL, half)
    return rowwise(kernel, [info, states] + flat, [(shape, F32), (shape, BF)])


def add_small(info, near, got, groups=1):
    rows, width = near.shape
    half = width // 2

    def kernel(info_ref, near_ref, got_ref, near_out, far_out):
        total = near_ref[...] + got_ref[...].astype(F32)
        size = half // groups
        for g in range(groups):
            to = slice(g * size, (g + 1) * size)
            near_out[:, to] = total[:, 2 * g * size : (2 * g + 1) * size]
            far_out[:, to] = total[:, (2 * g + 1) * size : (2 * g + 2) * size].astype(BF)

    return rowwise(kernel, [info, near, got], [((rows, half), F32), ((rows, half), BF)])


def add_pair(info, near, got):
    def kernel(info_ref, near_ref, got_ref, out_ref):
        out_ref[...] = near_ref[...] + got_ref[...].astype(F32)

    return rowwise(kernel, [info, near, got], [(near.shape, F32)])[0]


def place_small(info, near, far, states):
    size = near.shape[1]

    def kernel(info_ref, near_ref, far_ref, state_ref, gain_ref, gate_ref):
        c = info_ref[0]
        state_ref[pl.ds(pl.multiple_of(c * states, states), states)] = near_ref[:states]
        state_ref[pl.ds(pl.multiple_of((1 - c) * states, states), states)] = far_ref[:states]
        total = near_ref[states:] + far_ref[states:]
        gain_ref[...] = total[:3]
        gate_ref[...] = total[3:4]

    return rowwise(kernel, [info, near, far], [((2 * states, size), F32), ((3, size), F32), ((1, size), F32)])


def place_rows(info, keep, got):
    shape = (2,) + keep.shape

    def kernel(info_ref, keep_ref, got_ref, out_ref):
        y = info_ref[2]
        out_ref[y] = keep_ref[...]
        out_ref[1 - y] = got_ref[...].astype(keep.dtype)

    return rowwise(kernel, [info, keep, got], [(shape, keep.dtype)])[0]


def place_state(info, near, near_c, far, far_c):
    rows, width = near.shape

    def kernel(info_ref, near_ref, near_c_ref, far_ref, far_c_ref, out_ref):
        c, y = info_ref[0], info_ref[2]
        here = pl.ds(pl.multiple_of(c * rows, rows), rows)
        there = pl.ds(pl.multiple_of((1 - c) * rows, rows), rows)
        out_ref[y, here] = near_ref[...]
        out_ref[y, there] = near_c_ref[...]
        out_ref[1 - y, here] = far_ref[...]
        out_ref[1 - y, there] = far_c_ref[...]

    return rowwise(kernel, [info, near, near_c, far, far_c], [((2, 2 * rows, width), near.dtype)])[0]


SCALE = HEAD_DIM ** (-0.5)


def key_tiles(b, j):
    tiles = []
    if b > 0:
        tiles += [(b - 1, jj, "after" if jj == j else "all") for jj in range(j, 2)]
    tiles += [(b, jj, "until" if jj == j else "all") for jj in range(j + 1)]
    return tiles


def tile_mask(kind, size, limit):
    rows = lax.broadcasted_iota(jnp.int32, (size, size), 0)
    columns = lax.broadcasted_iota(jnp.int32, (size, size), 1)
    mask = None
    if kind == "after":
        mask = columns > rows
    if kind == "until":
        mask = columns <= rows
    if limit is not None:
        inside = columns < limit
        mask = inside if mask is None else mask & inside
    return mask


def masked_scores(queries, keys, masks):
    scores = mm_nt(queries, keys) * SCALE
    parts, place = [], 0
    for size, mask in masks:
        part = scores[:, place : place + size]
        parts.append(part if mask is None else jnp.where(mask, part, MASKED))
        place += size
    return jnp.concatenate(parts, axis=1)


def attention_plan(b, last, size, core, count, states):
    def start(block, j):
        return pl.multiple_of(block * 2 * size + jnp.bitwise_xor(core, j) * size, size)

    plan = []
    for j in range(2):
        tiles, masks = [], []
        for block, jj, kind in key_tiles(b, j):
            limit = count - jj * size if block == b and last else None
            tiles.append((block, jj))
            masks.append((size, tile_mask(kind, size, limit)))
        plan.append((tiles, masks + [(states, None)]))
    state_masks = [(states, None)]
    for jj in range(2):
        state_masks.append((size, tile_mask("all", size, count - jj * size if last else None)))
    return start, plan, state_masks


def block_spec(rows, width):
    return pl.BlockSpec((1, rows, width), lambda y: (y, 0, 0))


def head_slices(lanes, h):
    return [slice(p * lanes + h * HEAD_DIM, p * lanes + (h + 1) * HEAD_DIM) for p in range(3)]


def attend_rows(queries, keys, values, masks):
    scores = masked_scores(queries, keys, masks)
    top = jnp.max(scores, axis=1, keepdims=True)
    weights = jnp.exp(scores - top)
    total = jnp.sum(weights, axis=1, keepdims=True)
    mixed = mm(weights.astype(BF), values) / total
    return mixed.astype(BF), top + jnp.log(total)


def attend_rows_back(queries, keys, values, masks, log_total, grad):
    scores = masked_scores(queries, keys, masks)
    probs = jnp.exp(scores - log_total)
    grad_probs = mm_nt(grad, values)
    row_sum = jnp.sum(grad_probs * probs, axis=1, keepdims=True)
    low = (probs * (grad_probs - row_sum)).astype(BF)
    return mm(low, keys) * SCALE, mm_tn(low, queries) * SCALE, mm_tn(probs.astype(BF), grad)


def token_pairs(b, heads, states):
    return 2 * heads * BLOCK * (BLOCK * (1.25 if b else 0.75) + states)


def forward_tokens(b, blocks, info, tokens, states, deps=()):
    lanes = tokens.shape[2] // 3
    heads = lanes // HEAD_DIM
    size = BLOCK // 2
    count_states = states.shape[1]

    def kernel(info_ref, token_ref, state_ref, mixed_ref, log_ref):
        start, plan, state_masks = attention_plan(
            b, b == blocks - 1, size, info_ref[0], info_ref[1], count_states
        )
        for h in range(heads):
            query, key, value = head_slices(lanes, h)
            for j, (tiles, masks) in enumerate(plan):
                rows = [pl.ds(start(*place), size) for place in tiles]
                keys = jnp.concatenate([token_ref[0, at, key] for at in rows] + [state_ref[0, :, key]], axis=0)
                values = jnp.concatenate([token_ref[0, at, value] for at in rows] + [state_ref[0, :, value]], axis=0)
                here = pl.ds(start(0, j), size)
                mixed_ref[0, here, query], log_ref[0, here, h : h + 1] = attend_rows(
                    token_ref[0, pl.ds(start(b, j), size), query], keys, values, masks
                )

    pairs = int(token_pairs(b, heads, count_states))
    return call(
        kernel,
        (2,),
        [info, tokens, states],
        [smem(), block_spec((b + 1) * BLOCK, 3 * lanes), block_spec(count_states, 3 * lanes)],
        [((2, BLOCK, lanes), BF), ((2, BLOCK, 128), F32)],
        [block_spec(BLOCK, lanes), block_spec(BLOCK, 128)],
        flops=4 * pairs * HEAD_DIM,
        exps=pairs,
        deps=deps,
    )


def forward_states(b, blocks, info, tokens, states, deps=()):
    lanes = tokens.shape[2] // 3
    heads = lanes // HEAD_DIM
    size = BLOCK // 2
    count_states = states.shape[1]

    def kernel(info_ref, token_ref, state_ref, mixed_ref, log_ref):
        start, plan, state_masks = attention_plan(
            0, b == blocks - 1, size, info_ref[0], info_ref[1], count_states
        )
        for h in range(heads):
            query, key, value = head_slices(lanes, h)
            rows = [pl.ds(start(0, j), size) for j in range(2)]
            keys = jnp.concatenate([state_ref[0, :, key]] + [token_ref[0, at, key] for at in rows], axis=0)
            values = jnp.concatenate([state_ref[0, :, value]] + [token_ref[0, at, value] for at in rows], axis=0)
            for begin in range(0, count_states, size):
                here = slice(begin, begin + size)
                mixed_ref[0, here, query], log_ref[0, here, h : h + 1] = attend_rows(
                    state_ref[0, here, query], keys, values, state_masks
                )

    pairs = 2 * heads * count_states * (count_states + BLOCK)
    return call(
        kernel,
        (2,),
        [info, tokens, states],
        [smem(), pl.BlockSpec((1, BLOCK, 3 * lanes), lambda y: (y, b, 0)), block_spec(count_states, 3 * lanes)],
        [((2, count_states, lanes), BF), ((2, count_states, 128), F32)],
        [block_spec(count_states, lanes), block_spec(count_states, 128)],
        flops=4 * pairs * HEAD_DIM,
        exps=pairs,
        deps=deps,
    )


def add_part(sums, place, part):
    sums[place] = part if place not in sums else sums[place] + part


def backward_tokens(b, blocks, info, tokens, states, logs, grad_mixed, deps=(), long=False):
    lanes = tokens.shape[2] // 3
    heads = lanes // HEAD_DIM
    size = BLOCK // 2
    count_states = states.shape[1]

    def kernel(info_ref, token_ref, state_ref, log_ref, grad_ref, query_ref, own_ref, state_out_ref, *before_ref):
        start, plan, state_masks = attention_plan(
            b, b == blocks - 1, size, info_ref[0], info_ref[1], count_states
        )
        for h in range(heads):
            query, key, value = head_slices(lanes, h)
            sums = ({}, {})
            for j, (tiles, masks) in enumerate(plan):
                rows = [pl.ds(start(*place), size) for place in tiles]
                keys = jnp.concatenate([token_ref[0, at, key] for at in rows] + [state_ref[0, :, key]], axis=0)
                values = jnp.concatenate([token_ref[0, at, value] for at in rows] + [state_ref[0, :, value]], axis=0)
                here = pl.ds(start(0, j), size)
                dq, dk, dv = attend_rows_back(
                    token_ref[0, pl.ds(start(b, j), size), query],
                    keys,
                    values,
                    masks,
                    log_ref[0, here, h : h + 1],
                    grad_ref[0, here, query],
                )
                query_ref[0, here, query] = dq.astype(BF)
                for which, grads in enumerate((dk, dv)):
                    for i, place in enumerate(tiles):
                        add_part(sums[which], place, grads[i * size : (i + 1) * size])
                    add_part(sums[which], "state", grads[len(tiles) * size :])
            for which in range(2):
                columns = slice(which * lanes + h * HEAD_DIM, which * lanes + (h + 1) * HEAD_DIM)
                state_out_ref[0, :, columns] = sums[which]["state"].astype(BF)
                for j in range(2):
                    here = pl.ds(start(0, j), size)
                    own_ref[0, here, columns] = sums[which][(b, j)].astype(BF)
                    if b > 0:
                        before_ref[0][0, here, columns] = sums[which][(b - 1, j)].astype(BF)

    pairs = int(token_pairs(b, heads, count_states))
    outputs = [((2, BLOCK, lanes), BF), ((2, BLOCK, 2 * lanes), BF), ((2, count_states, 2 * lanes), BF)]
    out_specs = [block_spec(BLOCK, lanes), block_spec(BLOCK, 2 * lanes), block_spec(count_states, 2 * lanes)]
    if b > 0:
        outputs.append(((2, BLOCK, 2 * lanes), BF))
        out_specs.append(block_spec(BLOCK, 2 * lanes))
    return call(
        kernel,
        (2,),
        [info, tokens, states, logs, grad_mixed],
        [
            smem(),
            block_spec((b + 1) * BLOCK, 3 * lanes),
            block_spec(count_states, 3 * lanes),
            block_spec(BLOCK, 128),
            pl.BlockSpec((1, BLOCK, lanes), lambda y: (y, b, 0)),
        ],
        outputs,
        out_specs,
        flops=10 * pairs * HEAD_DIM,
        exps=pairs,
        deps=deps,
        long=long,
    )


def backward_states(b, blocks, info, tokens, states, logs, grad_mixed, token_sums, state_sums, deps=(), long=False):
    lanes = tokens.shape[2] // 3
    heads = lanes // HEAD_DIM
    size = BLOCK // 2
    count_states = states.shape[1]
    count = len(token_sums)

    def kernel(info_ref, token_ref, state_ref, log_ref, grad_ref, sum_ref, *rest):
        token_sum_refs, (state_out_ref, token_out_ref) = rest[:count], rest[count:]
        start, plan, state_masks = attention_plan(
            0, b == blocks - 1, size, info_ref[0], info_ref[1], count_states
        )
        for h in range(heads):
            query, key, value = head_slices(lanes, h)
            rows = [pl.ds(start(0, j), size) for j in range(2)]
            keys = jnp.concatenate([state_ref[0, :, key]] + [token_ref[0, at, key] for at in rows], axis=0)
            values = jnp.concatenate([state_ref[0, :, value]] + [token_ref[0, at, value] for at in rows], axis=0)
            sums = [None, None]
            for begin in range(0, count_states, size):
                here = slice(begin, begin + size)
                dq, dk, dv = attend_rows_back(
                    state_ref[0, here, query],
                    keys,
                    values,
                    state_masks,
                    log_ref[0, here, h : h + 1],
                    grad_ref[0, here, query],
                )
                state_out_ref[0, here, query] = dq.astype(BF)
                sums = [part if old is None else old + part for old, part in zip(sums, (dk, dv))]
            for which, to in ((0, key), (1, value)):
                columns = slice(which * lanes + h * HEAD_DIM, which * lanes + (h + 1) * HEAD_DIM)
                state_out_ref[0, :, to] = (sums[which][:count_states] + sum_ref[0, :, columns].astype(F32)).astype(BF)
                for j in range(2):
                    total = sums[which][count_states + j * size : count_states + (j + 1) * size]
                    for ref in token_sum_refs:
                        total = total + ref[0, rows[j], columns].astype(F32)
                    token_out_ref[0, rows[j], columns] = total.astype(BF)

    pairs = 2 * heads * count_states * (count_states + BLOCK)
    return call(
        kernel,
        (2,),
        [info, tokens, states, logs, grad_mixed, state_sums] + list(token_sums),
        [
            smem(),
            pl.BlockSpec((1, BLOCK, 3 * lanes), lambda y: (y, b, 0)),
            block_spec(count_states, 3 * lanes),
            block_spec(count_states, 128),
            block_spec(count_states, lanes),
            block_spec(count_states, 2 * lanes),
        ]
        + [block_spec(BLOCK, 2 * lanes)] * count,
        [((2, count_states, 3 * lanes), BF), ((2, BLOCK, 2 * lanes), BF)],
        [block_spec(count_states, 3 * lanes), block_spec(BLOCK, 2 * lanes)],
        flops=10 * pairs * HEAD_DIM,
        exps=pairs,
        deps=deps,
        long=long,
    )


def body(
    tokens,
    counts,
    token_weights,
    token_output,
    state_weights,
    state_output,
    hidden_up,
    hidden_down,
    norm_gains,
    gate_bias,
    init_state,
    cotangent,
    state_cotangent,
):
    y, c = lax.axis_index("y"), lax.axis_index("c")
    width = tokens.shape[3]
    state_half = init_state.shape[0] // 2
    blocks = 4 * tokens.shape[2] // BLOCK
    valid_count = lax.dynamic_index_in_dim(counts[:, 0], y, 0, keepdims=False)
    if lax.axis_size("r") == 1:
        places, back = width_places(), width_places_back()
        before, after = (lambda array: array), (lambda array: array)
    else:
        places = back = list(range(PIECES))
        before, after = to_local, from_local
    info = jnp.stack([jnp.asarray(v, jnp.int32) for v in [c, valid_count, y] + places + back])

    def micro(array, index):
        return lax.dynamic_index_in_dim(array[:, 0], index, 0, keepdims=False)

    ORDER.last = []
    shard_rows = token_output.shape[0]
    head, ff = token_output.shape[1], hidden_up.shape[1]
    at_state, at_state_out, at_token_out = 0, 3 * head, ff
    flat = lambda array: array.reshape(shard_rows, -1)
    token = Gather(flat(token_weights))
    token_got = swap(micro(tokens, 1 - y), "y")
    small = jnp.concatenate(
        [
            lax.dynamic_slice_in_dim(init_state, c * state_half, state_half, 0),
            norm_gains,
            gate_bias[None],
            jnp.zeros((12, init_state.shape[1]), BF),
        ],
        axis=0,
    )
    if lax.axis_size("r") > 1:
        small = lax.all_gather(small, "r", axis=1, tiled=True)
    small_got = swap_z(small, 2)
    w_token = token.spread(by_x=True)
    mid = Gather(join_columns([flat(state_weights), state_output], ()))
    small = stack_rows(small, small_got)
    small = stack_rows(small, swap_z(small, 1))
    small_got = swap(small, "x")
    x_rows = own_rows(info, before(micro(tokens, y)), before(token_got))
    small = spread_rows(info, small, small_got)
    gains = [small[state_half + i : state_half + i + 1].astype(F32) for i in range(3)]
    gate_open = jax.nn.sigmoid(small[state_half + 3 : state_half + 4].astype(F32))
    state_now = small[:state_half].astype(F32)
    normed = pair(norm_rows(info, x_rows, gains[0], token.low))
    state_norm = pair(norm_rows(info, state_now, gains[1]))
    w_mid = mid.spread(token.low)
    up = Gather(join_columns([hidden_up, token_output], ()))

    token_proj = project(*normed, w_token, 0, 3 * head, 3 * head // 2, blocks=blocks)
    w_up = up.spread(mid.low)
    down = Gather(join_columns([hidden_down], ()))
    dy_got = swap(micro(cotangent, 1 - y), "y")
    grad_final = lax.dynamic_slice(
        state_cotangent, (y, 0, c * state_half, 0), (1, 1, state_half, width)
    )[0, 0]
    grad_final = local_rows(info, before(grad_final))
    grad_update = pair(back_update(info, grad_final, gate_open))
    kept = []
    mixed = []
    for b in range(blocks):
        proj_wait, state_wait, merge_wait, token_wait = (
            (up.ring, [], up.low + [down.got], up.high) if b == 0 else ([], up.far, down.ring, down.low)
        )
        state_proj = project(*state_norm, w_mid, at_state, 3 * head, 3 * head, deps=proj_wait)
        state_flat, state_logs = forward_states(b, blocks, info, token_proj, state_proj, deps=state_wait)
        both = merge([[state_flat]], w_mid, at_state_out, deps=merge_wait)
        mixed_b, logs = forward_tokens(b, blocks, info, token_proj, state_proj, deps=token_wait)
        mixed.append(mixed_b)
        if b < blocks - 1:
            state_next, next_norm, update = step_state(info, state_now, both, gate_open, gains[1])
        else:
            final_rows, update = last_state(info, state_now, both, gate_open)
            state_next, next_norm = None, None
        kept.append((state_now, state_norm, state_proj, logs, state_logs, state_flat, update))
        state_now = state_next
        state_norm = None if next_norm is None else pair(next_norm)
        if b == 0:
            dy_rows = own_rows(info, before(micro(cotangent, y)), before(dy_got))
            dy_pair = pair(dy_rows)
            grad_state_mixed = project(*grad_update, w_mid, at_state_out, head, head)
            w_down = down.spread()
    hidden, hidden_own = add_norm(
        info, x_rows, merge([[part] for part in mixed], w_up, at_token_out, blocks=blocks, deps=down.high), gains[2]
    )
    hidden_norm = pair(hidden_own)
    activated, slope = project(*hidden_norm, w_up, 0, ff, ff // 2, activate=True)

    down_grad = Reduce(outer([([dy_pair], [activated], 1)], ff // 2, split=True, long=True))
    grad_up = project(*dy_pair, w_down, 0, ff, ff // 2, gate=slope, long=True)
    both = merge([[grad_up]], w_up, 0, halves=2)
    up_grad = Reduce(outer([([hidden_norm], [grad_up], 1)], ff // 2, split=True))
    down_grad.second()
    grad_hidden, branch, gain_hidden = back_hidden(info, hidden, both, gains[2], dy_rows)
    branch = pair(branch)

    grad_mixed = project(*branch, w_up, at_token_out, head, head, blocks=blocks)
    grad_state = grad_final
    gate_sums, gain_sums = [], []
    query_grads, pair_grads = [None] * blocks, [None] * blocks
    update_all, flat_all, norm_all, state_grads = [], [], [], []
    sums = [None] * blocks

    def tokens_back(b, **how):
        state_proj, logs = kept[b][2], kept[b][3]
        query_grads[b], *sums[b] = backward_tokens(b, blocks, info, token_proj, state_proj, logs, grad_mixed, **how)

    def states_back(b, later, **how):
        state_before, state_norm, state_proj, logs, state_logs, state_flat, update = kept[b]
        own_sums, state_sums, *before_sums = sums[b]
        state_grad, pair_grads[b] = backward_states(
            b, blocks, info, token_proj, state_proj, state_logs, grad_state_mixed, [own_sums] + later, state_sums, **how
        )
        update_all.append(grad_update)
        flat_all.append(state_flat)
        norm_all.append(state_norm)
        state_grads.append(state_grad)
        return merge([[state_grad]], w_mid, at_state, halves=1 if b else 2), before_sums

    def state_step(b, both, grad_state):
        state_before, update = kept[b][0], kept[b][-1]
        grad_state, low, gain_sum, gate_sum = back_state(
            info, grad_state, state_before, update, both, gate_open, gains[1], long=b > 0
        )
        gain_sums.append(gain_sum)
        gate_sums.append(gate_sum)
        return grad_state, low

    last = blocks - 1
    tokens_back(last, long=True)
    both, later = states_back(last, [])
    for b in range(last - 1, -1, -1):
        tokens_back(b)
        if b == last - 1:
            up_grad.second()
            down_grad.third()
        grad_state, low = state_step(b + 1, both, grad_state)
        grad_update = pair(low)
        grad_state_mixed = project(*grad_update, w_mid, at_state_out, head, head)
        if b == 0:
            early_grad = Reduce(
                outer(
                    [
                        ([branch], mixed, blocks),
                        ([normed], query_grads, blocks),
                        ([grad_update] + update_all, [kept[0][5]] + flat_all, 1),
                    ],
                    vmem=28,
                    split=True,
                )
            )
        both, later = states_back(b, later, long=b == 0)

    down_grad.fourth()
    early_grad.second()
    token_both = merge(
        [[query_grads[i], pair_grads[i]] for i in range(blocks)], w_token, 0, blocks=blocks, halves=2
    )
    grad_state, low = state_step(0, both, grad_state)
    late_grad = Reduce(outer([([normed], pair_grads, blocks), (norm_all, state_grads, 1)], vmem=28, split=True))
    keep, send, gain_token = back_input(info, x_rows, token_both, gains[0], grad_hidden)
    input_keep, input_got = after(keep), swap(after(send), "y")
    near, far = pack_small(info, grad_state, [[gain_token], gain_sums, [gain_hidden], gate_sums])
    far = swap_z(far, 1)
    up_grad.third()
    down_grad.finish()
    late_grad.second(early_grad.next)
    early_grad.third()
    out_both = merge([[activated]], w_down, 0, halves=2)
    up_grad.fourth()
    near, far = add_small(info, near, far, 2)
    far = swap_z(far, 2)
    keep, send = add_out(info, hidden, out_both)
    output_got = swap(after(send), "y")
    output_keep = after(keep)
    final_rows = after(final_rows)
    final_far = swap(final_rows, "y")
    early_grad.fourth()
    up_grad.finish()
    near, far = add_small(info, near, far)
    far = swap(far, "x")
    late_grad.third()
    near = add_pair(info, near, far)
    if lax.axis_size("r") > 1:
        near = lax.psum_scatter(near, "r", scatter_dimension=1, tiled=True)
    far = swap(near, "y")
    early_grad.finish()
    near = add_pair(info, near, far)
    far = swap(near, "c")
    late_grad.fourth()
    init_grad, grad_gains, grad_gate = place_small(info, near, far, state_half)
    output = place_rows(info, output_keep, output_got)[:, None]
    final_state = place_state(info, final_rows, swap(final_rows, "c"), final_far, swap(final_far, "c"))[:, None]
    input_grad = place_rows(info, input_keep, input_got)[:, None]
    late_grad.finish()
    grad_hidden_down, grad_hidden_up = down_grad.total, up_grad.total
    grad_token_output, grad_query, grad_state_output = [
        early_grad.total[:, i * head : (i + 1) * head] for i in range(3)
    ]
    late = late_grad.total
    grad_token_weights = jnp.stack([grad_query, late[:, :head], late[:, head : 2 * head]], axis=1)
    grad_state_weights = late[:, 2 * head :].reshape(-1, 3, head)
    return (
        output,
        final_state,
        input_grad,
        grad_token_weights,
        grad_token_output,
        grad_state_weights,
        grad_state_output,
        grad_hidden_up,
        grad_hidden_down,
        grad_gains,
        grad_gate[0],
        init_grad,
    )


def solution(mesh):
    dp, heads = mesh.devices.shape
    fine = Mesh(mesh.devices.reshape(dp // (2 * RING), RING, 2, heads // 2, 2), ("r", "z", "x", "y", "c"))
    d, h = ("r", "z", "x"), ("y", "c")
    return jax.shard_map(
        body,
        mesh=fine,
        in_specs=(
            P(None, d, h, None),
            P(None, d),
            P(d, None, h),
            P(d, h),
            P(d, None, h),
            P(d, h),
            P(d, h),
            P(d, h),
            P(None, d),
            P(d),
            P(None, d),
            P(None, d, h, None),
            P(None, d, None, None),
        ),
        out_specs=(
            P(None, d, h, None),
            P(None, d, None, None),
            P(None, d, h, None),
            P(d, None, h),
            P(d, h),
            P(d, None, h),
            P(d, h),
            P(d, h),
            P(d, h),
            P(None, d),
            P(d),
            P(None, d),
        ),
        check_vma=False,
    )
```
